32 devices in a mesh: dp: 32 (over z, y, x, core).
Axes of the slice: x: 2, y: 2, z: 4, core: 2. Of those that a mesh axis runs over, the one named last changes fastest.
Arguments:
- tokens: bfloat16 [4096, 1024], P('dp'), may hold values from -6 to 6
- lengths: int32 [128], P('dp'), may hold values from 0 to 128, as said below
- in_weight: bfloat16 [1024, 4384], P('dp'), may hold values from -0.1875 to 0.1875
- out_weight: bfloat16 [2048, 1024], P('dp'), may hold values from -0.125 to 0.125
- conv_weight: float32 [4, 2304], replicated, may hold values from -3 to 3
- conv_bias: float32 [2304], replicated, may hold values from -1.5 to 1.5
- dt_bias: float32 [32], replicated, may hold values from -5 to -1
- a_log: float32 [32], replicated, may hold values from 0 to 2.77
- skip_gain: float32 [32], replicated, may hold values from 0.5 to 1.5
- norm_gain: float32 [2048], replicated, may hold values from 0.25 to 1.75
- pre_gain: float32 [1024], replicated, may hold values from 0.25 to 1.75
- cotangent: bfloat16 [4096, 1024], P('dp'), may hold values from -6 to 6
Outputs:
- mixed: bfloat16 [4096, 1024], P('dp')
- tokens_grad: float32 [4096, 1024], P('dp')
- in_weight_grad: float32 [1024, 4384], P('dp')
- out_weight_grad: float32 [2048, 1024], P('dp')
- conv_weight_grad: float32 [4, 2304], replicated
- conv_bias_grad: float32 [2304], replicated
- dt_bias_grad: float32 [32], replicated
- a_log_grad: float32 [32], replicated
- skip_gain_grad: float32 [32], replicated
- norm_gain_grad: float32 [2048], replicated
- pre_gain_grad: float32 [1024], replicated
The draws below stay inside these ranges and needn't reach their ends.
Inputs may be any that keep to these rules, and one draw needn't show every extreme that they name: Each device's 4 lengths sum to at most 128; in every draw one device holds a single sequence of exactly 128 tokens.
All inputs are finite; a program needn't handle non-finite values.
Results may differ from the reference program's by a relative error of at most 0.0092.
Values may be sent and summed in bfloat16 or wider, within the bound.
No kernel may reach another device: no remote copies, remote signals or barrier semaphores. Data moves between devices by JAX's collectives and lax.ppermute only.
A program may use at most 128 MiB of HBM per device.

```python
import jax
import jax.numpy as jnp
from jax import lax

D = 1024
INNER = 2048
KCONV = 4
SCAN_ROWS = 64
CAP = 128
SLOTS = 4
HEADS = 32
CONVW = 2304
PROJ = 4384
TOKENS = 4096
SEQ_SLOTS = 128


def draw_lengths(key, part):
    key = jax.random.fold_in(key, 11)
    key_total, key_cut, key_full = jax.random.split(key, 3)
    device_count = SEQ_SLOTS // SLOTS
    totals = jax.random.randint(key_total, (device_count,), CAP // 4, CAP + 1)
    cut_points = jnp.sort(jax.random.randint(key_cut, (device_count, SLOTS - 1), 0, CAP + 1), axis=1)
    cut_points = jnp.minimum(cut_points, totals[:, None])
    cut_edges = jnp.concatenate([jnp.zeros((device_count, 1), jnp.int32), cut_points, totals[:, None]], axis=1)
    seq_lengths = cut_edges[:, 1:] - cut_edges[:, :-1]
    full_device = jax.random.randint(key_full, (), 0, device_count)
    single = jnp.concatenate([jnp.full((1,), CAP, jnp.int32), jnp.zeros((SLOTS - 1,), jnp.int32)])
    chosen = (jnp.arange(device_count) == full_device)[:, None]
    seq_lengths = jnp.where(chosen, single[None, :], seq_lengths)
    return seq_lengths.reshape(-1).astype(jnp.int32)


def levels(own_key, shape, pieces, low, largest):
    def one(axis_at, blocks):
        draws = jax.random.uniform(jax.random.fold_in(jax.random.fold_in(own_key, 6), axis_at), (blocks,), jnp.float32, low / len(pieces), largest / len(pieces))
        return jnp.repeat(jnp.exp(draws), shape[axis_at] // blocks).reshape((-1,) + (1,) * (len(shape) - axis_at - 1))

    factor_of = one(*pieces[0])
    for cut in pieces[1:]:
        factor_of = factor_of * one(*cut)
    return factor_of


def gaussian(key, dims, width, most, pieces=(), held_as=jnp.bfloat16):
    factor_of = levels(key, dims, pieces, -0.22, 0.18) if pieces else 1.0
    entries = jax.random.normal(key, dims, jnp.float32) * width * factor_of
    return jnp.minimum(jnp.maximum(entries, -most), most).astype(held_as)


def setup_inputs(seed: int = 0) -> dict:
    key_list = jax.random.split(jax.random.key(seed), 13)
    return {
        "tokens": gaussian(key_list[0], (TOKENS, D), 1.0, 6.0, ((0, 32),)),
        "lengths": draw_lengths(jax.random.fold_in(key_list[12], 71), 0),
        "in_weight": gaussian(key_list[2], (D, PROJ), D ** -0.5, 0.1875, ((0, 32),)),
        "out_weight": gaussian(key_list[3], (INNER, D), INNER ** -0.5, 0.125, ((0, 32),)),
        "conv_weight": gaussian(key_list[4], (KCONV, CONVW), KCONV ** -0.5, 3.0, (), jnp.float32),
        "conv_bias": gaussian(key_list[5], (CONVW,), 0.3, 1.5, (), jnp.float32),
        "dt_bias": jnp.clip(jax.random.uniform(key_list[6], (HEADS,), jnp.float32, -5.0, -1.0), -5.0, -1.0),
        "a_log": jnp.clip(jax.random.uniform(key_list[7], (HEADS,), jnp.float32, 0.0, 2.77), 0.0, 2.77),
        "skip_gain": jnp.clip(jax.random.uniform(key_list[8], (HEADS,), jnp.float32, 0.5, 1.5), 0.5, 1.5),
        "norm_gain": jnp.clip(1.0 + 0.15 * jax.random.normal(key_list[9], (INNER,), jnp.float32), 0.25, 1.75),
        "pre_gain": jnp.clip(1.0 + 0.15 * jax.random.normal(key_list[10], (D,), jnp.float32), 0.25, 1.75),
        "cotangent": gaussian(key_list[11], (TOKENS, D), 1.0, 6.0, ((0, 32),)),
    }


EPS = 1e-05
HIGH = lax.Precision.HIGHEST

@jax.custom_vjp
def low(v):
    return lax.optimization_barrier(v.astype(jnp.bfloat16)).astype(jnp.float32)

@jax.custom_vjp
def low_back(v):
    return v

def low_keep(v):
    return (low(v), None)

def low_pass(kept, grad):
    return (grad,)

def back_keep(v):
    return (v, None)

def back_low(kept, grad):
    return (low(grad),)
low.defvjp(low_keep, low_pass)
low_back.defvjp(back_keep, back_low)

def prenorm(hidden_in, gain_row):
    return hidden_in * lax.rsqrt(lax.optimization_barrier(jnp.mean(hidden_in * hidden_in, axis=-1, keepdims=True)) + EPS) * gain_row

def shifted(array, offset, filler):
    padding = jnp.full((offset,) + array.shape[1:], filler, array.dtype)
    return jnp.concatenate([padding, array[:-offset]], axis=0)

def segments(seq_lengths, row_count):
    seq_ends = jnp.cumsum(seq_lengths, dtype=jnp.int32)
    position = jnp.arange(row_count, dtype=jnp.int32)
    segment = lax.optimization_barrier(jnp.sum((position[:, None] >= seq_ends[None, :]).astype(jnp.int32), axis=1, dtype=jnp.int32))
    live_rows = (position < seq_ends[-1]).astype(jnp.float32)
    return (segment, live_rows)

def block_step(carry, block_item):
    state_mat, prev_segment = carry
    values, key_rows, read_rows, step_size, log_decay, block_segment = block_item
    cumulative = jnp.cumsum(log_decay, axis=0)
    position = jnp.arange(block_segment.shape[0], dtype=jnp.int32)
    causal = (block_segment[:, None] == block_segment[None, :]) & (position[:, None] >= position[None, :])
    distance = cumulative[:, None, :] - cumulative[None, :, :]
    decay_mask = jnp.where(causal[:, :, None], jnp.exp(jnp.where(causal[:, :, None], distance, 0.0)), 0.0)
    scores = jnp.dot(read_rows, key_rows.T, precision=HIGH)
    weighting = scores[:, :, None] * decay_mask * step_size[None, :, :]
    inside = jnp.einsum('ijh,jhp->ihp', weighting, values, precision=HIGH)
    entering = (block_segment == prev_segment).astype(jnp.float32)
    carried = jnp.einsum('in,hnp->ihp', read_rows, state_mat, precision=HIGH)
    carried = carried * (jnp.exp(cumulative) * entering[:, None])[:, :, None]
    last_same = (block_segment == block_segment[-1]).astype(jnp.float32)
    tail_weight = jnp.exp(cumulative[-1][None, :] - cumulative) * last_same[:, None] * step_size
    new_state = state_mat * (jnp.exp(cumulative[-1]) * entering[-1])[:, None, None]
    new_state = new_state + jnp.einsum('jn,jh,jhp->hnp', key_rows, tail_weight, values, precision=HIGH)
    return ((new_state, block_segment[-1]), inside + carried)

def mixer_core(projected, conv_weight, conv_bias, dt_bias, a_log, skip_gain, norm_gain, segment):
    inner_width = norm_gain.shape[0]
    head_count = dt_bias.shape[0]
    conv_width = conv_bias.shape[0]
    state_width = (conv_width - inner_width) // 2
    head_size = inner_width // head_count
    row_count = projected.shape[0]
    gate_in = projected[:, :inner_width]
    conv_src = projected[:, inner_width:inner_width + conv_width]
    dt_raw = projected[:, inner_width + conv_width:]
    conv_sum = conv_bias[None, :] + conv_weight[0][None, :] * conv_src
    for offset in range(1, conv_weight.shape[0]):
        same_rows = (segment == shifted(segment, offset, -1)).astype(jnp.float32)
        conv_sum = conv_sum + conv_weight[offset][None, :] * shifted(conv_src, offset, 0.0) * same_rows[:, None]
    activated = jax.nn.silu(conv_sum)
    values = activated[:, :inner_width].reshape(row_count, head_count, head_size)
    key_rows = activated[:, inner_width:inner_width + state_width]
    read_rows = activated[:, inner_width + state_width:]
    step_size = jax.nn.softplus(dt_raw + dt_bias[None, :])
    log_decay = -step_size * jnp.exp(a_log)[None, :]
    blocks = row_count // SCAN_ROWS
    items = (values.reshape(blocks, SCAN_ROWS, head_count, head_size), key_rows.reshape(blocks, SCAN_ROWS, state_width), read_rows.reshape(blocks, SCAN_ROWS, state_width), step_size.reshape(blocks, SCAN_ROWS, head_count), log_decay.reshape(blocks, SCAN_ROWS, head_count), segment.reshape(blocks, SCAN_ROWS))
    start = (jnp.zeros((head_count, state_width, head_size), jnp.float32), jnp.array(-1, jnp.int32))
    _, scanned = lax.scan(jax.checkpoint(block_step), start, items)
    scan_out = scanned.reshape(row_count, inner_width) + (skip_gain[None, :, None] * values).reshape(row_count, inner_width)
    gated_out = scan_out * jax.nn.silu(gate_in)
    return gated_out * lax.rsqrt(lax.optimization_barrier(jnp.mean(gated_out * gated_out, axis=-1, keepdims=True)) + EPS) * norm_gain[None, :]

def forward(hidden_in, w_in, w_out, conv_weight, conv_bias, dt_bias, a_log, skip_gain, norm_gain, pre_gain, segment, live_rows):
    normed = low(prenorm(hidden_in, pre_gain))
    projected = low_back(jnp.dot(normed, w_in, precision=HIGH))
    gated_norm = low(mixer_core(projected, conv_weight, conv_bias, dt_bias, a_log, skip_gain, norm_gain, segment))
    branch = jnp.dot(gated_norm, w_out, precision=HIGH)
    return live_rows[:, None] * (hidden_in + branch)

def reference(tokens, lengths, in_weight, out_weight, conv_weight, conv_bias, dt_bias, a_log, skip_gain, norm_gain, pre_gain, cotangent):
    device_count = lengths.shape[0] // SLOTS
    row_count = tokens.shape[0] // device_count
    width_model = tokens.shape[1]
    params = (in_weight.astype(jnp.float32), out_weight.astype(jnp.float32), conv_weight, conv_bias, dt_bias, a_log, skip_gain, norm_gain, pre_gain)
    blocks = (tokens.reshape(device_count, row_count, width_model), cotangent.reshape(device_count, row_count, width_model), lengths.reshape(device_count, SLOTS))

    def one_device(totals, block_item):
        token_rows, cot_rows, seq_lengths = block_item
        segment, live_rows = segments(seq_lengths, row_count)

        def layer_fn(hidden_in, *weights):
            return forward(hidden_in, *weights, segment, live_rows)
        output, pullback = jax.vjp(layer_fn, token_rows.astype(jnp.float32), *params)
        grads = pullback(cot_rows.astype(jnp.float32))
        totals = jax.tree.map(jnp.add, totals, tuple(grads[1:]))
        return (totals, (output.astype(jnp.bfloat16), grads[0]))
    zero_grads = tuple((jnp.zeros_like(param) for param in params))
    totals, (mixed, tokens_grad) = lax.scan(one_device, zero_grads, blocks)
    return (mixed.reshape(-1, width_model), tokens_grad.reshape(-1, width_model), totals[0], totals[1], totals[2], totals[3], totals[4], totals[5], totals[6], totals[7], totals[8])
```

```python
import functools

import jax
import jax.numpy as jnp
from jax import lax
from jax.experimental import pallas as pl
from jax.experimental.pallas import tpu as pltpu
from jax.sharding import PartitionSpec as P

SCAN_ROWS = 64


EPS = 1e-05
HIGH = lax.Precision.HIGHEST
BF = jnp.bfloat16
F32 = jnp.float32
NEG = -1e30
LANES = 128
QUAD = 4
WIDE1 = 896
VMEM_BYTES = 44 * 1024 * 1024


def mm(a, b):
    return lax.dot_general(a, b, (((1,), (0,)), ((), ())), preferred_element_type=F32)


def mm_t(a, b):
    return lax.dot_general(a, b, (((1,), (1,)), ((), ())), preferred_element_type=F32)


def mm_l(a, b):
    return lax.dot_general(a, b, (((0,), (0,)), ((), ())), preferred_element_type=F32)


def mm_high(a, b):
    return lax.dot_general(
        a, b, (((1,), (0,)), ((), ())), precision=HIGH, preferred_element_type=F32
    )


def call(kernel, out_shapes, inputs, scratch=(), flops=1e8, name=None):
    in_specs = [
        pl.BlockSpec(memory_space=pltpu.SMEM if a.dtype == jnp.int32 else pltpu.VMEM)
        for a in inputs
    ]
    shapes = [jax.ShapeDtypeStruct(s, d) for s, d in out_shapes]
    nbytes = sum(a.size * a.dtype.itemsize for a in inputs) + sum(
        s.size * s.dtype.itemsize for s in shapes
    )
    return pl.pallas_call(
        kernel,
        out_shape=shapes,
        in_specs=in_specs,
        out_specs=[pl.BlockSpec(memory_space=pltpu.VMEM)] * len(shapes),
        scratch_shapes=list(scratch),
        cost_estimate=pl.CostEstimate(flops=int(flops), bytes_accessed=nbytes, transcendentals=0),
        compiler_params=pltpu.CompilerParams(vmem_limit_bytes=VMEM_BYTES),
        name=name,
    )(*inputs)


def iota(shape, axis):
    return lax.broadcasted_iota(jnp.int32, shape, axis)


def sigmoid(v):
    return 1.0 / (1.0 + jnp.exp(-v))


def softplus(v):
    return jnp.maximum(v, 0.0) + jnp.log1p(jnp.exp(-jnp.abs(v)))


def segment_of(position, ends):
    seg = jnp.zeros(position.shape, jnp.int32)
    for s in range(4):
        seg = seg + (position >= ends[:, s : s + 1]).astype(jnp.int32)
    return seg


def same_masks(ends, rows, taps):
    position = iota((rows, 1), 0)
    seg = segment_of(position, ends)
    masks = []
    for k in range(1, taps):
        seg_k = segment_of(position - k, ends)
        masks.append(((seg == seg_k) & (position >= k)).astype(F32))
    return masks


def scan_bias(ends, rows):
    seg_col = segment_of(iota((rows, 1), 0), ends)
    seg_row = segment_of(iota((1, rows), 1), ends)
    causal = (seg_col == seg_row) & (iota((rows, rows), 0) >= iota((rows, rows), 1))
    return jnp.where(causal, 0.0, NEG)


def tri_block(rows):
    i, j = iota((rows, rows), 0), iota((rows, rows), 1)
    return ((i >= j) & (i // SCAN_ROWS == j // SCAN_ROWS)).astype(F32)


def steps_of(dt_raw, dtb, neg_rate, rows):
    step = softplus(dt_raw + dtb)
    log_decay = step * neg_rate
    cum = mm_high(tri_block(rows), log_decay)
    return step, log_decay, cum


def decay_of(cum, cum_t, head, bias, cross):
    dist = cum[:, head : head + 1] - cum_t[head : head + 1, :]
    last = cum[SCAN_ROWS - 1 : SCAN_ROWS, head : head + 1]
    return jnp.exp(dist + cross * last + bias)


def conv_sum_of(xbc, cw, cb, masks):
    total = cb + cw[0:1, :] * xbc
    for k in range(1, len(masks) + 1):
        total = total + cw[k : k + 1, :] * (pltpu.roll(xbc, k, 0) * masks[k - 1])
    return total


def prep_kernel(me_ref, len_ref, tok_ref, cot_ref, w_ref, tokx_ref, ocot_ref, *rest):
    rows = tok_ref.shape[0]
    outs1, outs2, scr1, scr2 = rest[0:4], rest[4:8], rest[8], rest[9]
    t = me_ref[0] & (QUAD - 1)
    inner = outs2[0].shape[1] * QUAD
    heads = 32
    size = inner // heads
    own = heads // QUAD
    lane = iota((16, tok_ref.shape[1]), 1)
    end = jnp.int32(0)
    tail = jnp.zeros((16, tok_ref.shape[1]), jnp.int32)
    for s in range(4):
        end = end + len_ref[s]
        tail = tail + jnp.where(lane == s, end, 0)
    tokx_ref[0:rows, :] = tok_ref[...]
    tokx_ref[rows : rows + 16, :] = tail.astype(F32).astype(BF)
    live = (iota((rows, 1), 0) < end).astype(F32)
    ocot_ref[...] = (cot_ref[...].astype(F32) * live).astype(BF)
    w = w_ref[...].astype(F32)
    nrow = w.shape[0]
    conv_end = w.shape[1] - heads
    shared = w[:, 2 * inner : conv_end]
    dts = w[:, conv_end:].astype(BF)
    for q in range(QUAD):
        zs, xs = [], []
        for k in range(own):
            at = (k * QUAD + q) * size
            zs.append(w[:, at : at + size])
            xs.append(w[:, inner + at : inner + at + size])
        pick = (iota((heads, LANES), 0) == iota((heads, LANES), 1) * QUAD + q) & (
            iota((heads, LANES), 1) < own
        )
        dt_own = mm(dts, pick.astype(BF))
        scr2[q] = jnp.concatenate(zs, 1).astype(BF)
        scr1[q] = jnp.concatenate(xs + [shared, dt_own], 1).astype(BF)
    for r in range(QUAD):
        outs1[r][...] = scr1[t ^ r]
        outs2[r][...] = scr2[t ^ r]


def join_kernel(me_ref, *refs):
    t = me_ref[0] & (QUAD - 1)
    out = refs[QUAD]
    nrow = refs[0].shape[0]
    for r in range(QUAD):
        out[pl.ds(pl.multiple_of((t ^ r) * nrow, nrow), nrow), :] = refs[r][...]


def project_kernel(me_ref, *refs):
    chunks = 8
    toks, ws = refs[0:QUAD], refs[QUAD : QUAD + chunks]
    gain_ref, norm_ref, proj_ref, ends_ref = refs[QUAD + chunks : QUAD + chunks + 4]
    zy = me_ref[0] // QUAD
    rows = ends_ref.shape[1]
    for r in range(QUAD):
        hidden = toks[r][0:rows, :].astype(F32)
        scale = lax.rsqrt(jnp.mean(hidden * hidden, axis=1, keepdims=True) + EPS)
        for k in range(chunks):
            at = pl.ds(pl.multiple_of((zy ^ k) * LANES, LANES), LANES)
            part = toks[r][0:rows, at].astype(F32) * scale * gain_ref[:, at]
            norm_ref[r * rows : (r + 1) * rows, k * LANES : (k + 1) * LANES] = part.astype(BF)
        ends_ref[r : r + 1, :] = toks[r][rows : rows + 16, 0:LANES].astype(F32)[0:1, :]
    w = jnp.concatenate([c[...] for c in ws], axis=0)
    proj_ref[...] = mm(norm_ref[...], w)


def scan_kernel(proj_ref, ends_ref, cw_ref, cb_ref, head_ref, out_ref):
    rows = LANES
    width = out_ref.shape[1]
    own = 8
    size = width // own
    state = LANES
    convw = width + 2 * state
    dtb, rate, skip = head_ref[0:1, :], head_ref[1:2, :], head_ref[2:3, :]
    neg_rate = -jnp.exp(rate)
    cross = ((iota((rows, rows), 0) >= SCAN_ROWS) & (iota((rows, rows), 1) < SCAN_ROWS)).astype(F32)

    def body(b, carry):
        at = pl.ds(pl.multiple_of(b * rows, rows), rows)
        ends = ends_ref[pl.ds(b, 1), :].astype(jnp.int32)
        bias = scan_bias(ends, rows)
        masks = same_masks(ends, rows, 4)
        xbc = proj_ref[at, 0:convw]
        conv = conv_sum_of(xbc, cw_ref[...], cb_ref[...], masks)
        act = conv * sigmoid(conv)
        key, read = act[:, width : width + state], act[:, width + state : convw]
        scores = mm_t(read.astype(BF), key.astype(BF))
        step, _, cum = steps_of(proj_ref[at, convw : convw + LANES], dtb, neg_rate, rows)
        cum_t = cum.T
        for h in range(own):
            x = act[:, h * size : (h + 1) * size]
            weight = scores * decay_of(cum, cum_t, h, bias, cross)
            y = mm(weight.astype(BF), (x * step[:, h : h + 1]).astype(BF))
            out_ref[at, h * size : (h + 1) * size] = y + skip[:, h : h + 1] * x
        return carry

    lax.fori_loop(0, ends_ref.shape[0], body, 0)


def cot_kernel(me_ref, *refs):
    chunks = 8
    ws, cots = refs[0:chunks], refs[chunks : chunks + QUAD]
    wfull_ref, cot_ref, dgn_ref = refs[chunks + QUAD :]
    zy = me_ref[0] // QUAD
    size = ws[0].shape[0]
    rows = cots[0].shape[0]
    for k in range(chunks):
        wfull_ref[pl.ds(pl.multiple_of((zy ^ k) * size, size), size), :] = ws[k][...]
    for r in range(QUAD):
        cot_ref[r * rows : (r + 1) * rows, :] = cots[r][...]
    dgn_ref[...] = mm_t(cot_ref[...], wfull_ref[...])


def gate_kernel(*refs):
    chunks = 8
    ws = refs[0:chunks]
    norm_ref, scan_ref, dgn_ref, gain_ref, z_ref, stat_ref = refs[chunks:]
    w = jnp.concatenate([c[...] for c in ws], axis=0)
    z = mm(norm_ref[...], w)
    z_ref[...] = z
    gated = scan_ref[...] * (z * sigmoid(z))
    s1 = jnp.sum(gated * gated, axis=1, keepdims=True)
    s2 = jnp.sum(gain_ref[...] * dgn_ref[...] * gated, axis=1, keepdims=True)
    lane = iota((z.shape[0], LANES), 1)
    both = jnp.where(lane == 0, s1, 0.0) + jnp.where(lane == 1, s2, 0.0)
    stat_ref[...] = both.T[0:8, :]


def ungate_kernel(inner, *refs):
    stats = refs[0:QUAD]
    z_ref, scan_ref, dgn_ref, gain_ref, norm_ref, gn_ref, dscan_ref, dz_ref, ngain_ref = refs[
        QUAD : QUAD + 9
    ]
    outs = refs[QUAD + 9 :]
    rows = stats[0].shape[1] // QUAD
    total = stats[0][...]
    for r in range(1, QUAD):
        total = total + jnp.concatenate(
            [stats[r][:, (b ^ r) * rows : ((b ^ r) + 1) * rows] for b in range(QUAD)], 1
        )
    pad = jnp.concatenate([total, jnp.zeros((LANES - 8, total.shape[1]), F32)], 0).T
    s1, s2 = pad[:, 0:1], pad[:, 1:2]
    r = lax.rsqrt(s1 / inner + EPS)
    z = z_ref[...]
    sig = sigmoid(z)
    silu = z * sig
    scan = scan_ref[...]
    gain = gain_ref[...]
    gated = scan * silu
    unit = gated * r
    gn_ref[...] = (unit * gain).astype(BF)
    dgn = dgn_ref[...]
    ngain_ref[...] = jnp.sum(dgn * unit, axis=0, keepdims=True)
    dgated = r * (gain * dgn) - unit * (r * r * s2 / inner)
    dscan_ref[...] = dgated * silu
    dz = (dgated * scan * (sig * (1.0 + z * (1.0 - sig)))).astype(BF)
    dz_ref[...] = dz
    for k in (1, 3, 5, 7, 2, 4, 6, 0):
        lhs = norm_ref[:, k * LANES : (k + 1) * LANES]
        outs[k][...] = mm_l(lhs, dz).astype(BF)


def outgrad_kernel(me_ref, gn_ref, cot_ref, *refs):
    outs, scr = refs[0:8], refs[8]
    zy = me_ref[0] // QUAD
    size = outs[0].shape[0]
    scr[...] = mm_l(gn_ref[...], cot_ref[...]).astype(BF)
    for k in range(8):
        outs[k][...] = scr[pl.ds(pl.multiple_of((zy ^ k) * size, size), size), :]


def branch_kernel(gn_ref, w_ref, *outs):
    full = mm(gn_ref[...], w_ref[...])
    rows = outs[0].shape[0]
    for r in range(QUAD):
        outs[r][...] = full[r * rows : (r + 1) * rows, :].astype(outs[r].dtype)


def scan_back_kernel(proj_ref, dscan_ref, ends_ref, cw_ref, cb_ref, head_ref, pc_ref, small_ref):
    rows = LANES
    width = dscan_ref.shape[1]
    own = 8
    size = width // own
    state = LANES
    convw = width + 2 * state
    dtb, rate, skip = head_ref[0:1, :], head_ref[1:2, :], head_ref[2:3, :]
    neg_rate = -jnp.exp(rate)
    cross = ((iota((rows, rows), 0) >= SCAN_ROWS) & (iota((rows, rows), 1) < SCAN_ROWS)).astype(F32)
    after = (iota((rows, rows), 1) >= iota((rows, rows), 0)).astype(F32)
    lane = iota((rows, LANES), 1)
    lane1 = iota((1, LANES), 1)
    small_ref[...] = jnp.zeros(small_ref.shape, F32)

    def body(b, carry):
        at = pl.ds(pl.multiple_of(b * rows, rows), rows)
        ends = ends_ref[pl.ds(b, 1), :].astype(jnp.int32)
        bias = scan_bias(ends, rows)
        masks = same_masks(ends, rows, 4)
        xbc = proj_ref[at, 0:convw]
        cw = cw_ref[...]
        conv = conv_sum_of(xbc, cw, cb_ref[...], masks)
        sig = sigmoid(conv)
        act = conv * sig
        key = act[:, width : width + state].astype(BF)
        read = act[:, width + state : convw].astype(BF)
        scores = mm_t(read, key)
        raw = proj_ref[at, convw : convw + LANES]
        step, log_decay, cum = steps_of(raw, dtb, neg_rate, rows)
        cum_t = cum.T
        dscores = jnp.zeros((rows, rows), F32)
        row_sums = jnp.zeros((rows, LANES), F32)
        dstep = jnp.zeros((rows, LANES), F32)
        dskip = jnp.zeros((1, LANES), F32)
        col_sums = []
        dxs = []
        for h in range(own):
            x = act[:, h * size : (h + 1) * size]
            s = step[:, h : h + 1]
            decay = decay_of(cum, cum_t, h, bias, cross)
            weight = scores * decay
            xs = (x * s).astype(BF)
            dy = dscan_ref[at, h * size : (h + 1) * size]
            dyl = dy.astype(BF)
            dweight = mm_t(dyl, xs)
            dx_s = mm_l(weight.astype(BF), dyl)
            dscores = dscores + dweight * decay
            t = dweight * weight
            row_sums = row_sums + jnp.where(lane == h, jnp.sum(t, axis=1, keepdims=True), 0.0)
            col_sums.append(jnp.sum(t, axis=0, keepdims=True))
            dstep = dstep + jnp.where(lane == h, jnp.sum(dx_s * x, axis=1, keepdims=True), 0.0)
            dskip = dskip + jnp.where(lane1 == h, jnp.sum(dy * x), 0.0)
            dxs.append(dx_s * s + skip[:, h : h + 1] * dy)
        cols = jnp.concatenate(col_sums + [jnp.zeros((rows - own, rows), F32)], 0).T
        dlog = mm_high(after, row_sums - cols)
        dstep = dstep + dlog * neg_rate
        ddt = dstep * sigmoid(raw + dtb)
        ddt = jnp.where(lane < own, ddt, 0.0)
        low = dscores.astype(BF)
        dkey = mm_l(low, read)
        dread = mm(low, key)
        dconv = jnp.concatenate(dxs + [dkey, dread], 1) * (sig * (1.0 + conv * (1.0 - sig)))
        dxbc = cw[0:1, :] * dconv
        small_ref[0:1, 0:convw] += jnp.sum(dconv * xbc, axis=0, keepdims=True)
        for k in range(1, 4):
            masked = dconv * masks[k - 1]
            dxbc = dxbc + cw[k : k + 1, :] * pltpu.roll(masked, rows - k, 0)
            small_ref[k : k + 1, 0:convw] += jnp.sum(
                masked * pltpu.roll(xbc, k, 0), axis=0, keepdims=True
            )
        small_ref[4:5, 0:convw] += jnp.sum(dconv, axis=0, keepdims=True)
        small_ref[5:6, 0:LANES] += jnp.sum(ddt, axis=0, keepdims=True)
        small_ref[6:7, 0:LANES] += jnp.where(
            lane1 < own, jnp.sum(dlog * log_decay, axis=0, keepdims=True), 0.0
        )
        small_ref[7:8, 0:LANES] += dskip
        pc_ref[at, 0:convw] = dxbc.astype(BF)
        pc_ref[at, convw : convw + LANES] = ddt.astype(BF)
        return carry

    lax.fori_loop(0, ends_ref.shape[0], body, 0)


def ingrad_kernel(order, norm_ref, pc_ref, *outs):
    for n, k in enumerate(order):
        lhs = norm_ref[:, k * LANES : (k + 1) * LANES]
        outs[n][...] = mm_l(lhs, pc_ref[...]).astype(BF)


def normcot_kernel(me_ref, *refs):
    chunks = 8
    w1, w2 = refs[0:chunks], refs[chunks : 2 * chunks]
    pc_ref, dz_ref, small_in, ngain_ref = refs[2 * chunks : 2 * chunks + 4]
    toks = refs[2 * chunks + 4 : 2 * chunks + 4 + QUAD]
    outs = refs[2 * chunks + 4 + QUAD : 2 * chunks + 4 + 2 * QUAD]
    small_ref = refs[2 * chunks + 4 + 2 * QUAD]
    zy = me_ref[0] // QUAD
    rows = outs[0].shape[0]
    small_ref[...] = small_in[...]
    small_ref[8:9, 0 : ngain_ref.shape[1]] = ngain_ref[...]
    for k in range(chunks):
        part = mm_t(pc_ref[...], w1[k][...]) + mm_t(dz_ref[...], w2[k][...])
        at = pl.ds(pl.multiple_of((zy ^ k) * LANES, LANES), LANES)
        for r in range(QUAD):
            outs[r][:, at] = part[r * rows : (r + 1) * rows, :]
    pre = jnp.zeros((1, outs[0].shape[1]), F32)
    for r in range(QUAD):
        hidden = toks[r][0:rows, :].astype(F32)
        scale = lax.rsqrt(jnp.mean(hidden * hidden, axis=1, keepdims=True) + EPS)
        pre = pre + jnp.sum(outs[r][...] * (hidden * scale), axis=0, keepdims=True)
    small_ref[9:10, :] = pre


def pair_add_kernel(a0, b0, a2, b2, o0, o2):
    o0[...] = a0[...] + b0[...]
    o2[...] = a2[...] + b2[...]


def mixed_kernel(len_ref, tok_ref, a_ref, b_ref, out_ref):
    rows = tok_ref.shape[0]
    end = len_ref[0] + len_ref[1] + len_ref[2] + len_ref[3]
    live = (iota((rows, 1), 0) < end).astype(F32)
    total = tok_ref[...].astype(F32) + (a_ref[...] + b_ref[...])
    out_ref[...] = (live * total).astype(BF)


def tokgrad_kernel(tok_ref, cot_ref, gain_ref, a_ref, b_ref, out_ref):
    hidden = tok_ref[...].astype(F32)
    scale = lax.rsqrt(jnp.mean(hidden * hidden, axis=1, keepdims=True) + EPS)
    dn = (a_ref[...] + b_ref[...]) * gain_ref[...]
    inner = jnp.mean(dn * hidden, axis=1, keepdims=True)
    out_ref[...] = cot_ref[...].astype(F32) + scale * dn - hidden * (scale * scale * scale * inner)


def total_kernel(me_ref, *refs):
    ins, outs, scr = refs[0:5], refs[5:9], refs[9]
    t = me_ref[0] & (QUAD - 1)
    total = ins[0][...].astype(F32)
    for a in ins[1:]:
        total = total + a[...].astype(F32)
    scr[...] = total.astype(scr.dtype)
    nrow = outs[0].shape[0]
    for r in range(QUAD):
        outs[r][...] = scr[pl.ds(pl.multiple_of((t ^ r) * nrow, nrow), nrow), :]


def sum5_kernel(a, b, c, d, e, out_ref):
    out_ref[...] = (
        a[...].astype(F32)
        + b[...].astype(F32)
        + c[...].astype(F32)
        + d[...].astype(F32)
        + e[...].astype(F32)
    )


def weave(out_ref, at, parts, size):
    for k in range(8):
        for half in range(QUAD // 2):
            pair = [p[:, k * size : (k + 1) * size] for p in parts[2 * half : 2 * half + 2]]
            lo = at + (k * QUAD + 2 * half) * size
            out_ref[:, lo : lo + 2 * size] = jnp.concatenate(pair, 1)


def pick_heads(parts, heads):
    total = None
    for q in range(QUAD):
        sel = (iota((LANES, heads), 1) == iota((LANES, heads), 0) * QUAD + q).astype(F32)
        got = mm_high(parts[q], sel)
        total = got if total is None else total + got
    return total


def finish_kernel(me_ref, *refs):
    p1, p2 = refs[0:4], refs[4:8]
    out_ref, scr1, scr2 = refs[8:]
    t = me_ref[0] & (QUAD - 1)
    for r in range(QUAD):
        scr1[t ^ r] = p1[r][...].astype(F32)
        scr2[t ^ r] = p2[r][...].astype(F32)
    width = scr2.shape[2]
    inner = width * QUAD
    size = inner // 32
    conv_end = out_ref.shape[1] - 32
    weave(out_ref, 0, [scr2[q] for q in range(QUAD)], size)
    weave(out_ref, inner, [scr1[q][:, 0:width] for q in range(QUAD)], size)
    shared = width + conv_end - 2 * inner
    out_ref[:, 2 * inner : conv_end] = (
        scr1[0][:, width:shared] + scr1[1][:, width:shared]
    ) + (scr1[2][:, width:shared] + scr1[3][:, width:shared])
    out_ref[:, conv_end:] = pick_heads([scr1[q][:, shared : shared + LANES] for q in range(QUAD)], 32)


def small_kernel(me_ref, *refs):
    parts = refs[0:4]
    cw_ref, cb_ref, dt_ref, al_ref, sk_ref, ng_ref, pg_ref, scr = refs[4:]
    t = me_ref[0] & (QUAD - 1)
    for r in range(QUAD):
        scr[t ^ r] = parts[r][...]
    inner = ng_ref.shape[1]
    width = inner // QUAD
    size = inner // 32
    shared = width + cb_ref.shape[1] - inner
    for out, lo, hi in ((cw_ref, 0, 4), (cb_ref, 4, 5)):
        weave(out, 0, [scr[q][lo:hi, 0:width] for q in range(QUAD)], size)
        out[:, inner:] = (scr[0][lo:hi, width:shared] + scr[1][lo:hi, width:shared]) + (
            scr[2][lo:hi, width:shared] + scr[3][lo:hi, width:shared]
        )
    heads = pick_heads([scr[q][0:8, 0:LANES] for q in range(QUAD)], 32)
    dt_ref[...] = heads[5:6, :]
    al_ref[...] = heads[6:7, :]
    sk_ref[...] = heads[7:8, :]
    weave(ng_ref, 0, [scr[q][8:9, 0:width] for q in range(QUAD)], size)
    pg_ref[...] = (scr[0][9:10, :] + scr[1][9:10, :]) + (scr[2][9:10, :] + scr[3][9:10, :])


def quad_shards(
    count,
    tokens,
    lengths,
    in_weight,
    out_weight,
    conv_weight,
    conv_bias,
    dt_bias,
    a_log,
    skip_gain,
    norm_gain,
    pre_gain,
    cotangent,
):
    chunks = count // QUAD
    rows, model = tokens.shape
    inner = norm_gain.shape[0]
    heads = dt_bias.shape[0]
    own = heads // QUAD
    width = inner // QUAD
    size = inner // heads
    nrow, proj_width = in_weight.shape
    state = (conv_bias.shape[0] - inner) // 2
    wide1 = width + 2 * state + LANES
    total_rows = QUAD * rows

    def swap(a, mask):
        return lax.ppermute(a, "dp", [(i, i ^ mask) for i in range(count)])

    def zy_mask(k):
        return k * QUAD

    def gather(mine):
        got = [None] * chunks
        got[0] = mine
        for k in range(2, chunks, 2):
            got[k] = swap(mine, zy_mask(k))
        for k in range(0, chunks, 2):
            got[k + 1] = swap(got[k], zy_mask(1))
        return got

    def scatter(parts):
        sent = {}
        for k in (2, 4, 6, 0):
            sent[k] = swap(parts[k + 1], zy_mask(1))
        back = []
        for k in (2, 4, 6):
            both = (parts[k].astype(F32) + sent[k].astype(F32)).astype(BF)
            back.append(swap(both, zy_mask(k)))
        return [parts[0], sent[0]] + back

    me_scalar = lax.axis_index("dp").astype(jnp.int32)
    me = me_scalar.reshape(1)
    member = me_scalar % QUAD

    def mine(a):
        return lax.dynamic_index_in_dim(
            a.reshape(a.shape[:-1] + (own, QUAD, a.shape[-1] // heads)), member, a.ndim, False
        ).reshape(a.shape[:-1] + (a.shape[-1] // QUAD,))

    cw = jnp.concatenate([mine(conv_weight[:, :inner]), conv_weight[:, inner:]], 1)
    cb = jnp.concatenate([mine(conv_bias[:inner]), conv_bias[inner:]])[None, :]
    by_head = jnp.stack([mine(dt_bias), mine(a_log), mine(skip_gain)])
    by_head = jnp.pad(by_head, ((0, 5), (0, LANES - own)))
    gain = mine(norm_gain)[None, :]
    pre = pre_gain[None, :]

    wout = gather(out_weight)
    prepped = call(
        prep_kernel,
        [((rows + 16, model), BF), ((rows, model), BF)]
        + [((nrow, wide1), BF)] * QUAD
        + [((nrow, width), BF)] * QUAD,
        [me, lengths, tokens, cotangent, in_weight],
        [pltpu.VMEM((QUAD, nrow, wide1), BF), pltpu.VMEM((QUAD, nrow, width), BF)],
        name="prep",
    )
    tokx, ocot, cut1, cut2 = prepped[0], prepped[1], prepped[2:6], prepped[6:10]

    def join(cut):
        got = [cut[0]] + [swap(cut[r], r) for r in range(1, QUAD)]
        return call(
            join_kernel, [((QUAD * nrow, cut[0].shape[1]), BF)], [me] + got, name="join"
        )[0]

    def share(a):
        across = swap(a, 2)
        return [a, swap(a, 1), across, swap(across, 1)]

    own1 = join(cut1)
    w1 = gather(own1)
    toks = share(tokx)
    own2 = join(cut2)
    w2 = gather(own2)
    cots = share(ocot)

    normed, proj, ends = call(
        project_kernel,
        [((total_rows, model), BF), ((total_rows, wide1), F32), ((QUAD, rows), F32)],
        [me] + toks + w1 + [pre],
        flops=2 * total_rows * model * wide1,
        name="project",
    )
    (scan_out,) = call(
        scan_kernel,
        [((total_rows, width), F32)],
        [proj, ends, cw, cb, by_head],
        flops=2e9,
        name="scan",
    )
    w_full, cot_all, dgn = call(
        cot_kernel,
        [((width, model), BF), ((total_rows, model), BF), ((total_rows, width), F32)],
        [me] + wout + cots,
        flops=2 * total_rows * model * width,
        name="normcot",
    )
    z, stat = call(
        gate_kernel,
        [((total_rows, width), F32), ((8, total_rows), F32)],
        w2 + [normed, scan_out, dgn, gain],
        flops=2 * total_rows * model * width,
        name="gate",
    )
    stats = [stat] + [swap(stat, r) for r in range(1, QUAD)]
    ungated = call(
        functools.partial(ungate_kernel, float(inner)),
        [
            ((total_rows, width), BF),
            ((total_rows, width), F32),
            ((total_rows, width), BF),
            ((1, width), F32),
        ]
        + [((LANES, width), BF)] * chunks,
        stats + [z, scan_out, dgn, gain, normed],
        flops=2 * total_rows * model * width,
        name="ungate",
    )
    gn, dscan, dz, ngain_part = ungated[0:4]
    parts2 = scatter(ungated[4:])
    ograd = call(
        outgrad_kernel,
        [((size, model), BF)] * chunks,
        [me, gn, cot_all],
        [pltpu.VMEM((width, model), BF)],
        flops=2 * total_rows * model * width,
        name="outgrad",
    )
    parts3 = scatter(ograd)
    branch = call(
        branch_kernel,
        [((rows, model), F32)] * QUAD,
        [gn, w_full],
        flops=2 * total_rows * model * width,
        name="branch",
    )
    pc1, small = call(
        scan_back_kernel,
        [((total_rows, wide1), BF), ((16, model), F32)],
        [proj, dscan, ends, cw, cb, by_head],
        flops=6e9,
        name="scanback",
    )
    grads = [None] * chunks
    for order in ((3, 5, 7, 1), (2, 4, 6, 0)):
        got = call(
            functools.partial(ingrad_kernel, order),
            [((LANES, wide1), BF)] * len(order),
            [normed, pc1],
            flops=total_rows * model * wide1,
            name="ingrad",
        )
        for n, k in enumerate(order):
            grads[k] = got[n]
    parts1 = scatter(grads)

    def pair_sum(blocks):
        one, three = swap(blocks[1], 1), swap(blocks[3], 1)
        keep, send = call(
            pair_add_kernel,
            [(blocks[0].shape, F32)] * 2,
            [blocks[0], one, blocks[2], three],
            name="pair_add",
        )
        return keep, swap(send, 2)

    pre_parts = call(
        normcot_kernel,
        [((rows, model), F32)] * QUAD + [((16, model), F32)],
        [me] + w1 + w2 + [pc1, dz, small, ngain_part] + toks,
        flops=2 * total_rows * model * (wide1 + width),
        name="normedcot",
    )
    keep_m, got_m = pair_sum(branch)
    (mixed,) = call(
        mixed_kernel, [((rows, model), BF)], [lengths, tokens, keep_m, got_m], name="mixed"
    )
    keep_t, got_t = pair_sum(pre_parts[0:QUAD])
    (tokens_grad,) = call(
        tokgrad_kernel,
        [((rows, model), F32)],
        [tokens, ocot, pre, keep_t, got_t],
        name="tokgrad",
    )

    packed = pre_parts[QUAD]
    packed = packed + swap(packed, zy_mask(1))
    around = [swap(packed, zy_mask(k)) for k in range(2, chunks, 2)]
    packed = (packed + around[0]) + (around[1] + around[2])
    smalls = [packed] + [swap(packed, r) for r in range(1, QUAD)]
    small_out = call(
        small_kernel,
        [
            (conv_weight.shape, F32),
            ((1, conv_bias.shape[0]), F32),
            ((1, heads), F32),
            ((1, heads), F32),
            ((1, heads), F32),
            ((1, inner), F32),
            ((1, model), F32),
        ],
        [me] + smalls,
        [pltpu.VMEM((QUAD, 16, model), F32)],
        name="small",
    )

    (out_shard,) = call(sum5_kernel, [((size, model), F32)], parts3, name="outsum")

    def member_cut(parts):
        wide = parts[0].shape[1]
        cut = call(
            total_kernel,
            [((nrow, wide), BF)] * QUAD,
            [me] + parts,
            [pltpu.VMEM((QUAD * nrow, wide), BF)],
            name="total",
        )
        return [cut[0]] + [swap(cut[r], r) for r in range(1, QUAD)]

    got2 = member_cut(parts2)
    got1 = member_cut(parts1)
    (in_shard,) = call(
        finish_kernel,
        [((nrow, proj_width), F32)],
        [me] + got1 + got2,
        [pltpu.VMEM((QUAD, nrow, wide1), F32), pltpu.VMEM((QUAD, nrow, width), F32)],
        name="finish",
    )
    return (
        mixed,
        tokens_grad,
        in_shard,
        out_shard,
        small_out[0],
        small_out[1].reshape(-1),
        small_out[2].reshape(-1),
        small_out[3].reshape(-1),
        small_out[4].reshape(-1),
        small_out[5].reshape(-1),
        small_out[6].reshape(-1),
    )


def prenorm(hidden_in, gain_row):
    return (
        hidden_in
        * lax.rsqrt(jnp.mean(hidden_in * hidden_in, axis=-1, keepdims=True) + EPS)
        * gain_row
    )


def shifted(array, offset, filler):
    padding = jnp.full((offset,) + array.shape[1:], filler, array.dtype)
    return jnp.concatenate([padding, array[:-offset]], axis=0)


def segments(seq_lengths, row_count):
    seq_ends = jnp.cumsum(seq_lengths, dtype=jnp.int32)
    position = jnp.arange(row_count, dtype=jnp.int32)
    segment = jnp.sum(
        (position[:, None] >= seq_ends[None, :]).astype(jnp.int32), axis=1, dtype=jnp.int32
    )
    live_rows = (position < seq_ends[-1]).astype(jnp.float32)
    return (segment, live_rows)


def block_step(carry, block_item):
    state_mat, prev_segment = carry
    values, key_rows, read_rows, step_size, log_decay, block_segment = block_item
    cumulative = jnp.cumsum(log_decay, axis=0)
    position = jnp.arange(block_segment.shape[0], dtype=jnp.int32)
    causal = (block_segment[:, None] == block_segment[None, :]) & (
        position[:, None] >= position[None, :]
    )
    distance = cumulative[:, None, :] - cumulative[None, :, :]
    decay_mask = jnp.where(
        causal[:, :, None], jnp.exp(jnp.where(causal[:, :, None], distance, 0.0)), 0.0
    )
    scores = jnp.dot(read_rows, key_rows.T, precision=HIGH)
    weighting = scores[:, :, None] * decay_mask * step_size[None, :, :]
    inside = jnp.einsum("ijh,jhp->ihp", weighting, values, precision=HIGH)
    entering = (block_segment == prev_segment).astype(jnp.float32)
    carried = jnp.einsum("in,hnp->ihp", read_rows, state_mat, precision=HIGH)
    carried = carried * (jnp.exp(cumulative) * entering[:, None])[:, :, None]
    last_same = (block_segment == block_segment[-1]).astype(jnp.float32)
    tail_weight = jnp.exp(cumulative[-1][None, :] - cumulative) * last_same[:, None] * step_size
    new_state = state_mat * (jnp.exp(cumulative[-1]) * entering[-1])[:, None, None]
    new_state = new_state + jnp.einsum(
        "jn,jh,jhp->hnp", key_rows, tail_weight, values, precision=HIGH
    )
    return ((new_state, block_segment[-1]), inside + carried)


def mixer_core(projected, conv_weight, conv_bias, dt_bias, a_log, skip_gain, norm_gain, segment):
    inner_width = norm_gain.shape[0]
    head_count = dt_bias.shape[0]
    conv_width = conv_bias.shape[0]
    state_width = (conv_width - inner_width) // 2
    head_size = inner_width // head_count
    row_count = projected.shape[0]
    gate_in = projected[:, :inner_width]
    conv_src = projected[:, inner_width : inner_width + conv_width]
    dt_raw = projected[:, inner_width + conv_width :]
    conv_sum = conv_bias[None, :] + conv_weight[0][None, :] * conv_src
    for offset in range(1, conv_weight.shape[0]):
        same_rows = (segment == shifted(segment, offset, -1)).astype(jnp.float32)
        conv_sum = (
            conv_sum
            + conv_weight[offset][None, :] * shifted(conv_src, offset, 0.0) * same_rows[:, None]
        )
    activated = jax.nn.silu(conv_sum)
    values = activated[:, :inner_width].reshape(row_count, head_count, head_size)
    key_rows = activated[:, inner_width : inner_width + state_width]
    read_rows = activated[:, inner_width + state_width :]
    step_size = jax.nn.softplus(dt_raw + dt_bias[None, :])
    log_decay = -step_size * jnp.exp(a_log)[None, :]
    blocks = row_count // SCAN_ROWS
    items = (
        values.reshape(blocks, SCAN_ROWS, head_count, head_size),
        key_rows.reshape(blocks, SCAN_ROWS, state_width),
        read_rows.reshape(blocks, SCAN_ROWS, state_width),
        step_size.reshape(blocks, SCAN_ROWS, head_count),
        log_decay.reshape(blocks, SCAN_ROWS, head_count),
        segment.reshape(blocks, SCAN_ROWS),
    )
    start = (jnp.zeros((head_count, state_width, head_size), jnp.float32), jnp.array(-1, jnp.int32))
    _, scanned = lax.scan(jax.checkpoint(block_step), start, items)
    scan_out = scanned.reshape(row_count, inner_width) + (
        skip_gain[None, :, None] * values
    ).reshape(row_count, inner_width)
    gated_out = scan_out * jax.nn.silu(gate_in)
    return (
        gated_out
        * lax.rsqrt(jnp.mean(gated_out * gated_out, axis=-1, keepdims=True) + EPS)
        * norm_gain[None, :]
    )


def shards(
    tokens,
    lengths,
    in_weight,
    out_weight,
    conv_weight,
    conv_bias,
    dt_bias,
    a_log,
    skip_gain,
    norm_gain,
    pre_gain,
    cotangent,
):
    w_in, w_out = (
        lax.all_gather(in_weight, "dp", axis=0, tiled=True),
        lax.all_gather(out_weight, "dp", axis=0, tiled=True),
    )
    segment, live_rows = segments(lengths, tokens.shape[0])
    hidden_in = tokens.astype(jnp.float32)
    normed, norm_back = jax.vjp(prenorm, hidden_in, pre_gain)
    normed_low = normed.astype(jnp.bfloat16)
    projected = jnp.dot(normed_low, w_in, preferred_element_type=jnp.float32)
    proj_width = projected.shape[1]

    def mixer_local(proj_rows, conv_w, conv_b, bias_dt, decay_log, skip_w, gain_w):
        return mixer_core(proj_rows, conv_w, conv_b, bias_dt, decay_log, skip_w, gain_w, segment)

    gated_norm, mixer_back = jax.vjp(
        mixer_local, projected, conv_weight, conv_bias, dt_bias, a_log, skip_gain, norm_gain
    )
    gated_low = gated_norm.astype(jnp.bfloat16)
    branch = jnp.dot(gated_low, w_out, preferred_element_type=jnp.float32)
    mixed = (live_rows[:, None] * (hidden_in + branch)).astype(jnp.bfloat16)
    w_in, w_out = (
        lax.all_gather(in_weight, "dp", axis=0, tiled=True),
        lax.all_gather(out_weight, "dp", axis=0, tiled=True),
    )
    out_cot = cotangent.astype(jnp.float32) * live_rows[:, None]
    out_cot_low = out_cot.astype(jnp.bfloat16)
    norm_cot = lax.dot_general(
        out_cot_low, w_out, (((1,), (1,)), ((), ())), preferred_element_type=jnp.float32
    )
    proj_cot, conv_w_grad, conv_b_grad, bias_dt_grad, decay_grad, skip_grad, gain_grad = mixer_back(
        norm_cot
    )
    proj_cot_low = proj_cot.astype(jnp.bfloat16)
    normed_cot = lax.dot_general(
        proj_cot_low, w_in, (((1,), (1,)), ((), ())), preferred_element_type=jnp.float32
    )
    hidden_cot, pre_grad = norm_back(normed_cot)
    tokens_grad = out_cot + hidden_cot
    out_grad = lax.dot_general(
        gated_low, out_cot_low, (((0,), (0,)), ((), ())), preferred_element_type=jnp.float32
    )
    in_grad = lax.dot_general(
        normed_low, proj_cot_low, (((0,), (0,)), ((), ())), preferred_element_type=jnp.float32
    )
    in_wide = in_grad.reshape(2 * in_grad.shape[0], proj_width // 2)
    in_folded, out_shard = (
        lax.psum_scatter(in_wide, "dp", scatter_dimension=0, tiled=True),
        lax.psum_scatter(out_grad, "dp", scatter_dimension=0, tiled=True),
    )
    in_shard = in_folded.reshape(in_weight.shape[0], proj_width)
    summed = lax.psum(
        (conv_w_grad, conv_b_grad, bias_dt_grad, decay_grad, skip_grad, gain_grad, pre_grad), "dp"
    )
    return (
        mixed,
        tokens_grad,
        in_shard,
        out_shard,
        summed[0],
        summed[1],
        summed[2],
        summed[3],
        summed[4],
        summed[5],
        summed[6],
    )


def solution(mesh):
    count = mesh.shape["dp"]
    body = functools.partial(quad_shards, count) if count == 32 else shards
    return jax.shard_map(
        body,
        mesh=mesh,
        in_specs=(
            P("dp", None),
            P("dp"),
            P("dp", None),
            P("dp", None),
            P(),
            P(),
            P(),
            P(),
            P(),
            P(),
            P(),
            P("dp", None),
        ),
        out_specs=(
            P("dp", None),
            P("dp", None),
            P("dp", None),
            P("dp", None),
            P(),
            P(),
            P(),
            P(),
            P(),
            P(),
            P(),
        ),
        check_vma=False,
    )
```

```python
import functools

import jax
import jax.numpy as jnp
from jax import lax
from jax.experimental import pallas as pl
from jax.experimental.pallas import tpu as pltpu
from jax.sharding import PartitionSpec as P

SCAN_ROWS = 64


EPS = 1e-05
HIGH = lax.Precision.HIGHEST
BF = jnp.bfloat16
F32 = jnp.float32
NEG = -1e30
LANES = 128
QUAD = 4
SMALL = 8
VMEM_BYTES = 44 * 1024 * 1024
RAW_BYTES = 60 * 1024 * 1024


def mm(a, b):
    return lax.dot_general(a, b, (((1,), (0,)), ((), ())), preferred_element_type=F32)


def mm_t(a, b):
    return lax.dot_general(a, b, (((1,), (1,)), ((), ())), preferred_element_type=F32)


def mm_l(a, b):
    return lax.dot_general(a, b, (((0,), (0,)), ((), ())), preferred_element_type=F32)


def mm_high(a, b):
    return lax.dot_general(
        a, b, (((1,), (0,)), ((), ())), precision=HIGH, preferred_element_type=F32
    )


def call(kernel, out_shapes, inputs, scratch=(), flops=1e3, name=None, raw=(), limit=VMEM_BYTES):
    in_specs = [
        pl.BlockSpec(
            memory_space=pltpu.HBM
            if n in raw
            else (pltpu.SMEM if a.dtype == jnp.int32 else pltpu.VMEM)
        )
        for n, a in enumerate(inputs)
    ]
    shapes = [jax.ShapeDtypeStruct(s, d) for s, d in out_shapes]
    return pl.pallas_call(
        kernel,
        out_shape=shapes,
        in_specs=in_specs,
        out_specs=[pl.BlockSpec(memory_space=pltpu.VMEM)] * len(shapes),
        scratch_shapes=list(scratch),
        cost_estimate=pl.CostEstimate(flops=int(flops), bytes_accessed=1024, transcendentals=0),
        compiler_params=pltpu.CompilerParams(vmem_limit_bytes=limit),
        name=name,
    )(*inputs)


def iota(shape, axis):
    return lax.broadcasted_iota(jnp.int32, shape, axis)


def sigmoid(v):
    return 1.0 / (1.0 + jnp.exp(-v))


def softplus(v):
    return jnp.maximum(v, 0.0) + jnp.log1p(jnp.exp(-jnp.abs(v)))


def segment_of(position, ends):
    seg = jnp.zeros(position.shape, jnp.int32)
    for s in range(4):
        seg = seg + (position >= ends[:, s : s + 1]).astype(jnp.int32)
    return seg


def same_masks(ends, rows, taps):
    position = iota((rows, 1), 0)
    seg = segment_of(position, ends)
    masks = []
    for k in range(1, taps):
        seg_k = segment_of(position - k, ends)
        masks.append(((seg == seg_k) & (position >= k)).astype(F32))
    return masks


def scan_bias(ends, rows):
    seg_col = segment_of(iota((rows, 1), 0), ends)
    seg_row = segment_of(iota((1, rows), 1), ends)
    causal = (seg_col == seg_row) & (iota((rows, rows), 0) >= iota((rows, rows), 1))
    return jnp.where(causal, 0.0, NEG)


def tri_block(rows):
    i, j = iota((rows, rows), 0), iota((rows, rows), 1)
    return ((i >= j) & (i // SCAN_ROWS == j // SCAN_ROWS)).astype(F32)


def steps_of(dt_raw, dtb, neg_rate, rows):
    step = softplus(dt_raw + dtb)
    log_decay = step * neg_rate
    cum = mm_high(tri_block(rows), log_decay)
    return step, log_decay, cum


def decay_of(cum, cum_t, head, bias, cross):
    dist = cum[:, head : head + 1] - cum_t[head : head + 1, :]
    last = cum[SCAN_ROWS - 1 : SCAN_ROWS, head : head + 1]
    return jnp.exp(dist + cross * last + bias)


def conv_sum_of(xbc, cw, cb, masks):
    total = cb + cw[0:1, :] * xbc
    for k in range(1, len(masks) + 1):
        total = total + cw[k : k + 1, :] * (pltpu.roll(xbc, k, 0) * masks[k - 1])
    return total


def pair_lanes(row, pair, low):
    return jnp.where(low, row[:, 2 * pair : 2 * pair + 1], row[:, 2 * pair + 1 : 2 * pair + 2])


def scan_kernel(proj_ref, ends_ref, cw_ref, head_ref, out_ref):
    rows = LANES
    width = out_ref.shape[1]
    pairs = width // LANES
    convw = width + 2 * LANES
    dtb, rate, skip = head_ref[0:1, :], head_ref[1:2, :], head_ref[2:3, :]
    neg_rate = -jnp.exp(rate)
    cross = ((iota((rows, rows), 0) >= SCAN_ROWS) & (iota((rows, rows), 1) < SCAN_ROWS)).astype(F32)
    low = iota((rows, LANES), 1) < LANES // 2

    def body(b, carry):
        at = pl.ds(pl.multiple_of(b * rows, rows), rows)
        ends = ends_ref[pl.ds(b, 1), :].astype(jnp.int32)
        bias = scan_bias(ends, rows)
        masks = same_masks(ends, rows, 4)
        xbc = proj_ref[at, 0:convw]
        conv = conv_sum_of(xbc, cw_ref[...], cw_ref[4:5, :], masks)
        act = conv * sigmoid(conv)
        key, read = act[:, width : width + LANES], act[:, width + LANES : convw]
        scores = mm_t(read.astype(BF), key.astype(BF))
        step, _, cum = steps_of(proj_ref[at, convw : convw + LANES], dtb, neg_rate, rows)
        cum_t = cum.T
        for p in range(pairs):
            lanes = slice(p * LANES, (p + 1) * LANES)
            x = act[:, lanes]
            xs = x * pair_lanes(step, p, low)
            weight = jnp.concatenate(
                [scores * decay_of(cum, cum_t, h, bias, cross) for h in (2 * p, 2 * p + 1)], 1
            )
            split = jnp.concatenate([jnp.where(low, xs, 0.0), jnp.where(low, 0.0, xs)], 0)
            y = mm(weight.astype(BF), split.astype(BF))
            out_ref[at, lanes] = y + pair_lanes(skip, p, low[0:1, :]) * x
        return carry

    lax.fori_loop(0, ends_ref.shape[0], body, 0)


def scan_back_kernel(proj_ref, dscan_ref, ends_ref, cw_ref, head_ref, pc_ref, small_ref):
    rows = LANES
    width = dscan_ref.shape[1]
    pairs = width // LANES
    own = 2 * pairs
    convw = width + 2 * LANES
    dtb, rate, skip = head_ref[0:1, :], head_ref[1:2, :], head_ref[2:3, :]
    neg_rate = -jnp.exp(rate)
    src, dst = iota((rows, rows), 0), iota((rows, rows), 1)
    cross = ((src < SCAN_ROWS) & (dst >= SCAN_ROWS)).astype(F32)
    before = (src < dst).astype(F32)
    reach = (src >= dst).astype(BF)
    lane = iota((rows, LANES), 1)
    low = lane < LANES // 2
    by_head = (iota((width, LANES), 0) // (width // own) == iota((width, LANES), 1)).astype(F32)
    small_ref[...] = jnp.zeros(small_ref.shape, F32)

    def body(b, dskip):
        at = pl.ds(pl.multiple_of(b * rows, rows), rows)
        ends = ends_ref[pl.ds(b, 1), :].astype(jnp.int32)
        seg_col = segment_of(iota((rows, 1), 0), ends)
        seg_row = segment_of(iota((1, rows), 1), ends)
        bias = jnp.where((seg_col == seg_row) & (src <= dst), 0.0, NEG)
        masks = same_masks(ends, rows, 4)
        xbc = proj_ref[at, 0:convw]
        cw = cw_ref[...]
        conv = conv_sum_of(xbc, cw, cw[4:5, :], masks)
        sig = sigmoid(conv)
        act = conv * sig
        key = act[:, width : width + LANES].astype(BF)
        read = act[:, width + LANES : convw].astype(BF)
        scores = mm_t(key, read)
        scores = jnp.concatenate([scores, scores], 1)
        raw = proj_ref[at, convw : convw + LANES]
        step, log_decay, cum = steps_of(raw, dtb, neg_rate, rows)
        cum_t = cum.T
        dscores = jnp.zeros((rows, 2 * rows), F32)
        dlogs, dxs, prods, dsk = [], [], [], []
        for p in range(pairs):
            lanes = slice(p * LANES, (p + 1) * LANES)
            x = act[:, lanes]
            s = pair_lanes(step, p, low)
            decays = []
            for h in (2 * p, 2 * p + 1):
                last = cum[SCAN_ROWS - 1 : SCAN_ROWS, h : h + 1]
                dist = cum_t[h : h + 1, :] - cum[:, h : h + 1]
                decays.append(jnp.exp(dist + (cross * last + bias)))
            decay = jnp.concatenate(decays, 1)
            weight = scores * decay
            dy = dscan_ref[at, lanes]
            split = jnp.concatenate([jnp.where(low, dy, 0.0), jnp.where(low, 0.0, dy)], 0).astype(BF)
            dweight = mm_t((x * s).astype(BF), split)
            dx_s = mm(weight.astype(BF), split)
            dscores = dscores + dweight * decay
            t = (dweight * weight).astype(BF)
            span = mm(jnp.concatenate([t[:, 0:rows], t[:, rows:]], 0), reach)
            dlogs.append(jnp.sum(span[0:rows, :] * before, axis=0, keepdims=True))
            dlogs.append(jnp.sum(span[rows:, :] * before, axis=0, keepdims=True))
            prods.append(dx_s * x)
            dsk.append(jnp.sum(dy * x, axis=0, keepdims=True))
            dxs.append(dx_s * s + pair_lanes(skip, p, low[0:1, :]) * dy)
        dlog = jnp.concatenate(dlogs + [jnp.zeros((rows - own, rows), F32)], 0).T
        dstep = mm_high(jnp.concatenate(prods, 1), by_head) + dlog * neg_rate
        ddt = jnp.where(lane < own, dstep * sigmoid(raw + dtb), 0.0)
        dsc = (dscores[:, 0:rows] + dscores[:, rows:]).astype(BF)
        dkey = mm(dsc, read)
        dread = mm_l(dsc, key)
        dconv = jnp.concatenate(dxs + [dkey, dread], 1) * (sig * (1.0 + conv * (1.0 - sig)))
        dxbc = cw[0:1, :] * dconv
        small_ref[0:1, 0:convw] += jnp.sum(dconv * xbc, axis=0, keepdims=True)
        for k in range(1, 4):
            masked = dconv * masks[k - 1]
            dxbc = dxbc + cw[k : k + 1, :] * pltpu.roll(masked, rows - k, 0)
            small_ref[k : k + 1, 0:convw] += jnp.sum(
                masked * pltpu.roll(xbc, k, 0), axis=0, keepdims=True
            )
        small_ref[4:5, 0:convw] += jnp.sum(dconv, axis=0, keepdims=True)
        small_ref[5:6, width : width + LANES] += jnp.sum(ddt, axis=0, keepdims=True)
        small_ref[5:6, width + LANES : width + 2 * LANES] += jnp.sum(
            dlog * log_decay, axis=0, keepdims=True
        )
        pc_ref[at, 0:convw] = dxbc.astype(BF)
        pc_ref[at, convw : convw + LANES] = ddt.astype(BF)
        return dskip + jnp.concatenate(dsk, 1)

    dskip = lax.fori_loop(0, ends_ref.shape[0], body, jnp.zeros((1, width), F32))
    small_ref[5:6, width + 2 * LANES : width + 3 * LANES] = mm_high(dskip, by_head)


def weave(out_ref, at, parts, size):
    for k in range(8):
        for half in range(QUAD // 2):
            pair = [p[:, k * size : (k + 1) * size] for p in parts[2 * half : 2 * half + 2]]
            lo = at + (k * QUAD + 2 * half) * size
            out_ref[:, lo : lo + 2 * size] = jnp.concatenate(pair, 1)


def pick_heads(parts, heads):
    total = None
    for q in range(QUAD):
        sel = (iota((LANES, heads), 1) == iota((LANES, heads), 0) * QUAD + q).astype(F32)
        got = mm_high(parts[q], sel)
        total = got if total is None else total + got
    return total


def prep_kernel(me_ref, len_ref, w_hbm, tok_hbm, cot_hbm, wout_hbm, act_ref, wout_ref, *rest):
    outs, scr, w_ref, tok_ref, cot_ref, sems = rest[0:4], *rest[4:]
    copies = [
        pltpu.make_async_copy(src, dst, sems.at[n])
        for n, (src, dst) in enumerate(
            ((w_hbm, w_ref), (tok_hbm, tok_ref), (cot_hbm, cot_ref), (wout_hbm, wout_ref))
        )
    ]
    for c in copies:
        c.start()
    rows, model = tok_ref.shape
    t = me_ref[0] & (QUAD - 1)
    heads = 32
    own = heads // QUAD
    copies[0].wait()
    w = w_ref[...].astype(F32)
    inner = (w.shape[1] - heads - outs[0].shape[1] + LANES) * QUAD // (2 * (QUAD - 1))
    size = inner // heads
    conv_end = w.shape[1] - heads
    shared = w[:, 2 * inner : conv_end]
    dts = w[:, conv_end:].astype(BF)
    for q in range(QUAD):
        zs, xs = [], []
        for k in range(own):
            at = (k * QUAD + q) * size
            zs.append(w[:, at : at + size])
            xs.append(w[:, inner + at : inner + at + size])
        pick = (iota((heads, LANES), 0) == iota((heads, LANES), 1) * QUAD + q) & (
            iota((heads, LANES), 1) < own
        )
        scr[q] = jnp.concatenate(zs + xs + [shared, mm(dts, pick.astype(BF))], 1).astype(BF)
    for r in range(QUAD):
        outs[r][...] = scr[t ^ r]
    lane = iota((16, model), 1)
    end = jnp.int32(0)
    tail = jnp.zeros((16, model), jnp.int32)
    for s in range(4):
        end = end + len_ref[s]
        tail = tail + jnp.where(lane == s, end, 0)
    act_ref[rows : rows + 16, :] = tail.astype(F32).astype(BF)
    copies[1].wait()
    act_ref[0:rows, :] = tok_ref[...]
    copies[2].wait()
    live = (iota((rows, 1), 0) < end).astype(F32)
    act_ref[rows + 16 :, :] = (cot_ref[...].astype(F32) * live).astype(BF)
    copies[3].wait()


def params_kernel(me_ref, *refs):
    raws, (cwb_ref, head_ref, gain_ref, pre_ref) = refs[0:7], refs[7:11]
    cw_ref, cb_ref, dt_ref, al_ref, sk_ref, ng_ref, pg_ref = refs[11:18]
    sems = refs[18]
    copies = [
        pltpu.make_async_copy(src, dst, sems.at[n])
        for n, (src, dst) in enumerate(zip(raws, refs[11:18]))
    ]
    for c in copies:
        c.start()
    for c in copies:
        c.wait()
    pre_ref[...] = pg_ref[...]
    t = me_ref[0] & (QUAD - 1)
    heads = dt_ref.shape[1]
    own = heads // QUAD
    inner = ng_ref.shape[1]
    width = inner // QUAD
    size = inner // heads

    def mine(a):
        total = jnp.zeros((a.shape[0], width), F32)
        for q in range(QUAD):
            cut = [a[:, (k * QUAD + q) * size : (k * QUAD + q + 1) * size] for k in range(own)]
            total = jnp.where(t == q, jnp.concatenate(cut, 1), total)
        return total

    taps = cw_ref.shape[0]
    cwb_ref[...] = jnp.zeros(cwb_ref.shape, F32)
    cwb_ref[0:taps, 0:width] = mine(cw_ref[...])
    cwb_ref[0:taps, width:] = cw_ref[:, inner:]
    cwb_ref[taps : taps + 1, 0:width] = mine(cb_ref[...])
    cwb_ref[taps : taps + 1, width:] = cb_ref[:, inner:]
    gain_ref[...] = mine(ng_ref[...])
    pick = (iota((heads, LANES), 0) == iota((heads, LANES), 1) * QUAD + t) & (
        iota((heads, LANES), 1) < own
    )
    rows = jnp.concatenate(
        [dt_ref[...], al_ref[...], sk_ref[...], jnp.zeros((5, heads), F32)], 0
    )
    head_ref[...] = mm_high(rows, pick.astype(F32))


def join_kernel(me_ref, c0, c1, c2, c3, wout_ref, a_ref, b_ref):
    t = me_ref[0] & (QUAD - 1)
    nrow = c0.shape[0]
    width = b_ref.shape[1]
    for r, c in enumerate((c0, c1, c2, c3)):
        at = pl.ds(pl.multiple_of((t ^ r) * nrow, nrow), nrow)
        a_ref[at, :] = c[:, width:]
        b_ref[at, :] = c[:, 0:width]
    size = wout_ref.shape[0]
    b_ref[QUAD * nrow : QUAD * nrow + size, :] = wout_ref[:, 0:width]
    b_ref[QUAD * nrow + size :, :] = wout_ref[:, width:]


def project_kernel(me_ref, *refs):
    chunks = 8
    acts, ws = refs[0:QUAD], refs[QUAD : QUAD + chunks]
    gain_ref, norm_ref, proj_ref, ends_ref = refs[QUAD + chunks :]
    zy = me_ref[0] // QUAD
    rows = ends_ref.shape[1]
    for r in range(QUAD):
        hidden = acts[r][0:rows, :].astype(F32)
        scale = lax.rsqrt(jnp.mean(hidden * hidden, axis=1, keepdims=True) + EPS)
        for k in range(chunks):
            at = pl.ds(pl.multiple_of((zy ^ k) * LANES, LANES), LANES)
            part = acts[r][0:rows, at].astype(F32) * scale * gain_ref[:, at]
            norm_ref[r * rows : (r + 1) * rows, k * LANES : (k + 1) * LANES] = part.astype(BF)
        ends_ref[r : r + 1, :] = acts[r][rows : rows + 16, 0:LANES].astype(F32)[0:1, :]
    w = jnp.concatenate([c[...] for c in ws], axis=0)
    proj_ref[...] = mm(norm_ref[...], w)


def cot_kernel(me_ref, *refs):
    chunks = 8
    ws, acts = refs[0:chunks], refs[chunks : chunks + QUAD]
    wfull_ref, cot_ref, dgn_ref = refs[chunks + QUAD :]
    zy = me_ref[0] // QUAD
    width = ws[0].shape[1]
    size = width // chunks
    rows = cot_ref.shape[0] // QUAD
    for k in range(chunks):
        at = pl.ds(pl.multiple_of((zy ^ k) * size, size), size)
        base = ws[k].shape[0] - 2 * size
        wfull_ref[at, 0:width] = ws[k][base : base + size, :]
        wfull_ref[at, width:] = ws[k][base + size :, :]
    for r in range(QUAD):
        cot_ref[r * rows : (r + 1) * rows, :] = acts[r][rows + 16 :, :]
    dgn_ref[...] = mm_t(cot_ref[...], wfull_ref[...])


def gate_kernel(*refs):
    chunks = 8
    ws = refs[0:chunks]
    norm_ref, scan_ref, dgn_ref, gain_ref, z_ref, stat_ref = refs[chunks:]
    w = jnp.concatenate([c[0:LANES, :] for c in ws], axis=0)
    z = mm(norm_ref[...], w)
    z_ref[...] = z
    gated = scan_ref[...] * (z * sigmoid(z))
    s1 = jnp.sum(gated * gated, axis=1, keepdims=True)
    s2 = jnp.sum(gain_ref[...] * dgn_ref[...] * gated, axis=1, keepdims=True)
    lane = iota((z.shape[0], LANES), 1)
    both = jnp.where(lane == 0, s1, 0.0) + jnp.where(lane == 1, s2, 0.0)
    stat_ref[...] = both.T[0:8, :]


def ungate_kernel(inner, me_ref, *refs):
    chunks = 8
    stats, ws = refs[0:QUAD], refs[QUAD : QUAD + chunks]
    z_ref, scan_ref, dgn_ref, gain_ref, norm_ref, cot_ref = refs[QUAD + chunks : QUAD + chunks + 6]
    gn_ref, dscan_ref, dz_ref, ngain_ref, pre_ref = refs[QUAD + chunks + 6 : QUAD + chunks + 11]
    keeps, send67, send3, send1, scr = refs[QUAD + chunks + 11 : QUAD + chunks + 15], *refs[
        QUAD + chunks + 15 :
    ]
    full = keeps[0].shape[0]
    outs = {0: keeps[0], 2: keeps[1], 4: keeps[2], 5: keeps[3], 3: send3, 1: send1}
    outs[6], outs[7] = send67.at[0:full, :], send67.at[full:, :]
    zy = me_ref[0] // QUAD
    rows = stats[0].shape[1] // QUAD
    total = stats[0][...]
    for r in range(1, QUAD):
        total = total + jnp.concatenate(
            [stats[r][:, (b ^ r) * rows : ((b ^ r) + 1) * rows] for b in range(QUAD)], 1
        )
    pad = jnp.concatenate([total, jnp.zeros((LANES - 8, total.shape[1]), F32)], 0).T
    s1, s2 = pad[:, 0:1], pad[:, 1:2]
    r = lax.rsqrt(s1 / inner + EPS)
    z = z_ref[...]
    sig = sigmoid(z)
    silu = z * sig
    scan = scan_ref[...]
    gain = gain_ref[...]
    unit = scan * silu * r
    gn = (unit * gain).astype(BF)
    gn_ref[...] = gn
    scr[...] = mm_l(gn, cot_ref[...])
    dgn = dgn_ref[...]
    ngain_ref[...] = jnp.sum(dgn * unit, axis=0, keepdims=True)
    dgated = r * (gain * dgn) - unit * (r * r * s2 / inner)
    dscan_ref[...] = dgated * silu
    dz = (dgated * scan * (sig * (1.0 + z * (1.0 - sig)))).astype(BF)
    dz_ref[...] = dz
    width = dz.shape[1]
    size = width // chunks
    lane = iota((LANES, LANES), 1)
    pre = jnp.zeros((LANES, LANES), F32)
    for k in range(chunks):
        grad = mm_l(norm_ref[:, k * LANES : (k + 1) * LANES], dz)
        dot = jnp.sum(grad * ws[k][0:LANES, :].astype(F32), axis=1, keepdims=True)
        pre = pre + jnp.where(lane == k, dot, 0.0)
        out = outs[k]
        out[0:LANES, :] = grad.astype(out.dtype)
        at = pl.ds(pl.multiple_of((zy ^ k) * size, size), size)
        out[LANES : LANES + size, :] = scr[at, 0:width].astype(out.dtype)
        out[LANES + size : LANES + 2 * size, :] = scr[at, width:].astype(out.dtype)
    pre_ref[...] = pre


def split_small(out_ref, base, small):
    high = small.astype(BF)
    low = (small - high.astype(F32)).astype(BF)
    out_ref[base : base + 2 * SMALL, :] = jnp.concatenate(
        [high.astype(F32), low.astype(F32)], 0
    ).astype(BF)


def joined_small(ref, base):
    both = ref[base : base + 2 * SMALL, :].astype(F32)
    return both[0:SMALL, :] + both[SMALL:, :]


def ingrad_kernel(me_ref, norm_ref, pc_ref, small_ref, ngain_ref, preb_ref, gain_ref, *refs):
    chunks = 8
    ws = refs[0:chunks]
    keeps, send67, send3, send1, mine_ref, scr = refs[chunks : chunks + 4], *refs[chunks + 4 :]
    outs = {0: keeps[0], 2: keeps[1], 4: keeps[2], 5: keeps[3], 3: send3, 1: send1}
    outs[6], outs[7] = send67.at[0:LANES, :], send67.at[LANES:, :]
    zy = me_ref[0] // QUAD
    lane = iota((LANES, LANES), 1)
    pre = preb_ref[...]
    for k in range(chunks):
        grad = mm_l(norm_ref[:, k * LANES : (k + 1) * LANES], pc_ref[...])
        dot = jnp.sum(grad * ws[k][...].astype(F32), axis=1, keepdims=True)
        pre = pre + jnp.where(lane == k, dot, 0.0)
        outs[k][0:LANES, :] = grad.astype(outs[k].dtype)
    pre = pre.T
    for k in range(chunks):
        scr[pl.ds(zy ^ k, 1), :] = pre[k : k + 1, :]
    wide = mine_ref.shape[1]
    per = wide // LANES
    gain = gain_ref[...]
    placed = jnp.concatenate([scr[k : k + 1, :] for k in range(chunks)], 1) / gain
    width = ngain_ref.shape[1]
    mine_ref[...] = small_ref[...]
    mine_ref[5:6, 0:width] = ngain_ref[...]
    mine_ref[6:7, :] = placed[:, 0:wide]
    mine_ref[7:8, 0 : (chunks - per) * LANES] = placed[:, wide:]
    split_small(send3, LANES, mine_ref[...])


def add_near_kernel(keep_ref, got_ref, small_ref, out_ref, sum_ref):
    out_ref[0:LANES, :] = (keep_ref[...] + got_ref[0:LANES, :].astype(F32)).astype(BF)
    total = small_ref[...] + joined_small(got_ref, LANES)
    sum_ref[...] = total
    split_small(out_ref, LANES, total)


def add_two_kernel(keep_ref, got_ref, out_ref):
    out_ref[...] = (keep_ref[...] + got_ref[...].astype(F32)).astype(BF)


def add_side_kernel(keep_ref, got_ref, out_ref):
    full = keep_ref.shape[0]
    out_ref[...] = (keep_ref[...] + got_ref[full:, :].astype(F32)).astype(BF)


def add_far_kernel(keep_ref, got_ref, side_ref, out_ref):
    full = keep_ref.shape[0]
    out_ref[...] = (
        keep_ref[...] + got_ref[0:full, :].astype(F32) + side_ref[...].astype(F32)
    ).astype(BF)


def add_last_kernel(keep_ref, got_ref, side_ref, small_ref, near_ref, out_ref, sum_ref):
    out_ref[0:LANES, :] = (
        keep_ref[...] + got_ref[0:LANES, :].astype(F32) + side_ref[...].astype(F32)
    ).astype(BF)
    total = small_ref[...] + joined_small(near_ref, LANES)
    sum_ref[...] = total
    split_small(out_ref, LANES, total)


def tail_kernel(me_ref, *refs):
    chunks = 8
    w1, w2 = refs[0:chunks], refs[chunks : 2 * chunks]
    pc_ref, dz_ref, gn_ref, wfull_ref, keep_ref, send_ref = refs[2 * chunks :]
    zy = me_ref[0] // QUAD
    rows = keep_ref.shape[0] // 2
    model = wfull_ref.shape[1]

    def put(part, at):
        keep_ref[0:rows, at] = part[0:rows, :]
        send_ref[0:rows, at] = part[rows : 2 * rows, :].astype(BF)
        keep_ref[rows:, at] = part[2 * rows : 3 * rows, :]
        send_ref[rows:, at] = part[3 * rows :, :].astype(BF)

    put(mm(gn_ref[...], wfull_ref[...]), pl.ds(0, model))
    for k in range(chunks):
        part = mm_t(pc_ref[...], w1[k][...]) + mm_t(dz_ref[...], w2[k][0:LANES, :])
        put(part, pl.ds(pl.multiple_of(model + (zy ^ k) * LANES, LANES), LANES))


def pair_kernel(keep_ref, got_ref, mine_ref, send_ref):
    rows = mine_ref.shape[0]
    total = keep_ref[...] + got_ref[...].astype(F32)
    mine_ref[...] = total[0:rows, :]
    send_ref[...] = total[rows:, :].astype(BF)


def rows_kernel(act_ref, gain_ref, a_ref, b_ref, mixed_ref, grad_ref):
    rows, model = mixed_ref.shape
    hidden = act_ref[0:rows, :].astype(F32)
    end = act_ref[rows : rows + 16, 0:LANES].astype(F32)[0:1, 3:4]
    live = (iota((rows, 1), 0).astype(F32) < end).astype(F32)
    total = a_ref[...] + b_ref[...].astype(F32)
    mixed_ref[...] = (live * (hidden + total[:, 0:model])).astype(BF)
    scale = lax.rsqrt(jnp.mean(hidden * hidden, axis=1, keepdims=True) + EPS)
    dn = total[:, model:] * gain_ref[...]
    inner = jnp.mean(dn * hidden, axis=1, keepdims=True)
    back = scale * dn - hidden * (scale * scale * scale * inner)
    grad_ref[...] = act_ref[rows + 16 :, :].astype(F32) + back


def total_kernel(me_ref, *refs):
    a, b, small_ref = refs[0:4], refs[4:8], refs[8]
    wout_ref, mine_ref, msmall_ref, s1, s2, s3, scr = refs[9:]
    t = me_ref[0] & (QUAD - 1)
    nrow = mine_ref.shape[0]
    chunk = QUAD * nrow
    ta = a[0][...]
    for got in a[1:]:
        ta = ta + got[0:chunk, :].astype(F32)
    small = small_ref[...] + joined_small(a[3], chunk)
    tb = b[0][...].astype(F32)
    for got in b[1:]:
        tb = tb + got[...].astype(F32)
    size = wout_ref.shape[0]
    width = tb.shape[1]
    wout_ref[:, 0:width] = tb[chunk : chunk + size, :]
    wout_ref[:, width:] = tb[chunk + size :, :]
    scr[:, 0:width] = tb[0:chunk, :]
    scr[:, width:] = ta
    msmall_ref[...] = small
    for r, out in enumerate((mine_ref, s1, s2, s3)):
        at = pl.ds(pl.multiple_of((t ^ r) * nrow, nrow), nrow)
        out[0:nrow, :] = scr[at, :].astype(out.dtype)
    wide = small.shape[1]
    for out in (s1, s2, s3):
        split_small(out.at[:, 0:wide], nrow, small)


def finish_kernel(me_ref, mine_ref, msmall_ref, *refs):
    got = refs[0:3]
    out_ref, cw_ref, cb_ref, dt_ref, al_ref, sk_ref, ng_ref, pg_ref, scr, sscr, row_ref = refs[3:]
    t = me_ref[0] & (QUAD - 1)
    nrow = mine_ref.shape[0]
    wide = msmall_ref.shape[1]
    scr[t] = mine_ref[...]
    sscr[t] = msmall_ref[...]
    for r in range(1, QUAD):
        scr[t ^ r] = got[r - 1][0:nrow, :].astype(F32)
        sscr[t ^ r] = joined_small(got[r - 1].at[:, 0:wide], nrow)
    inner = ng_ref.shape[1]
    width = inner // QUAD
    heads = dt_ref.shape[1]
    size = inner // heads
    conv_end = out_ref.shape[1] - heads
    shared = 2 * width + conv_end - 2 * inner

    def added(ref, rows, lanes):
        return (ref[0][rows, lanes] + ref[1][rows, lanes]) + (ref[2][rows, lanes] + ref[3][rows, lanes])

    every = slice(0, nrow)
    weave(out_ref, 0, [scr[q][:, 0:width] for q in range(QUAD)], size)
    weave(out_ref, inner, [scr[q][:, width : 2 * width] for q in range(QUAD)], size)
    out_ref[:, 2 * inner : conv_end] = added(scr, every, slice(2 * width, shared))
    out_ref[:, conv_end:] = pick_heads(
        [scr[q][:, shared : shared + LANES] for q in range(QUAD)], heads
    )
    conv = shared - width
    weave(cw_ref, 0, [sscr[q][0:4, 0:width] for q in range(QUAD)], size)
    cw_ref[:, inner:] = added(sscr, slice(0, 4), slice(width, conv))
    weave(row_ref, 0, [sscr[q][4:5, 0:width] for q in range(QUAD)], size)
    row_ref[:, inner:] = added(sscr, slice(4, 5), slice(width, conv))
    for n in range(cb_ref.shape[0]):
        cb_ref[n : n + 1, :] = row_ref[:, n * LANES : (n + 1) * LANES]
    weave(ng_ref, 0, [sscr[q][5:6, 0:width] for q in range(QUAD)], size)
    lists = [
        pick_heads([sscr[q][:, at : at + LANES] for q in range(QUAD)], heads)[5:6, :]
        for at in (width, width + LANES, width + 2 * LANES)
    ]
    dt_ref[...], al_ref[...], sk_ref[...] = lists
    pg_ref[:, 0:wide] = added(sscr, slice(6, 7), slice(0, wide))
    pg_ref[:, wide:] = added(sscr, slice(7, 8), slice(0, pg_ref.shape[1] - wide))


def quad_shards(
    count,
    tokens,
    lengths,
    in_weight,
    out_weight,
    conv_weight,
    conv_bias,
    dt_bias,
    a_log,
    skip_gain,
    norm_gain,
    pre_gain,
    cotangent,
):
    chunks = count // QUAD
    rows, model = tokens.shape
    inner = norm_gain.shape[0]
    heads = dt_bias.shape[0]
    width = inner // QUAD
    size = inner // heads
    nrow, proj_width = in_weight.shape
    convw = width + conv_bias.shape[0] - inner
    wide = convw + LANES
    both = width + wide
    total_rows = QUAD * rows
    chunk = QUAD * nrow
    chunk_b = chunk + 2 * size

    def swap(a, mask):
        return lax.ppermute(a, "dp", [(i, i ^ mask) for i in range(count)])

    def after(a, *others):
        return lax.optimization_barrier((a,) + others)[0]

    def gather(mine, later=()):
        z = after(mine, *later) if later else mine
        got = [mine, None, None, None, swap(z, 4 * QUAD), None, None, None]
        got[2] = swap(z, 2 * QUAD)
        got[1] = swap(mine, QUAD)
        got[5] = swap(got[4], QUAD)
        got[6] = swap(got[4], 2 * QUAD)
        got[3] = swap(got[2], QUAD)
        got[7] = swap(got[5], 2 * QUAD)
        return got

    me = lax.axis_index("dp").astype(jnp.int32).reshape(1)

    prepped = call(
        prep_kernel,
        [((2 * rows + 16, model), BF), (out_weight.shape, BF)] + [((nrow, both), BF)] * QUAD,
        [me, lengths, in_weight, tokens, cotangent, out_weight],
        [
            pltpu.VMEM((QUAD, nrow, both), BF),
            pltpu.VMEM(in_weight.shape, BF),
            pltpu.VMEM(tokens.shape, BF),
            pltpu.VMEM(tokens.shape, BF),
            pltpu.SemaphoreType.DMA((4,)),
        ],
        name="prep",
        raw=(2, 3, 4, 5),
        limit=RAW_BYTES,
    )
    act, own_out, cut = prepped[0], prepped[1], prepped[2:]
    got = [swap(cut[r], r) for r in range(1, QUAD)]
    shapes = [(4, conv_bias.shape[0])] + [(1, n) for n in (conv_bias.shape[0], heads, heads, heads, inner, model)]
    cwb, by_head, gain, pre = call(
        params_kernel,
        [((8, convw), F32), ((8, LANES), F32), ((1, width), F32), ((1, model), F32)],
        [me, conv_weight]
        + [a[None, :] for a in (conv_bias, dt_bias, a_log, skip_gain, norm_gain, pre_gain)],
        [pltpu.VMEM(a, F32) for a in shapes] + [pltpu.SemaphoreType.DMA((7,))],
        name="params",
        raw=tuple(range(1, 8)),
        limit=RAW_BYTES,
    )
    got[1] = after(got[1], cwb, by_head, gain, pre)
    own_a, own_b = call(
        join_kernel,
        [((chunk, wide), BF), ((chunk_b, width), BF)],
        [me, cut[0]] + got + [own_out],
        name="join",
    )
    w1 = gather(own_a)
    w2 = gather(own_b, (w1[2],))
    across = swap(act, 2)
    acts = [act, swap(act, 1), across, swap(across, 1)]
    normed, proj, ends = call(
        project_kernel,
        [((total_rows, model), BF), ((total_rows, wide), F32), ((QUAD, rows), F32)],
        [me] + acts + w1 + [pre],
        name="project",
    )
    (scan_out,) = call(
        scan_kernel,
        [((total_rows, width), F32)],
        [proj, ends, cwb, by_head],
        name="scan",
    )
    w_full, cot_all, dgn = call(
        cot_kernel,
        [((width, model), BF), ((total_rows, model), BF), ((total_rows, width), F32)],
        [me] + w2 + acts,
        name="normcot",
    )
    z, stat = call(
        gate_kernel,
        [((total_rows, width), F32), ((8, total_rows), F32)],
        w2 + [normed, scan_out, dgn, gain],
        name="gate",
    )
    stats = [stat] + [swap(stat, r) for r in range(1, QUAD)]
    ungated = call(
        functools.partial(ungate_kernel, float(inner)),
        [
            ((total_rows, width), BF),
            ((total_rows, width), F32),
            ((total_rows, width), BF),
            ((1, width), F32),
            ((LANES, LANES), F32),
        ]
        + [((chunk_b, width), F32)] * 4
        + [((2 * chunk_b, width), BF)]
        + [((chunk_b, width), BF)] * 2,
        [me] + stats + w2 + [z, scan_out, dgn, gain, normed, cot_all],
        [pltpu.VMEM((width, model), F32)],
        name="ungate",
    )
    gn, dscan, dz, ngain_part, pre_b = ungated[0:5]
    keep_b, (send67, send3, send1) = ungated[5:9], ungated[9:]
    got67_b, got3_b, got1_b = swap(send67, 2 * QUAD), swap(send3, QUAD), swap(send1, QUAD)
    pc1, small = call(
        scan_back_kernel,
        [((total_rows, wide), BF), ((SMALL, wide), F32)],
        [proj, dscan, ends, cwb, by_head],
        name="scanback",
    )
    ingrads = call(
        ingrad_kernel,
        [((chunk, wide), F32)] * 4
        + [((2 * chunk, wide), BF), ((chunk + 2 * SMALL, wide), BF), ((chunk, wide), BF)]
        + [((SMALL, wide), F32)],
        [me, normed, pc1, small, ngain_part, pre_b, pre] + w1,
        [pltpu.VMEM((chunks, LANES), F32)],
        name="ingrad",
    )
    keep_a, (send67, send3, send1, small) = list(ingrads[0:4]), ingrads[4:8]
    got67_a, got3_a, got1_a = swap(send67, 2 * QUAD), swap(send3, QUAD), swap(send1, QUAD)
    got67_b = after(got67_b, small)
    got3_b = after(got3_b, small)

    (side,) = call(add_side_kernel, [((chunk_b, width), BF)], [keep_b[3], got67_b], name="side")
    got5_b = swap(side, QUAD)
    (near,) = call(add_two_kernel, [((chunk_b, width), BF)], [keep_b[1], got3_b], name="near")
    got2_b = swap(near, 2 * QUAD)
    (far,) = call(
        add_far_kernel, [((chunk_b, width), BF)], [keep_b[2], got67_b, got5_b], name="far"
    )
    got4_b = swap(far, 4 * QUAD)

    (side,) = call(add_side_kernel, [((chunk, wide), BF)], [keep_a[3], got67_a], name="side")
    got5_a = swap(side, QUAD)
    riding = [((chunk + 2 * SMALL, wide), BF), ((SMALL, wide), F32)]
    near, small1 = call(add_near_kernel, riding, [keep_a[1], got3_a, small], name="near")
    got2_a = swap(near, 2 * QUAD)
    far, small2 = call(
        add_last_kernel, riding, [keep_a[2], got67_a, got5_a, small1, got2_a], name="far"
    )
    got4_a = swap(far, 4 * QUAD)

    pc1, dz = lax.optimization_barrier((pc1, dz, small))[0:2]
    keep, send = call(
        tail_kernel,
        [((2 * rows, 2 * model), F32), ((2 * rows, 2 * model), BF)],
        [me] + w1 + w2 + [pc1, dz, gn, w_full],
        name="tail",
    )
    mine, send = call(
        pair_kernel,
        [((rows, 2 * model), F32), ((rows, 2 * model), BF)],
        [keep, swap(send, 1)],
        name="pair",
    )
    crossed = swap(send, 2)
    mixed, tokens_grad = call(
        rows_kernel,
        [((rows, model), BF), ((rows, model), F32)],
        [act, pre, mine, crossed],
        name="rows",
    )

    out_shard, own, own_small, *cuts = call(
        total_kernel,
        [((size, model), F32), ((nrow, both), F32), ((SMALL, wide), F32)]
        + [((nrow + 2 * SMALL, both), BF)] * 3,
        [me, keep_a[0], got1_a, got2_a, got4_a, keep_b[0], got1_b, got2_b, got4_b, small2],
        [pltpu.VMEM((chunk, both), F32)],
        name="total",
    )
    own, mixed, tokens_grad = lax.optimization_barrier((own, mixed, tokens_grad))
    done = call(
        finish_kernel,
        [
            ((nrow, proj_width), F32),
            (conv_weight.shape, F32),
            ((conv_bias.shape[0] // LANES, LANES), F32),
            ((1, heads), F32),
            ((1, heads), F32),
            ((1, heads), F32),
            ((1, inner), F32),
            ((1, model), F32),
        ],
        [me, own, own_small] + [swap(a, r + 1) for r, a in enumerate(cuts)],
        [pltpu.VMEM((QUAD, nrow, both), F32), pltpu.VMEM((QUAD, SMALL, wide), F32), pltpu.VMEM((1, conv_bias.shape[0]), F32)],
        name="finish",
    )
    return (mixed, tokens_grad, done[0], out_shard, done[1]) + tuple(
        a.reshape(-1) for a in done[2:]
    )


def prenorm(hidden_in, gain_row):
    return (
        hidden_in
        * lax.rsqrt(jnp.mean(hidden_in * hidden_in, axis=-1, keepdims=True) + EPS)
        * gain_row
    )


def shifted(array, offset, filler):
    padding = jnp.full((offset,) + array.shape[1:], filler, array.dtype)
    return jnp.concatenate([padding, array[:-offset]], axis=0)


def segments(seq_lengths, row_count):
    seq_ends = jnp.cumsum(seq_lengths, dtype=jnp.int32)
    position = jnp.arange(row_count, dtype=jnp.int32)
    segment = jnp.sum(
        (position[:, None] >= seq_ends[None, :]).astype(jnp.int32), axis=1, dtype=jnp.int32
    )
    live_rows = (position < seq_ends[-1]).astype(jnp.float32)
    return (segment, live_rows)


def block_step(carry, block_item):
    state_mat, prev_segment = carry
    values, key_rows, read_rows, step_size, log_decay, block_segment = block_item
    cumulative = jnp.cumsum(log_decay, axis=0)
    position = jnp.arange(block_segment.shape[0], dtype=jnp.int32)
    causal = (block_segment[:, None] == block_segment[None, :]) & (
        position[:, None] >= position[None, :]
    )
    distance = cumulative[:, None, :] - cumulative[None, :, :]
    decay_mask = jnp.where(
        causal[:, :, None], jnp.exp(jnp.where(causal[:, :, None], distance, 0.0)), 0.0
    )
    scores = jnp.dot(read_rows, key_rows.T, precision=HIGH)
    weighting = scores[:, :, None] * decay_mask * step_size[None, :, :]
    inside = jnp.einsum("ijh,jhp->ihp", weighting, values, precision=HIGH)
    entering = (block_segment == prev_segment).astype(jnp.float32)
    carried = jnp.einsum("in,hnp->ihp", read_rows, state_mat, precision=HIGH)
    carried = carried * (jnp.exp(cumulative) * entering[:, None])[:, :, None]
    last_same = (block_segment == block_segment[-1]).astype(jnp.float32)
    tail_weight = jnp.exp(cumulative[-1][None, :] - cumulative) * last_same[:, None] * step_size
    new_state = state_mat * (jnp.exp(cumulative[-1]) * entering[-1])[:, None, None]
    new_state = new_state + jnp.einsum(
        "jn,jh,jhp->hnp", key_rows, tail_weight, values, precision=HIGH
    )
    return ((new_state, block_segment[-1]), inside + carried)


def mixer_core(projected, conv_weight, conv_bias, dt_bias, a_log, skip_gain, norm_gain, segment):
    inner_width = norm_gain.shape[0]
    head_count = dt_bias.shape[0]
    conv_width = conv_bias.shape[0]
    state_width = (conv_width - inner_width) // 2
    head_size = inner_width // head_count
    row_count = projected.shape[0]
    gate_in = projected[:, :inner_width]
    conv_src = projected[:, inner_width : inner_width + conv_width]
    dt_raw = projected[:, inner_width + conv_width :]
    conv_sum = conv_bias[None, :] + conv_weight[0][None, :] * conv_src
    for offset in range(1, conv_weight.shape[0]):
        same_rows = (segment == shifted(segment, offset, -1)).astype(jnp.float32)
        conv_sum = (
            conv_sum
            + conv_weight[offset][None, :] * shifted(conv_src, offset, 0.0) * same_rows[:, None]
        )
    activated = jax.nn.silu(conv_sum)
    values = activated[:, :inner_width].reshape(row_count, head_count, head_size)
    key_rows = activated[:, inner_width : inner_width + state_width]
    read_rows = activated[:, inner_width + state_width :]
    step_size = jax.nn.softplus(dt_raw + dt_bias[None, :])
    log_decay = -step_size * jnp.exp(a_log)[None, :]
    blocks = row_count // SCAN_ROWS
    items = (
        values.reshape(blocks, SCAN_ROWS, head_count, head_size),
        key_rows.reshape(blocks, SCAN_ROWS, state_width),
        read_rows.reshape(blocks, SCAN_ROWS, state_width),
        step_size.reshape(blocks, SCAN_ROWS, head_count),
        log_decay.reshape(blocks, SCAN_ROWS, head_count),
        segment.reshape(blocks, SCAN_ROWS),
    )
    start = (jnp.zeros((head_count, state_width, head_size), jnp.float32), jnp.array(-1, jnp.int32))
    _, scanned = lax.scan(jax.checkpoint(block_step), start, items)
    scan_out = scanned.reshape(row_count, inner_width) + (
        skip_gain[None, :, None] * values
    ).reshape(row_count, inner_width)
    gated_out = scan_out * jax.nn.silu(gate_in)
    return (
        gated_out
        * lax.rsqrt(jnp.mean(gated_out * gated_out, axis=-1, keepdims=True) + EPS)
        * norm_gain[None, :]
    )


def shards(
    tokens,
    lengths,
    in_weight,
    out_weight,
    conv_weight,
    conv_bias,
    dt_bias,
    a_log,
    skip_gain,
    norm_gain,
    pre_gain,
    cotangent,
):
    w_in, w_out = (
        lax.all_gather(in_weight, "dp", axis=0, tiled=True),
        lax.all_gather(out_weight, "dp", axis=0, tiled=True),
    )
    segment, live_rows = segments(lengths, tokens.shape[0])
    hidden_in = tokens.astype(jnp.float32)
    normed, norm_back = jax.vjp(prenorm, hidden_in, pre_gain)
    normed_low = normed.astype(jnp.bfloat16)
    projected = jnp.dot(normed_low, w_in, preferred_element_type=jnp.float32)
    proj_width = projected.shape[1]

    def mixer_local(proj_rows, conv_w, conv_b, bias_dt, decay_log, skip_w, gain_w):
        return mixer_core(proj_rows, conv_w, conv_b, bias_dt, decay_log, skip_w, gain_w, segment)

    gated_norm, mixer_back = jax.vjp(
        mixer_local, projected, conv_weight, conv_bias, dt_bias, a_log, skip_gain, norm_gain
    )
    gated_low = gated_norm.astype(jnp.bfloat16)
    branch = jnp.dot(gated_low, w_out, preferred_element_type=jnp.float32)
    mixed = (live_rows[:, None] * (hidden_in + branch)).astype(jnp.bfloat16)
    w_in, w_out = (
        lax.all_gather(in_weight, "dp", axis=0, tiled=True),
        lax.all_gather(out_weight, "dp", axis=0, tiled=True),
    )
    out_cot = cotangent.astype(jnp.float32) * live_rows[:, None]
    out_cot_low = out_cot.astype(jnp.bfloat16)
    norm_cot = lax.dot_general(
        out_cot_low, w_out, (((1,), (1,)), ((), ())), preferred_element_type=jnp.float32
    )
    proj_cot, conv_w_grad, conv_b_grad, bias_dt_grad, decay_grad, skip_grad, gain_grad = mixer_back(
        norm_cot
    )
    proj_cot_low = proj_cot.astype(jnp.bfloat16)
    normed_cot = lax.dot_general(
        proj_cot_low, w_in, (((1,), (1,)), ((), ())), preferred_element_type=jnp.float32
    )
    hidden_cot, pre_grad = norm_back(normed_cot)
    tokens_grad = out_cot + hidden_cot
    out_grad = lax.dot_general(
        gated_low, out_cot_low, (((0,), (0,)), ((), ())), preferred_element_type=jnp.float32
    )
    in_grad = lax.dot_general(
        normed_low, proj_cot_low, (((0,), (0,)), ((), ())), preferred_element_type=jnp.float32
    )
    in_wide = in_grad.reshape(2 * in_grad.shape[0], proj_width // 2)
    in_folded, out_shard = (
        lax.psum_scatter(in_wide, "dp", scatter_dimension=0, tiled=True),
        lax.psum_scatter(out_grad, "dp", scatter_dimension=0, tiled=True),
    )
    in_shard = in_folded.reshape(in_weight.shape[0], proj_width)
    summed = lax.psum(
        (conv_w_grad, conv_b_grad, bias_dt_grad, decay_grad, skip_grad, gain_grad, pre_grad), "dp"
    )
    return (
        mixed,
        tokens_grad,
        in_shard,
        out_shard,
        summed[0],
        summed[1],
        summed[2],
        summed[3],
        summed[4],
        summed[5],
        summed[6],
    )


def solution(mesh):
    count = mesh.shape["dp"]
    body = functools.partial(quad_shards, count) if count == 32 else shards
    return jax.shard_map(
        body,
        mesh=mesh,
        in_specs=(
            P("dp", None),
            P("dp"),
            P("dp", None),
            P("dp", None),
            P(),
            P(),
            P(),
            P(),
            P(),
            P(),
            P(),
            P("dp", None),
        ),
        out_specs=(
            P("dp", None),
            P("dp", None),
            P("dp", None),
            P("dp", None),
            P(),
            P(),
            P(),
            P(),
            P(),
            P(),
            P(),
        ),
        check_vma=False,
    )
```

```python
import functools

import jax
import jax.numpy as jnp
from jax import lax
from jax.experimental import pallas as pl
from jax.experimental.pallas import tpu as pltpu
from jax.sharding import PartitionSpec as P

SCAN_ROWS = 64


EPS = 1e-05
HIGH = lax.Precision.HIGHEST
BF = jnp.bfloat16
F32 = jnp.float32
NEG = -1e30
LANES = 128
PROJECT_COST = 4e9
SCAN_COST = 1.6e10
QUAD = 4
SMALL = 16
VMEM_BYTES = 44 * 1024 * 1024
RAW_BYTES = 60 * 1024 * 1024


def mm(a, b):
    return lax.dot_general(a, b, (((1,), (0,)), ((), ())), preferred_element_type=F32)


def mm_t(a, b):
    return lax.dot_general(a, b, (((1,), (1,)), ((), ())), preferred_element_type=F32)


def mm_l(a, b):
    return lax.dot_general(a, b, (((0,), (0,)), ((), ())), preferred_element_type=F32)


def mm_high(a, b):
    return lax.dot_general(
        a, b, (((1,), (0,)), ((), ())), precision=HIGH, preferred_element_type=F32
    )


def call(kernel, out_shapes, inputs, scratch=(), flops=1e3, name=None, raw=(), limit=VMEM_BYTES):
    in_specs = [
        pl.BlockSpec(
            memory_space=pltpu.HBM
            if n in raw
            else (pltpu.SMEM if a.dtype == jnp.int32 else pltpu.VMEM)
        )
        for n, a in enumerate(inputs)
    ]
    shapes = [jax.ShapeDtypeStruct(s, d) for s, d in out_shapes]
    return pl.pallas_call(
        kernel,
        out_shape=shapes,
        in_specs=in_specs,
        out_specs=[pl.BlockSpec(memory_space=pltpu.VMEM)] * len(shapes),
        scratch_shapes=list(scratch),
        cost_estimate=pl.CostEstimate(flops=int(flops), bytes_accessed=1024, transcendentals=0),
        compiler_params=pltpu.CompilerParams(vmem_limit_bytes=limit),
        name=name,
    )(*inputs)


def iota(shape, axis):
    return lax.broadcasted_iota(jnp.int32, shape, axis)


def sigmoid(v):
    return 1.0 / (1.0 + jnp.exp(-v))


def softplus(v):
    return jnp.maximum(v, 0.0) + jnp.log1p(jnp.exp(-jnp.abs(v)))


def segment_of(position, ends):
    seg = jnp.zeros(position.shape, jnp.int32)
    for s in range(4):
        seg = seg + (position >= ends[:, s : s + 1]).astype(jnp.int32)
    return seg


def same_masks(ends, rows, taps):
    position = iota((rows, 1), 0)
    seg = segment_of(position, ends)
    masks = []
    for k in range(1, taps):
        seg_k = segment_of(position - k, ends)
        masks.append(((seg == seg_k) & (position >= k)).astype(F32))
    return masks


def scan_bias(ends, rows):
    seg_col = segment_of(iota((rows, 1), 0), ends)
    seg_row = segment_of(iota((1, rows), 1), ends)
    causal = (seg_col == seg_row) & (iota((rows, rows), 0) >= iota((rows, rows), 1))
    return jnp.where(causal, 0.0, NEG)


def tri_block(rows):
    i, j = iota((rows, rows), 0), iota((rows, rows), 1)
    return ((i >= j) & (i // SCAN_ROWS == j // SCAN_ROWS)).astype(F32)


def steps_of(dt_raw, dtb, neg_rate, rows):
    step = softplus(dt_raw + dtb)
    log_decay = step * neg_rate
    cum = mm_high(tri_block(rows), log_decay)
    return step, log_decay, cum


def decay_of(cum, cum_t, head, bias, cross):
    dist = cum[:, head : head + 1] - cum_t[head : head + 1, :]
    last = cum[SCAN_ROWS - 1 : SCAN_ROWS, head : head + 1]
    return jnp.exp(dist + cross * last + bias)


def conv_sum_of(xbc, cw, cb, masks):
    total = cb + cw[0:1, :] * xbc
    for k in range(1, len(masks) + 1):
        total = total + cw[k : k + 1, :] * (pltpu.roll(xbc, k, 0) * masks[k - 1])
    return total


def pair_lanes(row, pair, low):
    return jnp.where(low, row[:, 2 * pair : 2 * pair + 1], row[:, 2 * pair + 1 : 2 * pair + 2])


def scan_kernel(me_ref, own_ref, g1, g2, g3, ends_ref, cw_ref, head_ref, out_ref, proj_ref, scr):
    rows = LANES
    width = out_ref.shape[1]
    t = me_ref[0] & (QUAD - 1)
    part = scr.shape[2]
    scr[t] = own_ref[:, width : width + part]
    for r, g in ((1, g1), (2, g2), (3, g3)):
        scr[t ^ r] = unfold(g[...].astype(F32), r)
    proj_ref[:, 0:width] = own_ref[:, 0:width]
    proj_ref[:, width : width + 2 * LANES] = jnp.concatenate([scr[q] for q in range(QUAD)], 1)
    proj_ref[:, width + 2 * LANES :] = jnp.concatenate(
        [own_ref[:, width + part :], jnp.zeros((own_ref.shape[0], LANES - part), F32)], 1
    )
    pairs = width // LANES
    convw = width + 2 * LANES
    dtb, rate, skip = head_ref[0:1, :], head_ref[1:2, :], head_ref[2:3, :]
    neg_rate = -jnp.exp(rate)
    cross = ((iota((rows, rows), 0) >= SCAN_ROWS) & (iota((rows, rows), 1) < SCAN_ROWS)).astype(F32)
    low = iota((rows, LANES), 1) < LANES // 2

    def body(b, carry):
        at = pl.ds(pl.multiple_of(b * rows, rows), rows)
        ends = ends_ref[pl.ds(b, 1), :].astype(jnp.int32)
        bias = scan_bias(ends, rows)
        masks = same_masks(ends, rows, 4)
        xbc = proj_ref[at, 0:convw]
        conv = conv_sum_of(xbc, cw_ref[...], cw_ref[4:5, :], masks)
        act = conv * sigmoid(conv)
        key, read = act[:, width : width + LANES], act[:, width + LANES : convw]
        scores = mm_t(read.astype(BF), key.astype(BF))
        step, _, cum = steps_of(proj_ref[at, convw : convw + LANES], dtb, neg_rate, rows)
        cum_t = cum.T
        for p in range(pairs):
            lanes = slice(p * LANES, (p + 1) * LANES)
            x = act[:, lanes]
            xs = x * pair_lanes(step, p, low)
            weight = jnp.concatenate(
                [scores * decay_of(cum, cum_t, h, bias, cross) for h in (2 * p, 2 * p + 1)], 1
            )
            split = jnp.concatenate([jnp.where(low, xs, 0.0), jnp.where(low, 0.0, xs)], 0)
            y = mm(weight.astype(BF), split.astype(BF))
            out_ref[at, lanes] = y + pair_lanes(skip, p, low[0:1, :]) * x
        return carry

    lax.fori_loop(0, ends_ref.shape[0], body, 0)


def scan_back_kernel(
    me_ref, proj_ref, dscan_ref, ends_ref, cw_ref, head_ref, pc_ref, small_ref, p0, p1, p2, p3, scr
):
    rows = LANES
    width = dscan_ref.shape[1]
    pairs = width // LANES
    own = 2 * pairs
    convw = width + 2 * LANES
    dtb, rate, skip = head_ref[0:1, :], head_ref[1:2, :], head_ref[2:3, :]
    neg_rate = -jnp.exp(rate)
    src, dst = iota((rows, rows), 0), iota((rows, rows), 1)
    cross = ((src < SCAN_ROWS) & (dst >= SCAN_ROWS)).astype(F32)
    before = (src < dst).astype(F32)
    reach = (src >= dst).astype(BF)
    lane = iota((rows, LANES), 1)
    low = lane < LANES // 2
    by_head = (iota((width, LANES), 0) // (width // own) == iota((width, LANES), 1)).astype(F32)
    small_ref[...] = jnp.zeros(small_ref.shape, F32)
    t = me_ref[0] & (QUAD - 1)
    part = scr.shape[2]

    def add_small(k, v):
        total = jnp.sum(v, axis=0, keepdims=True)
        small_ref[k : k + 1, 0:width] += total[:, 0:width]
        small_ref[5 + k : 6 + k, 0 : 2 * LANES] += total[:, width:]

    def body(b, dskip):
        at = pl.ds(pl.multiple_of(b * rows, rows), rows)
        ends = ends_ref[pl.ds(b, 1), :].astype(jnp.int32)
        seg_col = segment_of(iota((rows, 1), 0), ends)
        seg_row = segment_of(iota((1, rows), 1), ends)
        bias = jnp.where((seg_col == seg_row) & (src <= dst), 0.0, NEG)
        masks = same_masks(ends, rows, 4)
        xbc = proj_ref[at, 0:convw]
        cw = cw_ref[...]
        conv = conv_sum_of(xbc, cw, cw[4:5, :], masks)
        sig = sigmoid(conv)
        act = conv * sig
        key = act[:, width : width + LANES].astype(BF)
        read = act[:, width + LANES : convw].astype(BF)
        scores = mm_t(key, read)
        scores = jnp.concatenate([scores, scores], 1)
        raw = proj_ref[at, convw : convw + LANES]
        step, log_decay, cum = steps_of(raw, dtb, neg_rate, rows)
        cum_t = cum.T
        dscores = jnp.zeros((rows, 2 * rows), F32)
        dlogs, dxs, prods, dsk = [], [], [], []
        for p in range(pairs):
            lanes = slice(p * LANES, (p + 1) * LANES)
            x = act[:, lanes]
            s = pair_lanes(step, p, low)
            decays = []
            for h in (2 * p, 2 * p + 1):
                last = cum[SCAN_ROWS - 1 : SCAN_ROWS, h : h + 1]
                dist = cum_t[h : h + 1, :] - cum[:, h : h + 1]
                decays.append(jnp.exp(dist + (cross * last + bias)))
            decay = jnp.concatenate(decays, 1)
            weight = scores * decay
            dy = dscan_ref[at, lanes]
            split = jnp.concatenate([jnp.where(low, dy, 0.0), jnp.where(low, 0.0, dy)], 0).astype(BF)
            dweight = mm_t((x * s).astype(BF), split)
            dx_s = mm(weight.astype(BF), split)
            dscores = dscores + dweight * decay
            t = (dweight * weight).astype(BF)
            span = mm(jnp.concatenate([t[:, 0:rows], t[:, rows:]], 0), reach)
            dlogs.append(jnp.sum(span[0:rows, :] * before, axis=0, keepdims=True))
            dlogs.append(jnp.sum(span[rows:, :] * before, axis=0, keepdims=True))
            prods.append(dx_s * x)
            dsk.append(jnp.sum(dy * x, axis=0, keepdims=True))
            dxs.append(dx_s * s + pair_lanes(skip, p, low[0:1, :]) * dy)
        dlog = jnp.concatenate(dlogs + [jnp.zeros((rows - own, rows), F32)], 0).T
        dstep = mm_high(jnp.concatenate(prods, 1), by_head) + dlog * neg_rate
        ddt = jnp.where(lane < own, dstep * sigmoid(raw + dtb), 0.0)
        dsc = (dscores[:, 0:rows] + dscores[:, rows:]).astype(BF)
        dkey = mm(dsc, read)
        dread = mm_l(dsc, key)
        dconv = jnp.concatenate(dxs + [dkey, dread], 1) * (sig * (1.0 + conv * (1.0 - sig)))
        dxbc = cw[0:1, :] * dconv
        add_small(0, dconv * xbc)
        for k in range(1, 4):
            masked = dconv * masks[k - 1]
            dxbc = dxbc + cw[k : k + 1, :] * pltpu.roll(masked, rows - k, 0)
            add_small(k, masked * pltpu.roll(xbc, k, 0))
        add_small(4, dconv)
        small_ref[11:12, 0:LANES] += jnp.sum(ddt, axis=0, keepdims=True)
        small_ref[11:12, LANES : 2 * LANES] += jnp.sum(dlog * log_decay, axis=0, keepdims=True)
        pc_ref[at, 0:width] = dxbc[:, 0:width].astype(BF)
        for q in range(QUAD):
            scr[q, at, :] = dxbc[:, width + q * part : width + (q + 1) * part]
        pc_ref[at, width + part :] = ddt[:, 0:part].astype(BF)
        return dskip + jnp.concatenate(dsk, 1)

    dskip = lax.fori_loop(0, ends_ref.shape[0], body, jnp.zeros((1, width), F32))
    small_ref[11:12, 2 * LANES : 3 * LANES] = mm_high(dskip, by_head)
    half = scr.shape[1] // 2
    for r, out in enumerate((p0, p1, p2, p3)):
        mine = scr[t ^ r]
        out[...] = jnp.concatenate([mine[0:half, :], mine[half:, :]], 1).astype(out.dtype)


def weave(out_ref, at, parts, size):
    for k in range(8):
        for half in range(QUAD // 2):
            pair = [p[:, k * size : (k + 1) * size] for p in parts[2 * half : 2 * half + 2]]
            lo = at + (k * QUAD + 2 * half) * size
            out_ref[:, lo : lo + 2 * size] = jnp.concatenate(pair, 1)


def pick_heads(parts, heads):
    total = None
    for q in range(QUAD):
        deep = (parts[q].shape[1], heads)
        sel = (iota(deep, 1) == iota(deep, 0) * QUAD + q).astype(F32)
        got = mm_high(parts[q], sel)
        total = got if total is None else total + got
    return total


def prep_kernel(me_ref, len_ref, *refs):
    raws = refs[0:10]
    act_ref, cwb_ref, head_ref, gain_ref, pre_ref = refs[10:15]
    outs, scr = refs[15:19], refs[19]
    w_ref, tok_ref, cot_ref = refs[20:23]
    sems = refs[30]
    copies = [
        pltpu.make_async_copy(src, dst, sems.at[n])
        for n, (src, dst) in enumerate(zip(raws, refs[20:30]))
    ]
    for c in copies:
        c.start()
    rows, model = tok_ref.shape
    t = me_ref[0] & (QUAD - 1)
    heads = 32
    own = heads // QUAD
    copies[0].wait()
    w = w_ref[...].astype(F32)
    inner = gain_ref.shape[1] * QUAD
    size = inner // heads
    conv_end = w.shape[1] - heads
    shared = w[:, 2 * inner : conv_end]
    dts = w[:, conv_end:].astype(BF)
    for q in range(QUAD):
        zs, xs = [], []
        for k in range(own):
            at = (k * QUAD + q) * size
            zs.append(w[:, at : at + size])
            xs.append(w[:, inner + at : inner + at + size])
        part = shared.shape[1] // QUAD
        pick = (iota((heads, part), 0) == iota((heads, part), 1) * QUAD + q) & (
            iota((heads, part), 1) < own
        )
        mine = [shared[:, q * part : (q + 1) * part], mm(dts, pick.astype(BF))]
        scr[q] = jnp.concatenate(zs + xs + mine, 1).astype(BF)
    for r in range(QUAD):
        outs[r][...] = scr[t ^ r]
    lane = iota((16, model), 1)
    end = jnp.int32(0)
    tail = jnp.zeros((16, model), jnp.int32)
    for s in range(4):
        end = end + len_ref[s]
        tail = tail + jnp.where(lane == s, end, 0)
    act_ref[rows : rows + 16, :] = tail.astype(F32).astype(BF)
    copies[1].wait()
    act_ref[0:rows, :] = tok_ref[...]
    copies[2].wait()
    live = (iota((rows, 1), 0) < end).astype(F32)
    act_ref[rows + 16 :, :] = (cot_ref[...].astype(F32) * live).astype(BF)
    for c in copies[3:]:
        c.wait()
    share_params(t, refs[23:30], cwb_ref, head_ref, gain_ref, pre_ref)


def share_params(t, given, cwb_ref, head_ref, gain_ref, pre_ref):
    cw_ref, cb_ref, dt_ref, al_ref, sk_ref, ng_ref, pg_ref = given
    pre_ref[...] = pg_ref[...]
    bias = jnp.concatenate([cb_ref[n : n + 1, :] for n in range(cb_ref.shape[0])], 1)
    heads = dt_ref.shape[1]
    own = heads // QUAD
    inner = ng_ref.shape[1]
    width = inner // QUAD
    size = inner // heads

    def mine(a):
        total = jnp.zeros((a.shape[0], width), F32)
        for q in range(QUAD):
            cut = [a[:, (k * QUAD + q) * size : (k * QUAD + q + 1) * size] for k in range(own)]
            total = jnp.where(t == q, jnp.concatenate(cut, 1), total)
        return total

    taps = cw_ref.shape[0]
    cwb_ref[...] = jnp.zeros(cwb_ref.shape, F32)
    cwb_ref[0:taps, 0:width] = mine(cw_ref[...])
    cwb_ref[0:taps, width:] = cw_ref[:, inner:]
    cwb_ref[taps : taps + 1, 0:width] = mine(bias)
    cwb_ref[taps : taps + 1, width:] = bias[:, inner:]
    gain_ref[...] = mine(ng_ref[...])
    pick = (iota((heads, LANES), 0) == iota((heads, LANES), 1) * QUAD + t) & (
        iota((heads, LANES), 1) < own
    )
    rows = jnp.concatenate(
        [dt_ref[...], al_ref[...], sk_ref[...], jnp.zeros((5, heads), F32)], 0
    )
    head_ref[...] = mm_high(rows, pick.astype(F32))


def join_kernel(me_ref, c0, c1, c2, c3, wout_ref, a_ref, b_ref):
    t = me_ref[0] & (QUAD - 1)
    nrow = c0.shape[0]
    width = b_ref.shape[1]
    for r, c in enumerate((c0, c1, c2, c3)):
        at = pl.ds(pl.multiple_of((t ^ r) * nrow, nrow), nrow)
        a_ref[at, :] = c[:, width:]
        b_ref[at, :] = c[:, 0:width]
    size = wout_ref.shape[0]
    b_ref[QUAD * nrow : QUAD * nrow + size, :] = wout_ref[:, 0:width]
    b_ref[QUAD * nrow + size :, :] = wout_ref[:, width:]


def project_kernel(me_ref, *refs):
    chunks = 8
    acts, ws = refs[0:QUAD], refs[QUAD : QUAD + chunks]
    gain_ref, norm_ref, proj_ref, ends_ref, shared_ref = refs[QUAD + chunks :]
    zy = me_ref[0] // QUAD
    rows = ends_ref.shape[1]
    for r in range(QUAD):
        hidden = acts[r][0:rows, :].astype(F32)
        scale = lax.rsqrt(jnp.mean(hidden * hidden, axis=1, keepdims=True) + EPS)
        for k in range(chunks):
            at = pl.ds(pl.multiple_of((zy ^ k) * LANES, LANES), LANES)
            part = acts[r][0:rows, at].astype(F32) * scale * gain_ref[:, at]
            norm_ref[r * rows : (r + 1) * rows, k * LANES : (k + 1) * LANES] = part.astype(BF)
        ends_ref[r : r + 1, :] = acts[r][rows : rows + 16, 0:LANES].astype(F32)[0:1, :]
    w = jnp.concatenate([c[...] for c in ws], axis=0)
    proj = mm(norm_ref[...], w)
    proj_ref[...] = proj
    part = shared_ref.shape[1] // 2
    width = proj.shape[1] - 2 * part
    half = shared_ref.shape[0]
    shared = proj[:, width : width + part]
    shared_ref[...] = jnp.concatenate([shared[0:half, :], shared[half:, :]], 1).astype(BF)


def unfold(packed, flip):
    rows, part = packed.shape[0] // 2, packed.shape[1] // 2
    blocks = []
    for b in range(QUAD):
        j = b ^ flip
        blocks.append(
            packed[(j % 2) * rows : (j % 2 + 1) * rows, (j // 2) * part : (j // 2 + 1) * part]
        )
    return jnp.concatenate(blocks, 0)


def cot_kernel(me_ref, *refs):
    chunks = 8
    ws, acts = refs[0:chunks], refs[chunks : chunks + QUAD]
    wfull_ref, cot_ref, dgn_ref = refs[chunks + QUAD :]
    zy = me_ref[0] // QUAD
    width = ws[0].shape[1]
    size = width // chunks
    rows = cot_ref.shape[0] // QUAD
    for k in range(chunks):
        at = pl.ds(pl.multiple_of((zy ^ k) * size, size), size)
        base = ws[k].shape[0] - 2 * size
        wfull_ref[at, 0:width] = ws[k][base : base + size, :]
        wfull_ref[at, width:] = ws[k][base + size :, :]
    for r in range(QUAD):
        cot_ref[r * rows : (r + 1) * rows, :] = acts[r][rows + 16 :, :]
    dgn_ref[...] = mm_t(cot_ref[...], wfull_ref[...])


def gate_kernel(*refs):
    chunks = 8
    ws = refs[0:chunks]
    norm_ref, scan_ref, dgn_ref, gain_ref, z_ref, stat_ref = refs[chunks:]
    w = jnp.concatenate([c[0:LANES, :] for c in ws], axis=0)
    z = mm(norm_ref[...], w)
    z_ref[...] = z
    gated = scan_ref[...] * (z * sigmoid(z))
    s1 = jnp.sum(gated * gated, axis=1, keepdims=True)
    s2 = jnp.sum(gain_ref[...] * dgn_ref[...] * gated, axis=1, keepdims=True)
    lane = iota((z.shape[0], LANES), 1)
    both = jnp.where(lane == 0, s1, 0.0) + jnp.where(lane == 1, s2, 0.0)
    stat_ref[...] = both.T[0:8, :]


def ungate_kernel(inner, me_ref, *refs):
    chunks = 8
    stats, ws = refs[0:QUAD], refs[QUAD : QUAD + chunks]
    z_ref, scan_ref, dgn_ref, gain_ref, norm_ref, cot_ref = refs[QUAD + chunks : QUAD + chunks + 6]
    gn_ref, dscan_ref, dz_ref, ngain_ref, pre_ref = refs[QUAD + chunks + 6 : QUAD + chunks + 11]
    outs = dict(zip((0, 2, 4, 5, 7, 3), refs[QUAD + chunks + 11 :]))
    scr = refs[QUAD + chunks + 17]
    full = outs[0].shape[0]
    for one, two in ((7, 6), (3, 1)):
        outs[one], outs[two] = outs[one].at[0:full, :], outs[one].at[full:, :]
    zy = me_ref[0] // QUAD
    rows = stats[0].shape[1] // QUAD
    total = stats[0][...]
    for r in range(1, QUAD):
        total = total + jnp.concatenate(
            [stats[r][:, (b ^ r) * rows : ((b ^ r) + 1) * rows] for b in range(QUAD)], 1
        )
    pad = jnp.concatenate([total, jnp.zeros((LANES - 8, total.shape[1]), F32)], 0).T
    s1, s2 = pad[:, 0:1], pad[:, 1:2]
    r = lax.rsqrt(s1 / inner + EPS)
    z = z_ref[...]
    sig = sigmoid(z)
    silu = z * sig
    scan = scan_ref[...]
    gain = gain_ref[...]
    unit = scan * silu * r
    gn = (unit * gain).astype(BF)
    gn_ref[...] = gn
    scr[...] = mm_l(gn, cot_ref[...])
    dgn = dgn_ref[...]
    ngain_ref[...] = jnp.sum(dgn * unit, axis=0, keepdims=True)
    dgated = r * (gain * dgn) - unit * (r * r * s2 / inner)
    dscan_ref[...] = dgated * silu
    dz = (dgated * scan * (sig * (1.0 + z * (1.0 - sig)))).astype(BF)
    dz_ref[...] = dz
    width = dz.shape[1]
    size = width // chunks
    lane = iota((LANES, LANES), 1)
    pre = jnp.zeros((LANES, LANES), F32)
    for k in range(chunks):
        grad = mm_l(norm_ref[:, k * LANES : (k + 1) * LANES], dz)
        dot = jnp.sum(grad * ws[k][0:LANES, :].astype(F32), axis=1, keepdims=True)
        pre = pre + jnp.where(lane == k, dot, 0.0)
        out = outs[k]
        out[0:LANES, :] = grad.astype(out.dtype)
        at = pl.ds(pl.multiple_of((zy ^ k) * size, size), size)
        out[LANES : LANES + size, :] = scr[at, 0:width].astype(out.dtype)
        out[LANES + size : LANES + 2 * size, :] = scr[at, width:].astype(out.dtype)
    pre_ref[...] = pre


def put_small(out_ref, base, small):
    out_ref[base : base + SMALL, :] = small.astype(BF)


def get_small(ref, base):
    return ref[base : base + SMALL, :].astype(F32)


def ingrad_kernel(
    me_ref, norm_ref, pcx_ref, own_ref, g1, g2, g3, small_ref, ngain_ref, preb_ref, gain_ref, *refs
):
    chunks = 8
    ws, pc_ref, refs = refs[0:chunks], refs[chunks], refs[0:chunks] + refs[chunks + 1 :]
    part = own_ref.shape[1] // 2
    width = pc_ref.shape[1] - 2 * part
    shared = unfold(own_ref[...], 0)
    for r, g in ((1, g1), (2, g2), (3, g3)):
        shared = shared + unfold(g[...].astype(F32), r)
    pc_ref[:, 0:width] = pcx_ref[:, 0:width]
    pc_ref[:, width:] = jnp.concatenate(
        [shared, pcx_ref[:, width + part :].astype(F32)], 1
    ).astype(BF)
    outs = dict(zip((0, 2, 4, 6, 7, 3), refs[chunks : 2 * chunks - 2]))
    pair_ref = outs[7]
    outs[7], outs[5] = pair_ref.at[0:LANES, :], pair_ref.at[LANES : 2 * LANES, :]
    mine_ref, scr = refs[2 * chunks - 2 :]
    outs[3], outs[1] = outs[3].at[0:LANES, :], outs[3].at[LANES:, :]
    zy = me_ref[0] // QUAD
    lane = iota((LANES, LANES), 1)
    pre = preb_ref[...]
    for k in range(chunks):
        grad = mm_l(norm_ref[:, k * LANES : (k + 1) * LANES], pc_ref[...])
        dot = jnp.sum(grad * ws[k][...].astype(F32), axis=1, keepdims=True)
        pre = pre + jnp.where(lane == k, dot, 0.0)
        outs[k][0:LANES, :] = grad.astype(outs[k].dtype)
    pre = pre.T
    for k in range(chunks):
        scr[pl.ds(zy ^ k, 1), :] = pre[k : k + 1, :]
    wide = mine_ref.shape[1]
    per = wide // LANES
    gain = gain_ref[...]
    placed = jnp.concatenate([scr[k : k + 1, :] for k in range(chunks)], 1) / gain
    width = ngain_ref.shape[1]
    mine_ref[...] = small_ref[...]
    mine_ref[10:11, 0:width] = ngain_ref[...]
    mine_ref[12:13, :] = placed[:, 0:wide]
    mine_ref[13:14, 0 : (chunks - per) * LANES] = placed[:, wide:]
    put_small(pair_ref, 2 * LANES, mine_ref[...])


def add_near_kernel(keep_ref, got_ref, small_ref, out_ref, sum_ref):
    out_ref[0:LANES, :] = (keep_ref[...] + got_ref[0:LANES, :].astype(F32)).astype(BF)
    total = small_ref[...] + get_small(got_ref, 2 * LANES)
    sum_ref[...] = total
    put_small(out_ref, LANES, total)


def add_two_kernel(keep_ref, got_ref, out_ref):
    full = keep_ref.shape[0]
    out_ref[...] = (keep_ref[...] + got_ref[0:full, :].astype(F32)).astype(BF)


def add_far_kernel(keep_ref, got_ref, side_ref, out_ref):
    full = keep_ref.shape[0]
    out_ref[...] = (
        keep_ref[...] + got_ref[full:, :].astype(F32) + side_ref[...].astype(F32)
    ).astype(BF)


def add_last_kernel(keep_ref, got_ref, side_ref, small_ref, out_ref, sum_ref):
    out_ref[0:LANES, :] = (
        keep_ref[...]
        + got_ref[0:LANES, :].astype(F32)
        + side_ref[LANES : 2 * LANES, :].astype(F32)
    ).astype(BF)
    total = small_ref[...] + get_small(got_ref, LANES)
    sum_ref[...] = total
    put_small(out_ref, LANES, total)


def put_rows(part, keep_ref, send_ref, at):
    rows = keep_ref.shape[0] // 2
    keep_ref[0:rows, at] = part[0:rows, :]
    send_ref[0:rows, at] = part[rows : 2 * rows, :].astype(BF)
    keep_ref[rows:, at] = part[2 * rows : 3 * rows, :]
    send_ref[rows:, at] = part[3 * rows :, :].astype(BF)


def branch_kernel(gn_ref, wfull_ref, keep_ref, send_ref):
    put_rows(mm(gn_ref[...], wfull_ref[...]), keep_ref, send_ref, pl.ds(0, wfull_ref.shape[1]))


def tail_kernel(me_ref, *refs):
    chunks = 8
    w1, w2 = refs[0:chunks], refs[chunks : 2 * chunks]
    pc_ref, dz_ref, keep_ref, send_ref = refs[2 * chunks :]
    zy = me_ref[0] // QUAD
    for k in range(chunks):
        part = mm_t(pc_ref[...], w1[k][...]) + mm_t(dz_ref[...], w2[k][0:LANES, :])
        at = pl.ds(pl.multiple_of((zy ^ k) * LANES, LANES), LANES)
        put_rows(part, keep_ref, send_ref, at)


def pair_kernel(keep_ref, got_ref, mine_ref, send_ref):
    rows = mine_ref.shape[0]
    total = keep_ref[...] + got_ref[...].astype(F32)
    mine_ref[...] = total[0:rows, :]
    send_ref[...] = total[rows:, :].astype(BF)


def mixed_kernel(act_ref, a_ref, b_ref, mixed_ref):
    rows = mixed_ref.shape[0]
    hidden = act_ref[0:rows, :].astype(F32)
    end = act_ref[rows : rows + 16, 0:LANES].astype(F32)[0:1, 3:4]
    live = (iota((rows, 1), 0).astype(F32) < end).astype(F32)
    total = a_ref[...] + b_ref[...].astype(F32)
    mixed_ref[...] = (live * (hidden + total)).astype(BF)


def tokgrad_kernel(act_ref, gain_ref, a_ref, b_ref, grad_ref):
    rows = grad_ref.shape[0]
    hidden = act_ref[0:rows, :].astype(F32)
    scale = lax.rsqrt(jnp.mean(hidden * hidden, axis=1, keepdims=True) + EPS)
    dn = (a_ref[...] + b_ref[...].astype(F32)) * gain_ref[...]
    inner = jnp.mean(dn * hidden, axis=1, keepdims=True)
    back = scale * dn - hidden * (scale * scale * scale * inner)
    grad_ref[...] = act_ref[rows + 16 :, :].astype(F32) + back


def total_kernel(me_ref, *refs):
    a, b, small_ref = refs[0:4], refs[4:8], refs[8]
    wout_ref, mine_ref, msmall_ref, s1, s2, s3, scr = refs[9:]
    t = me_ref[0] & (QUAD - 1)
    nrow = mine_ref.shape[0]
    chunk = QUAD * nrow
    ta = a[0][...] + a[1][chunk:, :].astype(F32)
    for got in a[2:]:
        ta = ta + got[0:chunk, :].astype(F32)
    small = small_ref[...] + get_small(a[3], chunk)
    tb = b[0][...] + b[1][b[0].shape[0] :, :].astype(F32)
    for got in b[2:]:
        tb = tb + got[...].astype(F32)
    size = wout_ref.shape[0]
    width = tb.shape[1]
    wout_ref[:, 0:width] = tb[chunk : chunk + size, :]
    wout_ref[:, width:] = tb[chunk + size :, :]
    scr[:, 0:width] = tb[0:chunk, :]
    scr[:, width:] = ta
    msmall_ref[...] = small
    for r, out in enumerate((mine_ref, s1, s2, s3)):
        at = pl.ds(pl.multiple_of((t ^ r) * nrow, nrow), nrow)
        out[0:nrow, :] = scr[at, :].astype(out.dtype)
    wide = small.shape[1]
    for out in (s1, s2, s3):
        put_small(out.at[:, 0:wide], nrow, small)


def finish_kernel(me_ref, mine_ref, msmall_ref, *refs):
    got = refs[0:3]
    out_ref, cw_ref, cb_ref, dt_ref, al_ref, sk_ref, ng_ref, pg_ref, scr, sscr, row_ref = refs[3:]
    t = me_ref[0] & (QUAD - 1)
    nrow = mine_ref.shape[0]
    wide = msmall_ref.shape[1]
    scr[t] = mine_ref[...]
    sscr[t] = msmall_ref[...]
    for r in range(1, QUAD):
        scr[t ^ r] = got[r - 1][0:nrow, :].astype(F32)
        sscr[t ^ r] = get_small(got[r - 1].at[:, 0:wide], nrow)
    inner = ng_ref.shape[1]
    width = inner // QUAD
    heads = dt_ref.shape[1]
    size = inner // heads
    conv_end = out_ref.shape[1] - heads
    part = (conv_end - 2 * inner) // QUAD

    def added(ref, rows, lanes):
        return (ref[0][rows, lanes] + ref[1][rows, lanes]) + (ref[2][rows, lanes] + ref[3][rows, lanes])

    weave(out_ref, 0, [scr[q][:, 0:width] for q in range(QUAD)], size)
    weave(out_ref, inner, [scr[q][:, width : 2 * width] for q in range(QUAD)], size)
    out_ref[:, 2 * inner : conv_end] = jnp.concatenate(
        [scr[q][:, 2 * width : 2 * width + part] for q in range(QUAD)], 1
    )
    out_ref[:, conv_end:] = pick_heads(
        [scr[q][:, 2 * width + part :] for q in range(QUAD)], heads
    )
    weave(cw_ref, 0, [sscr[q][0:4, 0:width] for q in range(QUAD)], size)
    cw_ref[:, inner:] = added(sscr, slice(5, 9), slice(0, 2 * LANES))
    weave(row_ref, 0, [sscr[q][4:5, 0:width] for q in range(QUAD)], size)
    row_ref[:, inner:] = added(sscr, slice(9, 10), slice(0, 2 * LANES))
    for n in range(cb_ref.shape[0]):
        cb_ref[n : n + 1, :] = row_ref[:, n * LANES : (n + 1) * LANES]
    weave(ng_ref, 0, [sscr[q][10:11, 0:width] for q in range(QUAD)], size)
    lists = [
        pick_heads([sscr[q][8:16, at : at + LANES] for q in range(QUAD)], heads)[3:4, :]
        for at in (0, LANES, 2 * LANES)
    ]
    dt_ref[...], al_ref[...], sk_ref[...] = lists
    pg_ref[:, 0:wide] = added(sscr, slice(12, 13), slice(0, wide))
    pg_ref[:, wide:] = added(sscr, slice(13, 14), slice(0, pg_ref.shape[1] - wide))


def quad_shards(
    count,
    tokens,
    lengths,
    in_weight,
    out_weight,
    conv_weight,
    conv_bias,
    dt_bias,
    a_log,
    skip_gain,
    norm_gain,
    pre_gain,
    cotangent,
):
    chunks = count // QUAD
    rows, model = tokens.shape
    inner = norm_gain.shape[0]
    heads = dt_bias.shape[0]
    width = inner // QUAD
    size = inner // heads
    nrow, proj_width = in_weight.shape
    convw = width + conv_bias.shape[0] - inner
    part = (convw - width) // QUAD
    wide = width + 2 * part
    full = convw + LANES
    both = width + wide
    total_rows = QUAD * rows
    chunk = QUAD * nrow
    chunk_b = chunk + 2 * size

    def swap(a, mask):
        return lax.ppermute(a, "dp", [(i, i ^ mask) for i in range(count)])

    def after(a, *others):
        return lax.optimization_barrier((a,) + others)[0]

    def gather(mine, along=(), later=(), turn=()):
        z = after(mine, *later) if later else mine
        got = [mine, None, None, None, swap(z, 4 * QUAD), None, None, None]
        got[2] = swap(z, 2 * QUAD)
        got[1] = swap(mine, QUAD)
        got[4], got[2] = lax.optimization_barrier((got[4], got[2], got[1]) + along + turn)[0:2]
        got[5] = swap(got[4], QUAD)
        got[6] = swap(got[4], 2 * QUAD)
        got[3] = swap(got[2], QUAD)
        got[7] = swap(after(got[5], got[6]), 2 * QUAD)
        return got

    me = lax.axis_index("dp").astype(jnp.int32).reshape(1)

    lanes = conv_bias.reshape(-1, LANES)
    given = [in_weight, tokens, cotangent, conv_weight, lanes]
    given += [a[None, :] for a in (dt_bias, a_log, skip_gain, norm_gain, pre_gain)]
    prepped = call(
        prep_kernel,
        [
            ((2 * rows + 16, model), BF),
            ((8, convw), F32),
            ((8, LANES), F32),
            ((1, width), F32),
            ((1, model), F32),
        ]
        + [((nrow, both), BF)] * QUAD,
        [me, lengths] + given,
        [pltpu.VMEM((QUAD, nrow, both), BF)]
        + [pltpu.VMEM(a.shape, a.dtype) for a in given]
        + [pltpu.SemaphoreType.DMA((len(given),))],
        name="prep",
        raw=tuple(range(2, 12)),
        limit=RAW_BYTES,
    )
    act, cwb, by_head, gain, pre = prepped[0:5]
    cut = prepped[5:]
    got = [swap(cut[r], r) for r in range(1, QUAD)]
    beside = swap(act, 1)
    got[0] = after(got[0], beside)
    own_a, own_b = call(
        join_kernel,
        [((chunk, wide), BF), ((chunk_b, width), BF)],
        [me, cut[0]] + got + [out_weight],
        name="join",
    )
    across = swap(after(act, own_a), 2)
    w1 = gather(own_a, (across,))
    beyond = swap(across, 1)
    acts = [act, beside, across, beyond]
    w2 = gather(own_b, (), (w1[2],), (w1[3], w1[5]))
    normed, proj_own, ends, shared = call(
        project_kernel,
        [
            ((total_rows, model), BF),
            ((total_rows, wide), F32),
            ((QUAD, rows), F32),
            ((total_rows // 2, 2 * part), BF),
        ],
        [me] + acts + w1 + [pre],
        flops=PROJECT_COST,
        name="project",
    )
    scan_out, proj = call(
        scan_kernel,
        [((total_rows, width), F32), ((total_rows, full), F32)],
        [me, proj_own] + [swap(shared, r) for r in range(1, QUAD)] + [ends, cwb, by_head],
        [pltpu.VMEM((QUAD, total_rows, part), F32)],
        flops=SCAN_COST,
        name="scan",
    )
    w_full, cot_all, dgn = call(
        cot_kernel,
        [((width, model), BF), ((total_rows, model), BF), ((total_rows, width), F32)],
        [me] + w2 + acts,
        name="normcot",
    )
    z, stat = call(
        gate_kernel,
        [((total_rows, width), F32), ((8, total_rows), F32)],
        w2 + [normed, scan_out, dgn, gain],
        name="gate",
    )
    stats = [stat] + [swap(stat, r) for r in range(1, QUAD)]
    ungated = call(
        functools.partial(ungate_kernel, float(inner)),
        [
            ((total_rows, width), BF),
            ((total_rows, width), F32),
            ((total_rows, width), BF),
            ((1, width), F32),
            ((LANES, LANES), F32),
        ]
        + [((chunk_b, width), F32)] * 4
        + [((2 * chunk_b, width), BF)] * 2,
        [me] + stats + w2 + [z, scan_out, dgn, gain, normed, cot_all],
        [pltpu.VMEM((width, model), F32)],
        name="ungate",
    )
    gn, dscan, dz, ngain_part, pre_b = ungated[0:5]
    keep_b = ungated[5:9]

    got76_b, got31_b = swap(ungated[9], 2 * QUAD), swap(ungated[10], QUAD)
    fold = (total_rows // 2, 2 * part)
    pc_x, small, own_bc, *bc = call(
        scan_back_kernel,
        [((total_rows, wide), BF), ((SMALL, wide), F32), (fold, F32)] + [(fold, BF)] * 3,
        [me, proj, dscan, ends, cwb, by_head],
        [pltpu.VMEM((QUAD, total_rows, part), F32)],
        name="scanback",
    )
    got76_b, got31_b = lax.optimization_barrier((got76_b, got31_b, pc_x))[0:2]
    (side,) = call(add_two_kernel, [((chunk_b, width), BF)], [keep_b[3], got76_b], name="side")
    got5_b = swap(side, QUAD)
    (near,) = call(add_two_kernel, [((chunk_b, width), BF)], [keep_b[1], got31_b], name="near")
    got2_b = swap(near, 2 * QUAD)
    pair_shapes = [((2 * rows, model), F32), ((2 * rows, model), BF)]

    def pair(keep, send, *first):
        got = swap(send, 1)
        mine, cross = call(
            pair_kernel,
            [((rows, model), F32), ((rows, model), BF)],
            [keep, after(got, *first) if first else got],
            name="pair",
        )
        return mine, swap(cross, 2)

    mine_m, cross_m = pair(*call(branch_kernel, pair_shapes, [gn, w_full], name="branch"))
    (mixed,) = call(mixed_kernel, [((rows, model), BF)], [act, mine_m, cross_m], name="mixed")
    got_bc = [swap(a, r + 1) for r, a in enumerate(bc)]
    small, cross_m = lax.optimization_barrier((small, cross_m, near, side))[0:2]
    ingrads = call(
        ingrad_kernel,
        [((total_rows, wide), BF)]
        + [((chunk, wide), F32)] * 4
        + [((2 * chunk + SMALL, wide), BF), ((2 * chunk, wide), BF)]
        + [((SMALL, wide), F32)],
        [me, normed, pc_x, own_bc] + got_bc + [small, ngain_part, pre_b, pre] + w1,
        [pltpu.VMEM((chunks, LANES), F32)],
        name="ingrad",
    )
    pc1, *ingrads = ingrads
    keep_a, small = ingrads[0:4], ingrads[6]
    got75_a, got31_a = swap(ingrads[4], QUAD), swap(ingrads[5], QUAD)
    got5_b = after(got5_b, small)
    (far,) = call(
        add_far_kernel, [((chunk_b, width), BF)], [keep_b[2], got76_b, got5_b], name="far"
    )
    got4_b = swap(far, 4 * QUAD)
    far_b = far

    riding = [((chunk + SMALL, wide), BF), ((SMALL, wide), F32)]
    side, small1 = call(add_near_kernel, riding, [keep_a[3], got75_a, small], name="side")
    got6_a = swap(side, 2 * QUAD)
    far, small2 = call(add_last_kernel, riding, [keep_a[2], got6_a, got75_a, small1], name="far")
    (near,) = call(add_two_kernel, [((chunk, wide), BF)], [keep_a[1], got31_a], name="near")
    got2_a = swap(near, 2 * QUAD)
    got4_a = swap(far, 4 * QUAD)

    mine_t, cross_t = pair(
        *call(tail_kernel, pair_shapes, [me] + w1 + w2 + [after(pc1, far_b), dz], name="tail"), got4_b, got2_b
    )
    (tokens_grad,) = call(
        tokgrad_kernel, [((rows, model), F32)], [act, pre, mine_t, cross_t], name="tokgrad"
    )
    got4_a = after(got4_a, cross_t)

    out_shard, own, own_small, *cuts = call(
        total_kernel,
        [((size, model), F32), ((nrow, both), F32), ((SMALL, wide), F32)]
        + [((nrow + SMALL, both), BF)] * 3,
        [me, keep_a[0], got31_a, got2_a, got4_a, keep_b[0], got31_b, got2_b, got4_b, small2],
        [pltpu.VMEM((chunk, both), F32)],
        name="total",
    )
    own, mixed, tokens_grad = lax.optimization_barrier((own, mixed, tokens_grad))
    done = call(
        finish_kernel,
        [
            ((nrow, proj_width), F32),
            (conv_weight.shape, F32),
            ((conv_bias.shape[0] // LANES, LANES), F32),
            ((1, heads), F32),
            ((1, heads), F32),
            ((1, heads), F32),
            ((1, inner), F32),
            ((1, model), F32),
        ],
        [me, own, own_small] + [swap(a, r + 1) for r, a in enumerate(cuts)],
        [pltpu.VMEM((QUAD, nrow, both), F32), pltpu.VMEM((QUAD, SMALL, wide), F32), pltpu.VMEM((1, conv_bias.shape[0]), F32)],
        name="finish",
    )
    return (mixed, tokens_grad, done[0], out_shard, done[1]) + tuple(
        a.reshape(-1) for a in done[2:]
    )


def prenorm(hidden_in, gain_row):
    return (
        hidden_in
        * lax.rsqrt(jnp.mean(hidden_in * hidden_in, axis=-1, keepdims=True) + EPS)
        * gain_row
    )


def shifted(array, offset, filler):
    padding = jnp.full((offset,) + array.shape[1:], filler, array.dtype)
    return jnp.concatenate([padding, array[:-offset]], axis=0)


def segments(seq_lengths, row_count):
    seq_ends = jnp.cumsum(seq_lengths, dtype=jnp.int32)
    position = jnp.arange(row_count, dtype=jnp.int32)
    segment = jnp.sum(
        (position[:, None] >= seq_ends[None, :]).astype(jnp.int32), axis=1, dtype=jnp.int32
    )
    live_rows = (position < seq_ends[-1]).astype(jnp.float32)
    return (segment, live_rows)


def block_step(carry, block_item):
    state_mat, prev_segment = carry
    values, key_rows, read_rows, step_size, log_decay, block_segment = block_item
    cumulative = jnp.cumsum(log_decay, axis=0)
    position = jnp.arange(block_segment.shape[0], dtype=jnp.int32)
    causal = (block_segment[:, None] == block_segment[None, :]) & (
        position[:, None] >= position[None, :]
    )
    distance = cumulative[:, None, :] - cumulative[None, :, :]
    decay_mask = jnp.where(
        causal[:, :, None], jnp.exp(jnp.where(causal[:, :, None], distance, 0.0)), 0.0
    )
    scores = jnp.dot(read_rows, key_rows.T, precision=HIGH)
    weighting = scores[:, :, None] * decay_mask * step_size[None, :, :]
    inside = jnp.einsum("ijh,jhp->ihp", weighting, values, precision=HIGH)
    entering = (block_segment == prev_segment).astype(jnp.float32)
    carried = jnp.einsum("in,hnp->ihp", read_rows, state_mat, precision=HIGH)
    carried = carried * (jnp.exp(cumulative) * entering[:, None])[:, :, None]
    last_same = (block_segment == block_segment[-1]).astype(jnp.float32)
    tail_weight = jnp.exp(cumulative[-1][None, :] - cumulative) * last_same[:, None] * step_size
    new_state = state_mat * (jnp.exp(cumulative[-1]) * entering[-1])[:, None, None]
    new_state = new_state + jnp.einsum(
        "jn,jh,jhp->hnp", key_rows, tail_weight, values, precision=HIGH
    )
    return ((new_state, block_segment[-1]), inside + carried)


def mixer_core(projected, conv_weight, conv_bias, dt_bias, a_log, skip_gain, norm_gain, segment):
    inner_width = norm_gain.shape[0]
    head_count = dt_bias.shape[0]
    conv_width = conv_bias.shape[0]
    state_width = (conv_width - inner_width) // 2
    head_size = inner_width // head_count
    row_count = projected.shape[0]
    gate_in = projected[:, :inner_width]
    conv_src = projected[:, inner_width : inner_width + conv_width]
    dt_raw = projected[:, inner_width + conv_width :]
    conv_sum = conv_bias[None, :] + conv_weight[0][None, :] * conv_src
    for offset in range(1, conv_weight.shape[0]):
        same_rows = (segment == shifted(segment, offset, -1)).astype(jnp.float32)
        conv_sum = (
            conv_sum
            + conv_weight[offset][None, :] * shifted(conv_src, offset, 0.0) * same_rows[:, None]
        )
    activated = jax.nn.silu(conv_sum)
    values = activated[:, :inner_width].reshape(row_count, head_count, head_size)
    key_rows = activated[:, inner_width : inner_width + state_width]
    read_rows = activated[:, inner_width + state_width :]
    step_size = jax.nn.softplus(dt_raw + dt_bias[None, :])
    log_decay = -step_size * jnp.exp(a_log)[None, :]
    blocks = row_count // SCAN_ROWS
    items = (
        values.reshape(blocks, SCAN_ROWS, head_count, head_size),
        key_rows.reshape(blocks, SCAN_ROWS, state_width),
        read_rows.reshape(blocks, SCAN_ROWS, state_width),
        step_size.reshape(blocks, SCAN_ROWS, head_count),
        log_decay.reshape(blocks, SCAN_ROWS, head_count),
        segment.reshape(blocks, SCAN_ROWS),
    )
    start = (jnp.zeros((head_count, state_width, head_size), jnp.float32), jnp.array(-1, jnp.int32))
    _, scanned = lax.scan(jax.checkpoint(block_step), start, items)
    scan_out = scanned.reshape(row_count, inner_width) + (
        skip_gain[None, :, None] * values
    ).reshape(row_count, inner_width)
    gated_out = scan_out * jax.nn.silu(gate_in)
    return (
        gated_out
        * lax.rsqrt(jnp.mean(gated_out * gated_out, axis=-1, keepdims=True) + EPS)
        * norm_gain[None, :]
    )


def shards(
    tokens,
    lengths,
    in_weight,
    out_weight,
    conv_weight,
    conv_bias,
    dt_bias,
    a_log,
    skip_gain,
    norm_gain,
    pre_gain,
    cotangent,
):
    w_in, w_out = (
        lax.all_gather(in_weight, "dp", axis=0, tiled=True),
        lax.all_gather(out_weight, "dp", axis=0, tiled=True),
    )
    segment, live_rows = segments(lengths, tokens.shape[0])
    hidden_in = tokens.astype(jnp.float32)
    normed, norm_back = jax.vjp(prenorm, hidden_in, pre_gain)
    normed_low = normed.astype(jnp.bfloat16)
    projected = jnp.dot(normed_low, w_in, preferred_element_type=jnp.float32)
    proj_width = projected.shape[1]

    def mixer_local(proj_rows, conv_w, conv_b, bias_dt, decay_log, skip_w, gain_w):
        return mixer_core(proj_rows, conv_w, conv_b, bias_dt, decay_log, skip_w, gain_w, segment)

    gated_norm, mixer_back = jax.vjp(
        mixer_local, projected, conv_weight, conv_bias, dt_bias, a_log, skip_gain, norm_gain
    )
    gated_low = gated_norm.astype(jnp.bfloat16)
    branch = jnp.dot(gated_low, w_out, preferred_element_type=jnp.float32)
    mixed = (live_rows[:, None] * (hidden_in + branch)).astype(jnp.bfloat16)
    w_in, w_out = (
        lax.all_gather(in_weight, "dp", axis=0, tiled=True),
        lax.all_gather(out_weight, "dp", axis=0, tiled=True),
    )
    out_cot = cotangent.astype(jnp.float32) * live_rows[:, None]
    out_cot_low = out_cot.astype(jnp.bfloat16)
    norm_cot = lax.dot_general(
        out_cot_low, w_out, (((1,), (1,)), ((), ())), preferred_element_type=jnp.float32
    )
    proj_cot, conv_w_grad, conv_b_grad, bias_dt_grad, decay_grad, skip_grad, gain_grad = mixer_back(
        norm_cot
    )
    proj_cot_low = proj_cot.astype(jnp.bfloat16)
    normed_cot = lax.dot_general(
        proj_cot_low, w_in, (((1,), (1,)), ((), ())), preferred_element_type=jnp.float32
    )
    hidden_cot, pre_grad = norm_back(normed_cot)
    tokens_grad = out_cot + hidden_cot
    out_grad = lax.dot_general(
        gated_low, out_cot_low, (((0,), (0,)), ((), ())), preferred_element_type=jnp.float32
    )
    in_grad = lax.dot_general(
        normed_low, proj_cot_low, (((0,), (0,)), ((), ())), preferred_element_type=jnp.float32
    )
    in_wide = in_grad.reshape(2 * in_grad.shape[0], proj_width // 2)
    in_folded, out_shard = (
        lax.psum_scatter(in_wide, "dp", scatter_dimension=0, tiled=True),
        lax.psum_scatter(out_grad, "dp", scatter_dimension=0, tiled=True),
    )
    in_shard = in_folded.reshape(in_weight.shape[0], proj_width)
    summed = lax.psum(
        (conv_w_grad, conv_b_grad, bias_dt_grad, decay_grad, skip_grad, gain_grad, pre_grad), "dp"
    )
    return (
        mixed,
        tokens_grad,
        in_shard,
        out_shard,
        summed[0],
        summed[1],
        summed[2],
        summed[3],
        summed[4],
        summed[5],
        summed[6],
    )


def solution(mesh):
    count = mesh.shape["dp"]
    body = functools.partial(quad_shards, count) if count == 32 else shards
    return jax.shard_map(
        body,
        mesh=mesh,
        in_specs=(
            P("dp", None),
            P("dp"),
            P("dp", None),
            P("dp", None),
            P(),
            P(),
            P(),
            P(),
            P(),
            P(),
            P(),
            P("dp", None),
        ),
        out_specs=(
            P("dp", None),
            P("dp", None),
            P("dp", None),
            P("dp", None),
            P(),
            P(),
            P(),
            P(),
            P(),
            P(),
            P(),
        ),
        check_vma=False,
    )
```

```python
import functools

import jax
import jax.numpy as jnp
from jax import lax
from jax.experimental import pallas as pl
from jax.experimental.pallas import tpu as pltpu
from jax.sharding import PartitionSpec as P

SCAN_ROWS = 64


EPS = 1e-05
HIGH = lax.Precision.HIGHEST
BF = jnp.bfloat16
F32 = jnp.float32
NEG = -1e30
LANES = 128
OPT = {'along': 0, 'bsync': 1, 'abyy': 0, 'bbyy': 0, 'atie7': 1, 'btie7': 1, 'actx': 1, 'later': 1, 'turn': 1, 'pcost': 4000000000.0, 'scost': 16000000000.0, 'ucost': 1000.0, 'async': 1, 'y1b': 0, 'r1': 0, 'r2': 4, 'r3': 5, 'r4': 1, 'r5': 0, 'r6': 1, 'r7': 0, 'r8': 2, 'bcost': 1000.0}
PROJECT_COST = 4e9
SCAN_COST = 1.6e10
QUAD = 4
SMALL = 16
VMEM_BYTES = 44 * 1024 * 1024


def mm(a, b):
    return lax.dot_general(a, b, (((1,), (0,)), ((), ())), preferred_element_type=F32)


def mm_t(a, b):
    return lax.dot_general(a, b, (((1,), (1,)), ((), ())), preferred_element_type=F32)


def mm_l(a, b):
    return lax.dot_general(a, b, (((0,), (0,)), ((), ())), preferred_element_type=F32)


def mm_high(a, b):
    return lax.dot_general(
        a, b, (((1,), (0,)), ((), ())), precision=HIGH, preferred_element_type=F32
    )


def call(kernel, out_shapes, inputs, scratch=(), flops=1e3, name=None, raw=(), limit=VMEM_BYTES):
    in_specs = [
        pl.BlockSpec(
            memory_space=pltpu.HBM
            if n in raw
            else (pltpu.SMEM if a.dtype == jnp.int32 else pltpu.VMEM)
        )
        for n, a in enumerate(inputs)
    ]
    shapes = [jax.ShapeDtypeStruct(s, d) for s, d in out_shapes]
    inputs = [
        pltpu.with_memory_space_constraint(a, pltpu.HBM) if n in raw else a
        for n, a in enumerate(inputs)
    ]
    return pl.pallas_call(
        kernel,
        out_shape=shapes,
        in_specs=in_specs,
        out_specs=[pl.BlockSpec(memory_space=pltpu.VMEM)] * len(shapes),
        scratch_shapes=list(scratch),
        cost_estimate=pl.CostEstimate(flops=int(flops), bytes_accessed=1024, transcendentals=0),
        compiler_params=pltpu.CompilerParams(vmem_limit_bytes=limit),
        name=name,
    )(*inputs)


def iota(shape, axis):
    return lax.broadcasted_iota(jnp.int32, shape, axis)


def sigmoid(v):
    return 1.0 / (1.0 + jnp.exp(-v))


def softplus(v):
    return jnp.maximum(v, 0.0) + jnp.log1p(jnp.exp(-jnp.abs(v)))


def segment_of(position, ends):
    seg = jnp.zeros(position.shape, jnp.int32)
    for s in range(4):
        seg = seg + (position >= ends[:, s : s + 1]).astype(jnp.int32)
    return seg


def same_masks(ends, rows, taps):
    position = iota((rows, 1), 0)
    seg = segment_of(position, ends)
    masks = []
    for k in range(1, taps):
        seg_k = segment_of(position - k, ends)
        masks.append(((seg == seg_k) & (position >= k)).astype(F32))
    return masks


def scan_bias(ends, rows):
    seg_col = segment_of(iota((rows, 1), 0), ends)
    seg_row = segment_of(iota((1, rows), 1), ends)
    causal = (seg_col == seg_row) & (iota((rows, rows), 0) >= iota((rows, rows), 1))
    return jnp.where(causal, 0.0, NEG)


def tri_block(rows):
    i, j = iota((rows, rows), 0), iota((rows, rows), 1)
    return ((i >= j) & (i // SCAN_ROWS == j // SCAN_ROWS)).astype(F32)


def steps_of(dt_raw, dtb, neg_rate, rows):
    step = softplus(dt_raw + dtb)
    log_decay = step * neg_rate
    cum = mm_high(tri_block(rows), log_decay)
    return step, log_decay, cum


def decay_of(cum, cum_t, head, bias, cross):
    dist = cum[:, head : head + 1] - cum_t[head : head + 1, :]
    last = cum[SCAN_ROWS - 1 : SCAN_ROWS, head : head + 1]
    return jnp.exp(dist + cross * last + bias)


def conv_sum_of(xbc, cw, cb, masks):
    total = cb + cw[0:1, :] * xbc
    for k in range(1, len(masks) + 1):
        total = total + cw[k : k + 1, :] * (pltpu.roll(xbc, k, 0) * masks[k - 1])
    return total


def pair_lanes(row, pair, low):
    return jnp.where(low, row[:, 2 * pair : 2 * pair + 1], row[:, 2 * pair + 1 : 2 * pair + 2])


def scan_kernel(me_ref, own_ref, g1, g2, g3, ends_ref, cw_ref, head_ref, out_ref, proj_ref, scr):
    rows = LANES
    width = out_ref.shape[1]
    t = me_ref[0] & (QUAD - 1)
    part = scr.shape[2]
    scr[t] = own_ref[:, width : width + part]
    for r, g in ((1, g1), (2, g2), (3, g3)):
        scr[t ^ r] = unfold(g[...].astype(F32), r)
    proj_ref[:, 0:width] = own_ref[:, 0:width]
    proj_ref[:, width : width + 2 * LANES] = jnp.concatenate([scr[q] for q in range(QUAD)], 1)
    proj_ref[:, width + 2 * LANES :] = jnp.concatenate(
        [own_ref[:, width + part :], jnp.zeros((own_ref.shape[0], LANES - part), F32)], 1
    )
    pairs = width // LANES
    convw = width + 2 * LANES
    dtb, rate, skip = head_ref[0:1, :], head_ref[1:2, :], head_ref[2:3, :]
    neg_rate = -jnp.exp(rate)
    cross = ((iota((rows, rows), 0) >= SCAN_ROWS) & (iota((rows, rows), 1) < SCAN_ROWS)).astype(F32)
    low = iota((rows, LANES), 1) < LANES // 2

    def body(b, carry):
        at = pl.ds(pl.multiple_of(b * rows, rows), rows)
        ends = ends_ref[pl.ds(b, 1), :].astype(jnp.int32)
        bias = scan_bias(ends, rows)
        masks = same_masks(ends, rows, 4)
        xbc = proj_ref[at, 0:convw]
        conv = conv_sum_of(xbc, cw_ref[...], cw_ref[4:5, :], masks)
        act = conv * sigmoid(conv)
        key, read = act[:, width : width + LANES], act[:, width + LANES : convw]
        scores = mm_t(read.astype(BF), key.astype(BF))
        step, _, cum = steps_of(proj_ref[at, convw : convw + LANES], dtb, neg_rate, rows)
        cum_t = cum.T
        for p in range(pairs):
            lanes = slice(p * LANES, (p + 1) * LANES)
            x = act[:, lanes]
            xs = x * pair_lanes(step, p, low)
            weight = jnp.concatenate(
                [scores * decay_of(cum, cum_t, h, bias, cross) for h in (2 * p, 2 * p + 1)], 1
            )
            split = jnp.concatenate([jnp.where(low, xs, 0.0), jnp.where(low, 0.0, xs)], 0)
            y = mm(weight.astype(BF), split.astype(BF))
            out_ref[at, lanes] = y + pair_lanes(skip, p, low[0:1, :]) * x
        return carry

    lax.fori_loop(0, ends_ref.shape[0], body, 0)


def scan_back_kernel(
    me_ref, proj_ref, dscan_ref, ends_ref, cw_ref, head_ref, pc_ref, small_ref, p0, p1, p2, p3, scr
):
    rows = LANES
    width = dscan_ref.shape[1]
    pairs = width // LANES
    own = 2 * pairs
    convw = width + 2 * LANES
    dtb, rate, skip = head_ref[0:1, :], head_ref[1:2, :], head_ref[2:3, :]
    neg_rate = -jnp.exp(rate)
    src, dst = iota((rows, rows), 0), iota((rows, rows), 1)
    cross = ((src < SCAN_ROWS) & (dst >= SCAN_ROWS)).astype(F32)
    before = (src < dst).astype(F32)
    reach = (src >= dst).astype(BF)
    lane = iota((rows, LANES), 1)
    low = lane < LANES // 2
    by_head = (iota((width, LANES), 0) // (width // own) == iota((width, LANES), 1)).astype(F32)
    small_ref[...] = jnp.zeros(small_ref.shape, F32)
    t = me_ref[0] & (QUAD - 1)
    part = scr.shape[2]

    def add_small(k, v):
        total = jnp.sum(v, axis=0, keepdims=True)
        small_ref[k : k + 1, 0:width] += total[:, 0:width]
        small_ref[5 + k : 6 + k, 0 : 2 * LANES] += total[:, width:]

    def body(b, dskip):
        at = pl.ds(pl.multiple_of(b * rows, rows), rows)
        ends = ends_ref[pl.ds(b, 1), :].astype(jnp.int32)
        seg_col = segment_of(iota((rows, 1), 0), ends)
        seg_row = segment_of(iota((1, rows), 1), ends)
        bias = jnp.where((seg_col == seg_row) & (src <= dst), 0.0, NEG)
        masks = same_masks(ends, rows, 4)
        xbc = proj_ref[at, 0:convw]
        cw = cw_ref[...]
        conv = conv_sum_of(xbc, cw, cw[4:5, :], masks)
        sig = sigmoid(conv)
        act = conv * sig
        key = act[:, width : width + LANES].astype(BF)
        read = act[:, width + LANES : convw].astype(BF)
        scores = mm_t(key, read)
        scores = jnp.concatenate([scores, scores], 1)
        raw = proj_ref[at, convw : convw + LANES]
        step, log_decay, cum = steps_of(raw, dtb, neg_rate, rows)
        cum_t = cum.T
        dscores = jnp.zeros((rows, 2 * rows), F32)
        dlogs, dxs, prods, dsk = [], [], [], []
        for p in range(pairs):
            lanes = slice(p * LANES, (p + 1) * LANES)
            x = act[:, lanes]
            s = pair_lanes(step, p, low)
            decays = []
            for h in (2 * p, 2 * p + 1):
                last = cum[SCAN_ROWS - 1 : SCAN_ROWS, h : h + 1]
                dist = cum_t[h : h + 1, :] - cum[:, h : h + 1]
                decays.append(jnp.exp(dist + (cross * last + bias)))
            decay = jnp.concatenate(decays, 1)
            weight = scores * decay
            dy = dscan_ref[at, lanes]
            split = jnp.concatenate([jnp.where(low, dy, 0.0), jnp.where(low, 0.0, dy)], 0).astype(BF)
            dweight = mm_t((x * s).astype(BF), split)
            dx_s = mm(weight.astype(BF), split)
            dscores = dscores + dweight * decay
            t = (dweight * weight).astype(BF)
            span = mm(jnp.concatenate([t[:, 0:rows], t[:, rows:]], 0), reach)
            dlogs.append(jnp.sum(span[0:rows, :] * before, axis=0, keepdims=True))
            dlogs.append(jnp.sum(span[rows:, :] * before, axis=0, keepdims=True))
            prods.append(dx_s * x)
            dsk.append(jnp.sum(dy * x, axis=0, keepdims=True))
            dxs.append(dx_s * s + pair_lanes(skip, p, low[0:1, :]) * dy)
        dlog = jnp.concatenate(dlogs + [jnp.zeros((rows - own, rows), F32)], 0).T
        dstep = mm_high(jnp.concatenate(prods, 1), by_head) + dlog * neg_rate
        ddt = jnp.where(lane < own, dstep * sigmoid(raw + dtb), 0.0)
        dsc = (dscores[:, 0:rows] + dscores[:, rows:]).astype(BF)
        dkey = mm(dsc, read)
        dread = mm_l(dsc, key)
        dconv = jnp.concatenate(dxs + [dkey, dread], 1) * (sig * (1.0 + conv * (1.0 - sig)))
        dxbc = cw[0:1, :] * dconv
        add_small(0, dconv * xbc)
        for k in range(1, 4):
            masked = dconv * masks[k - 1]
            dxbc = dxbc + cw[k : k + 1, :] * pltpu.roll(masked, rows - k, 0)
            add_small(k, masked * pltpu.roll(xbc, k, 0))
        add_small(4, dconv)
        small_ref[11:12, 0:LANES] += jnp.sum(ddt, axis=0, keepdims=True)
        small_ref[11:12, LANES : 2 * LANES] += jnp.sum(dlog * log_decay, axis=0, keepdims=True)
        pc_ref[at, 0:width] = dxbc[:, 0:width].astype(BF)
        for q in range(QUAD):
            scr[q, at, :] = dxbc[:, width + q * part : width + (q + 1) * part]
        pc_ref[at, width + part :] = ddt[:, 0:part].astype(BF)
        return dskip + jnp.concatenate(dsk, 1)

    dskip = lax.fori_loop(0, ends_ref.shape[0], body, jnp.zeros((1, width), F32))
    small_ref[11:12, 2 * LANES : 3 * LANES] = mm_high(dskip, by_head)
    half = scr.shape[1] // 2
    for r, out in enumerate((p0, p1, p2, p3)):
        mine = scr[t ^ r]
        out[...] = jnp.concatenate([mine[0:half, :], mine[half:, :]], 1).astype(out.dtype)


def weave(out_ref, at, parts, size):
    for k in range(8):
        for half in range(QUAD // 2):
            pair = [p[:, k * size : (k + 1) * size] for p in parts[2 * half : 2 * half + 2]]
            lo = at + (k * QUAD + 2 * half) * size
            out_ref[:, lo : lo + 2 * size] = jnp.concatenate(pair, 1)


def pick_heads(parts, heads):
    total = None
    for q in range(QUAD):
        deep = (parts[q].shape[1], heads)
        sel = (iota(deep, 1) == iota(deep, 0) * QUAD + q).astype(F32)
        got = mm_high(parts[q], sel)
        total = got if total is None else total + got
    return total


def prep_kernel(me_ref, len_hbm, *refs):
    raws = refs[0:11]
    act_ref, cwb_ref, head_ref, gain_ref, pre_ref = refs[11:16]
    outs, wout_ref, scr = refs[16:20], refs[20], refs[21]
    w_ref, tok_ref, cot_ref = refs[22:25]
    sems, len_ref = refs[32], refs[33]
    lens = pltpu.make_async_copy(len_hbm, len_ref, sems.at[len(raws)])
    lens.start()
    copies = [
        pltpu.make_async_copy(src, dst, sems.at[n])
        for n, (src, dst) in enumerate(zip(raws, refs[22:32] + (wout_ref,)))
    ]
    for c in copies:
        c.start()
    rows, model = tok_ref.shape
    t = me_ref[0] & (QUAD - 1)
    heads = 32
    own = heads // QUAD
    copies[0].wait()
    w = w_ref[...].astype(F32)
    inner = gain_ref.shape[1] * QUAD
    size = inner // heads
    conv_end = w.shape[1] - heads
    shared = w[:, 2 * inner : conv_end]
    dts = w[:, conv_end:].astype(BF)
    for q in range(QUAD):
        zs, xs = [], []
        for k in range(own):
            at = (k * QUAD + q) * size
            zs.append(w[:, at : at + size])
            xs.append(w[:, inner + at : inner + at + size])
        part = shared.shape[1] // QUAD
        pick = (iota((heads, part), 0) == iota((heads, part), 1) * QUAD + q) & (
            iota((heads, part), 1) < own
        )
        mine = [shared[:, q * part : (q + 1) * part], mm(dts, pick.astype(BF))]
        scr[q] = jnp.concatenate(zs + xs + mine, 1).astype(BF)
    for r in range(QUAD):
        outs[r][...] = scr[t ^ r]
    lane = iota((16, model), 1)
    lens.wait()
    end = jnp.int32(0)
    tail = jnp.zeros((16, model), jnp.int32)
    for s in range(4):
        end = end + len_ref[s]
        tail = tail + jnp.where(lane == s, end, 0)
    act_ref[rows : rows + 16, :] = tail.astype(F32).astype(BF)
    copies[1].wait()
    act_ref[0:rows, :] = tok_ref[...]
    copies[2].wait()
    live = (iota((rows, 1), 0) < end).astype(F32)
    act_ref[rows + 16 :, :] = (cot_ref[...].astype(F32) * live).astype(BF)
    for c in copies[3:]:
        c.wait()
    share_params(t, refs[25:32], cwb_ref, head_ref, gain_ref, pre_ref)


def share_params(t, given, cwb_ref, head_ref, gain_ref, pre_ref):
    cw_ref, cb_ref, dt_ref, al_ref, sk_ref, ng_ref, pg_ref = given
    pre_ref[...] = pg_ref[...]
    bias = jnp.concatenate([cb_ref[n : n + 1, :] for n in range(cb_ref.shape[0])], 1)
    heads = dt_ref.shape[1]
    own = heads // QUAD
    inner = ng_ref.shape[1]
    width = inner // QUAD
    size = inner // heads

    def mine(a):
        total = jnp.zeros((a.shape[0], width), F32)
        for q in range(QUAD):
            cut = [a[:, (k * QUAD + q) * size : (k * QUAD + q + 1) * size] for k in range(own)]
            total = jnp.where(t == q, jnp.concatenate(cut, 1), total)
        return total

    taps = cw_ref.shape[0]
    cwb_ref[...] = jnp.zeros(cwb_ref.shape, F32)
    cwb_ref[0:taps, 0:width] = mine(cw_ref[...])
    cwb_ref[0:taps, width:] = cw_ref[:, inner:]
    cwb_ref[taps : taps + 1, 0:width] = mine(bias)
    cwb_ref[taps : taps + 1, width:] = bias[:, inner:]
    gain_ref[...] = mine(ng_ref[...])
    pick = (iota((heads, LANES), 0) == iota((heads, LANES), 1) * QUAD + t) & (
        iota((heads, LANES), 1) < own
    )
    rows = jnp.concatenate(
        [dt_ref[...], al_ref[...], sk_ref[...], jnp.zeros((5, heads), F32)], 0
    )
    head_ref[...] = mm_high(rows, pick.astype(F32))


def join_kernel(me_ref, c0, c1, c2, c3, wout_ref, a_ref, b_ref):
    t = me_ref[0] & (QUAD - 1)
    nrow = c0.shape[0]
    width = b_ref.shape[1]
    for r, c in enumerate((c0, c1, c2, c3)):
        at = pl.ds(pl.multiple_of((t ^ r) * nrow, nrow), nrow)
        a_ref[at, :] = c[:, width:]
        b_ref[at, :] = c[:, 0:width]
    size = wout_ref.shape[0]
    b_ref[QUAD * nrow : QUAD * nrow + size, :] = wout_ref[:, 0:width]
    b_ref[QUAD * nrow + size :, :] = wout_ref[:, width:]


def project_kernel(me_ref, *refs):
    chunks = 8
    acts, ws = refs[0:QUAD], refs[QUAD : QUAD + chunks]
    gain_ref, norm_ref, proj_ref, ends_ref, shared_ref = refs[QUAD + chunks :]
    zy = me_ref[0] // QUAD
    rows = ends_ref.shape[1]
    for r in range(QUAD):
        hidden = acts[r][0:rows, :].astype(F32)
        scale = lax.rsqrt(jnp.mean(hidden * hidden, axis=1, keepdims=True) + EPS)
        for k in range(chunks):
            at = pl.ds(pl.multiple_of((zy ^ k) * LANES, LANES), LANES)
            part = acts[r][0:rows, at].astype(F32) * scale * gain_ref[:, at]
            norm_ref[r * rows : (r + 1) * rows, k * LANES : (k + 1) * LANES] = part.astype(BF)
        ends_ref[r : r + 1, :] = acts[r][rows : rows + 16, 0:LANES].astype(F32)[0:1, :]
    w = jnp.concatenate([c[...] for c in ws], axis=0)
    proj = mm(norm_ref[...], w)
    proj_ref[...] = proj
    part = shared_ref.shape[1] // 2
    width = proj.shape[1] - 2 * part
    half = shared_ref.shape[0]
    shared = proj[:, width : width + part]
    shared_ref[...] = jnp.concatenate([shared[0:half, :], shared[half:, :]], 1).astype(BF)


def unfold(packed, flip):
    rows, part = packed.shape[0] // 2, packed.shape[1] // 2
    blocks = []
    for b in range(QUAD):
        j = b ^ flip
        blocks.append(
            packed[(j % 2) * rows : (j % 2 + 1) * rows, (j // 2) * part : (j // 2 + 1) * part]
        )
    return jnp.concatenate(blocks, 0)


def cot_kernel(me_ref, *refs):
    chunks = 8
    ws, acts = refs[0:chunks], refs[chunks : chunks + QUAD]
    wfull_ref, cot_ref, dgn_ref = refs[chunks + QUAD :]
    zy = me_ref[0] // QUAD
    width = ws[0].shape[1]
    size = width // chunks
    rows = cot_ref.shape[0] // QUAD
    for k in range(chunks):
        at = pl.ds(pl.multiple_of((zy ^ k) * size, size), size)
        base = ws[k].shape[0] - 2 * size
        wfull_ref[at, 0:width] = ws[k][base : base + size, :]
        wfull_ref[at, width:] = ws[k][base + size :, :]
    for r in range(QUAD):
        cot_ref[r * rows : (r + 1) * rows, :] = acts[r][rows + 16 :, :]
    dgn_ref[...] = mm_t(cot_ref[...], wfull_ref[...])


def gate_kernel(*refs):
    chunks = 8
    ws = refs[0:chunks]
    norm_ref, scan_ref, dgn_ref, gain_ref, z_ref, stat_ref = refs[chunks:]
    w = jnp.concatenate([c[0:LANES, :] for c in ws], axis=0)
    z = mm(norm_ref[...], w)
    z_ref[...] = z
    gated = scan_ref[...] * (z * sigmoid(z))
    s1 = jnp.sum(gated * gated, axis=1, keepdims=True)
    s2 = jnp.sum(gain_ref[...] * dgn_ref[...] * gated, axis=1, keepdims=True)
    lane = iota((z.shape[0], LANES), 1)
    both = jnp.where(lane == 0, s1, 0.0) + jnp.where(lane == 1, s2, 0.0)
    stat_ref[...] = both.T[0:8, :]


def ungate_kernel(inner, me_ref, *refs):
    chunks = 8
    stats, ws = refs[0:QUAD], refs[QUAD : QUAD + chunks]
    z_ref, scan_ref, dgn_ref, gain_ref, norm_ref, cot_ref = refs[QUAD + chunks : QUAD + chunks + 6]
    gn_ref, dscan_ref, dz_ref, ngain_ref, pre_ref = refs[QUAD + chunks + 6 : QUAD + chunks + 11]
    outs = dict(zip((0, 2, 4, 5, 7, 3), refs[QUAD + chunks + 11 :]))
    scr = refs[QUAD + chunks + 17]
    full = outs[0].shape[0]
    for one, two in ((7, 6), (3, 1)):
        outs[one], outs[two] = outs[one].at[0:full, :], outs[one].at[full:, :]
    zy = me_ref[0] // QUAD
    rows = stats[0].shape[1] // QUAD
    total = stats[0][...]
    for r in range(1, QUAD):
        total = total + jnp.concatenate(
            [stats[r][:, (b ^ r) * rows : ((b ^ r) + 1) * rows] for b in range(QUAD)], 1
        )
    pad = jnp.concatenate([total, jnp.zeros((LANES - 8, total.shape[1]), F32)], 0).T
    s1, s2 = pad[:, 0:1], pad[:, 1:2]
    r = lax.rsqrt(s1 / inner + EPS)
    z = z_ref[...]
    sig = sigmoid(z)
    silu = z * sig
    scan = scan_ref[...]
    gain = gain_ref[...]
    unit = scan * silu * r
    gn = (unit * gain).astype(BF)
    gn_ref[...] = gn
    scr[...] = mm_l(gn, cot_ref[...])
    dgn = dgn_ref[...]
    ngain_ref[...] = jnp.sum(dgn * unit, axis=0, keepdims=True)
    dgated = r * (gain * dgn) - unit * (r * r * s2 / inner)
    dscan_ref[...] = dgated * silu
    dz = (dgated * scan * (sig * (1.0 + z * (1.0 - sig)))).astype(BF)
    dz_ref[...] = dz
    width = dz.shape[1]
    size = width // chunks
    lane = iota((LANES, LANES), 1)
    pre = jnp.zeros((LANES, LANES), F32)
    for k in range(chunks):
        grad = mm_l(norm_ref[:, k * LANES : (k + 1) * LANES], dz)
        dot = jnp.sum(grad * ws[k][0:LANES, :].astype(F32), axis=1, keepdims=True)
        pre = pre + jnp.where(lane == k, dot, 0.0)
        out = outs[k]
        out[0:LANES, :] = grad.astype(out.dtype)
        at = pl.ds(pl.multiple_of((zy ^ k) * size, size), size)
        out[LANES : LANES + size, :] = scr[at, 0:width].astype(out.dtype)
        out[LANES + size : LANES + 2 * size, :] = scr[at, width:].astype(out.dtype)
    pre_ref[...] = pre


def put_small(out_ref, base, small):
    out_ref[base : base + SMALL, :] = small.astype(BF)


def get_small(ref, base):
    return ref[base : base + SMALL, :].astype(F32)


def ingrad_kernel(
    me_ref, norm_ref, pcx_ref, own_ref, g1, g2, g3, small_ref, ngain_ref, preb_ref, gain_ref, *refs
):
    chunks = 8
    ws, pc_ref, refs = refs[0:chunks], refs[chunks], refs[0:chunks] + refs[chunks + 1 :]
    part = own_ref.shape[1] // 2
    width = pc_ref.shape[1] - 2 * part
    shared = unfold(own_ref[...], 0)
    for r, g in ((1, g1), (2, g2), (3, g3)):
        shared = shared + unfold(g[...].astype(F32), r)
    pc_ref[:, 0:width] = pcx_ref[:, 0:width]
    pc_ref[:, width:] = jnp.concatenate(
        [shared, pcx_ref[:, width + part :].astype(F32)], 1
    ).astype(BF)
    outs = dict(zip((0, 2, 4, 6, 7, 3), refs[chunks : 2 * chunks - 2]))
    pair_ref = outs[7]
    outs[7], outs[5] = pair_ref.at[0:LANES, :], pair_ref.at[LANES : 2 * LANES, :]
    mine_ref, scr = refs[2 * chunks - 2 :]
    outs[3], outs[1] = outs[3].at[0:LANES, :], outs[3].at[LANES:, :]
    zy = me_ref[0] // QUAD
    lane = iota((LANES, LANES), 1)
    pre = preb_ref[...]
    for k in range(chunks):
        grad = mm_l(norm_ref[:, k * LANES : (k + 1) * LANES], pc_ref[...])
        dot = jnp.sum(grad * ws[k][...].astype(F32), axis=1, keepdims=True)
        pre = pre + jnp.where(lane == k, dot, 0.0)
        outs[k][0:LANES, :] = grad.astype(outs[k].dtype)
    pre = pre.T
    for k in range(chunks):
        scr[pl.ds(zy ^ k, 1), :] = pre[k : k + 1, :]
    wide = mine_ref.shape[1]
    per = wide // LANES
    gain = gain_ref[...]
    placed = jnp.concatenate([scr[k : k + 1, :] for k in range(chunks)], 1) / gain
    width = ngain_ref.shape[1]
    mine_ref[...] = small_ref[...]
    mine_ref[10:11, 0:width] = ngain_ref[...]
    mine_ref[12:13, :] = placed[:, 0:wide]
    mine_ref[13:14, 0 : (chunks - per) * LANES] = placed[:, wide:]
    put_small(pair_ref, 2 * LANES, mine_ref[...])


def add_near_kernel(keep_ref, got_ref, small_ref, out_ref, sum_ref):
    out_ref[0:LANES, :] = (keep_ref[...] + got_ref[0:LANES, :].astype(F32)).astype(BF)
    total = small_ref[...] + get_small(got_ref, 2 * LANES)
    sum_ref[...] = total
    put_small(out_ref, LANES, total)


def add_two_kernel(keep_ref, got_ref, out_ref):
    full = keep_ref.shape[0]
    out_ref[...] = (keep_ref[...] + got_ref[0:full, :].astype(F32)).astype(BF)


def add_far_kernel(keep_ref, got_ref, side_ref, out_ref):
    full = keep_ref.shape[0]
    out_ref[...] = (
        keep_ref[...] + got_ref[full:, :].astype(F32) + side_ref[...].astype(F32)
    ).astype(BF)


def add_last_kernel(keep_ref, got_ref, side_ref, small_ref, out_ref, sum_ref):
    out_ref[0:LANES, :] = (
        keep_ref[...]
        + got_ref[0:LANES, :].astype(F32)
        + side_ref[LANES : 2 * LANES, :].astype(F32)
    ).astype(BF)
    total = small_ref[...] + get_small(got_ref, LANES)
    sum_ref[...] = total
    put_small(out_ref, LANES, total)


def put_rows(part, keep_ref, send_ref, at):
    rows = keep_ref.shape[0] // 2
    keep_ref[0:rows, at] = part[0:rows, :]
    send_ref[0:rows, at] = part[rows : 2 * rows, :].astype(BF)
    keep_ref[rows:, at] = part[2 * rows : 3 * rows, :]
    send_ref[rows:, at] = part[3 * rows :, :].astype(BF)


def branch_kernel(gn_ref, wfull_ref, keep_ref, send_ref):
    put_rows(mm(gn_ref[...], wfull_ref[...]), keep_ref, send_ref, pl.ds(0, wfull_ref.shape[1]))


def tail_kernel(me_ref, *refs):
    chunks = 8
    w1, w2 = refs[0:chunks], refs[chunks : 2 * chunks]
    pc_ref, dz_ref, keep_ref, send_ref = refs[2 * chunks :]
    zy = me_ref[0] // QUAD
    for k in range(chunks):
        part = mm_t(pc_ref[...], w1[k][...]) + mm_t(dz_ref[...], w2[k][0:LANES, :])
        at = pl.ds(pl.multiple_of((zy ^ k) * LANES, LANES), LANES)
        put_rows(part, keep_ref, send_ref, at)


def pair_kernel(keep_ref, got_ref, mine_ref, send_ref):
    rows = mine_ref.shape[0]
    total = keep_ref[...] + got_ref[...].astype(F32)
    mine_ref[...] = total[0:rows, :]
    send_ref[...] = total[rows:, :].astype(BF)


def mixed_kernel(act_ref, a_ref, b_ref, mixed_ref):
    rows = mixed_ref.shape[0]
    hidden = act_ref[0:rows, :].astype(F32)
    end = act_ref[rows : rows + 16, 0:LANES].astype(F32)[0:1, 3:4]
    live = (iota((rows, 1), 0).astype(F32) < end).astype(F32)
    total = a_ref[...] + b_ref[...].astype(F32)
    mixed_ref[...] = (live * (hidden + total)).astype(BF)


def tokgrad_kernel(act_ref, gain_ref, a_ref, b_ref, grad_ref):
    rows = grad_ref.shape[0]
    hidden = act_ref[0:rows, :].astype(F32)
    scale = lax.rsqrt(jnp.mean(hidden * hidden, axis=1, keepdims=True) + EPS)
    dn = (a_ref[...] + b_ref[...].astype(F32)) * gain_ref[...]
    inner = jnp.mean(dn * hidden, axis=1, keepdims=True)
    back = scale * dn - hidden * (scale * scale * scale * inner)
    grad_ref[...] = act_ref[rows + 16 :, :].astype(F32) + back


def total_kernel(me_ref, *refs):
    a, b, small_ref = refs[0:4], refs[4:8], refs[8]
    wout_ref, mine_ref, msmall_ref, s1, s2, s3, scr = refs[9:]
    t = me_ref[0] & (QUAD - 1)
    nrow = mine_ref.shape[0]
    chunk = QUAD * nrow
    ta = a[0][...] + a[1][chunk:, :].astype(F32)
    for got in a[2:]:
        ta = ta + got[0:chunk, :].astype(F32)
    small = small_ref[...] + get_small(a[3], chunk)
    tb = b[0][...] + b[1][b[0].shape[0] :, :].astype(F32)
    for got in b[2:]:
        tb = tb + got[...].astype(F32)
    size = wout_ref.shape[0]
    width = tb.shape[1]
    wout_ref[:, 0:width] = tb[chunk : chunk + size, :]
    wout_ref[:, width:] = tb[chunk + size :, :]
    scr[:, 0:width] = tb[0:chunk, :]
    scr[:, width:] = ta
    msmall_ref[...] = small
    for r, out in enumerate((mine_ref, s1, s2, s3)):
        at = pl.ds(pl.multiple_of((t ^ r) * nrow, nrow), nrow)
        out[0:nrow, :] = scr[at, :].astype(out.dtype)
    wide = small.shape[1]
    for out in (s1, s2, s3):
        put_small(out.at[:, 0:wide], nrow, small)


def finish_kernel(me_ref, mine_ref, msmall_ref, *refs):
    got = refs[0:3]
    out_ref, cw_ref, cb_ref, dt_ref, al_ref, sk_ref, ng_ref, pg_ref, scr, sscr, row_ref = refs[3:]
    t = me_ref[0] & (QUAD - 1)
    nrow = mine_ref.shape[0]
    wide = msmall_ref.shape[1]
    scr[t] = mine_ref[...]
    sscr[t] = msmall_ref[...]
    for r in range(1, QUAD):
        scr[t ^ r] = got[r - 1][0:nrow, :].astype(F32)
        sscr[t ^ r] = get_small(got[r - 1].at[:, 0:wide], nrow)
    inner = ng_ref.shape[1]
    width = inner // QUAD
    heads = dt_ref.shape[1]
    size = inner // heads
    conv_end = out_ref.shape[1] - heads
    part = (conv_end - 2 * inner) // QUAD

    def added(ref, rows, lanes):
        return (ref[0][rows, lanes] + ref[1][rows, lanes]) + (ref[2][rows, lanes] + ref[3][rows, lanes])

    weave(out_ref, 0, [scr[q][:, 0:width] for q in range(QUAD)], size)
    weave(out_ref, inner, [scr[q][:, width : 2 * width] for q in range(QUAD)], size)
    out_ref[:, 2 * inner : conv_end] = jnp.concatenate(
        [scr[q][:, 2 * width : 2 * width + part] for q in range(QUAD)], 1
    )
    out_ref[:, conv_end:] = pick_heads(
        [scr[q][:, 2 * width + part :] for q in range(QUAD)], heads
    )
    weave(cw_ref, 0, [sscr[q][0:4, 0:width] for q in range(QUAD)], size)
    cw_ref[:, inner:] = added(sscr, slice(5, 9), slice(0, 2 * LANES))
    weave(row_ref, 0, [sscr[q][4:5, 0:width] for q in range(QUAD)], size)
    row_ref[:, inner:] = added(sscr, slice(9, 10), slice(0, 2 * LANES))
    for n in range(cb_ref.shape[0]):
        cb_ref[n : n + 1, :] = row_ref[:, n * LANES : (n + 1) * LANES]
    weave(ng_ref, 0, [sscr[q][10:11, 0:width] for q in range(QUAD)], size)
    lists = [
        pick_heads([sscr[q][8:16, at : at + LANES] for q in range(QUAD)], heads)[3:4, :]
        for at in (0, LANES, 2 * LANES)
    ]
    dt_ref[...], al_ref[...], sk_ref[...] = lists
    pg_ref[:, 0:wide] = added(sscr, slice(12, 13), slice(0, wide))
    pg_ref[:, wide:] = added(sscr, slice(13, 14), slice(0, pg_ref.shape[1] - wide))


def quad_shards(
    count,
    tokens,
    lengths,
    in_weight,
    out_weight,
    conv_weight,
    conv_bias,
    dt_bias,
    a_log,
    skip_gain,
    norm_gain,
    pre_gain,
    cotangent,
):
    chunks = count // QUAD
    rows, model = tokens.shape
    inner = norm_gain.shape[0]
    heads = dt_bias.shape[0]
    width = inner // QUAD
    size = inner // heads
    nrow, proj_width = in_weight.shape
    convw = width + conv_bias.shape[0] - inner
    part = (convw - width) // QUAD
    wide = width + 2 * part
    full = convw + LANES
    both = width + wide
    total_rows = QUAD * rows
    chunk = QUAD * nrow
    chunk_b = chunk + 2 * size

    def swap(a, mask):
        return lax.ppermute(a, "dp", [(i, i ^ mask) for i in range(count)])

    def after(a, *others):
        return lax.optimization_barrier((a,) + others)[0]

    def gather(mine, o, along=(), later=(), turn=(), last=()):
        z = after(mine, *later) if later else mine
        got = [mine, None, None, None, swap(z, 4 * QUAD), None, None, None]
        got[2] = swap(z, 2 * QUAD)
        got[1] = swap(after(mine, *last) if last else mine, QUAD)
        l2 = turn + (along if OPT['along'] == 0 else ())
        if OPT[o + 'sync'] == 1:
            got[4], got[2] = lax.optimization_barrier((got[4], got[2], got[1]) + l2)[0:2]
        elif OPT[o + 'sync'] == 2:
            got[4] = after(got[4], got[1], *l2)
        elif l2:
            got[4], got[2] = lax.optimization_barrier((got[4], got[2]) + l2)[0:2]
        got[5] = swap(got[4], QUAD)
        got[6] = swap(got[4], 2 * QUAD)
        got[3] = swap(got[2], QUAD)
        l3 = along if OPT['along'] == 1 else ()
        t = OPT[o + 'tie7']
        if OPT[o + 'byy']:
            l3 = l3 + ((), (got[5],), (got[5], got[3]), (got[3],))[t]
            got[7] = swap(after(got[6], *l3) if l3 else got[6], QUAD)
        else:
            l3 = l3 + ((), (got[6],), (got[6], got[3]), (got[3],))[t]
            got[7] = swap(after(got[5], *l3) if l3 else got[5], 2 * QUAD)
        return got

    me = lax.axis_index("dp").astype(jnp.int32).reshape(1)

    lanes = conv_bias.reshape(-1, LANES)
    given = [in_weight, tokens, cotangent, conv_weight, lanes]
    given += [a[None, :] for a in (dt_bias, a_log, skip_gain, norm_gain, pre_gain)]
    given += [out_weight]
    prepped = call(
        prep_kernel,
        [
            ((2 * rows + 16, model), BF),
            ((8, convw), F32),
            ((8, LANES), F32),
            ((1, width), F32),
            ((1, model), F32),
        ]
        + [((nrow, both), BF)] * QUAD
        + [(out_weight.shape, BF)],
        [me, lengths] + given,
        [pltpu.VMEM((QUAD, nrow, both), BF)]
        + [pltpu.VMEM(a.shape, a.dtype) for a in given[:-1]]
        + [pltpu.SemaphoreType.DMA((len(given) + 1,)), pltpu.SMEM(lengths.shape, jnp.int32)],
        name="prep",
        raw=tuple(range(1, 13)),
    )
    act, cwb, by_head, gain, pre = prepped[0:5]
    cut, own_out = prepped[5:9], prepped[9]
    got = [swap(cut[r], r) for r in range(1, QUAD)]
    beside = swap(act, 1)
    got[0] = after(got[0], beside)
    own_a, own_b = call(
        join_kernel,
        [((chunk, wide), BF), ((chunk_b, width), BF)],
        [me, cut[0]] + got + [own_out],
        name="join",
    )
    act_x = OPT['actx']
    if act_x == 0:
        across = swap(after(act, own_a), 2)
    elif act_x == 1:
        across = swap(after(act, *got), 2)
    if act_x < 2:
        w1 = gather(own_a, 'a', (across,))
    else:
        w1 = gather(own_a, 'a')
        across = swap(after(act, w1[(2, 4, 1)[act_x - 2]]), 2)
    beyond = swap(across, 1)
    acts = [act, beside, across, beyond]
    later = [(), (w1[2],), (w1[4],), (w1[1],), (w1[2], w1[4], w1[1])][OPT['later']]
    turn = [(), (w1[3], w1[5]), (w1[5],), (w1[7],), (w1[6],), (w1[3],), (w1[5], w1[6])][OPT['turn']]
    last = [(), (w1[1],), (w1[5],), (w1[3],), (w1[2],)][OPT['y1b']]
    w2 = gather(own_b, 'b', (), later, turn, last)
    normed, proj_own, ends, shared = call(
        project_kernel,
        [
            ((total_rows, model), BF),
            ((total_rows, wide), F32),
            ((QUAD, rows), F32),
            ((total_rows // 2, 2 * part), BF),
        ],
        [me] + acts + w1 + [pre],
        flops=OPT['pcost'],
        name="project",
    )
    scan_out, proj = call(
        scan_kernel,
        [((total_rows, width), F32), ((total_rows, full), F32)],
        [me, proj_own] + [swap(shared, r) for r in range(1, QUAD)] + [ends, cwb, by_head],
        [pltpu.VMEM((QUAD, total_rows, part), F32)],
        flops=OPT['scost'],
        name="scan",
    )
    w_full, cot_all, dgn = call(
        cot_kernel,
        [((width, model), BF), ((total_rows, model), BF), ((total_rows, width), F32)],
        [me] + w2 + acts,
        name="normcot",
    )
    z, stat = call(
        gate_kernel,
        [((total_rows, width), F32), ((8, total_rows), F32)],
        w2 + [normed, scan_out, dgn, gain],
        name="gate",
    )
    stats = [stat] + [swap(stat, r) for r in range(1, QUAD)]
    ungated = call(
        functools.partial(ungate_kernel, float(inner)),
        [
            ((total_rows, width), BF),
            ((total_rows, width), F32),
            ((total_rows, width), BF),
            ((1, width), F32),
            ((LANES, LANES), F32),
        ]
        + [((chunk_b, width), F32)] * 4
        + [((2 * chunk_b, width), BF)] * 2,
        [me] + stats + w2 + [z, scan_out, dgn, gain, normed, cot_all],
        [pltpu.VMEM((width, model), F32)],
        name="ungate",
        flops=OPT['ucost'],
    )
    gn, dscan, dz, ngain_part, pre_b = ungated[0:5]
    keep_b = ungated[5:9]

    got76_b, got31_b = swap(ungated[9], 2 * QUAD), swap(ungated[10], QUAD)
    fold = (total_rows // 2, 2 * part)
    pc_x, small, own_bc, *bc = call(
        scan_back_kernel,
        [((total_rows, wide), BF), ((SMALL, wide), F32), (fold, F32)] + [(fold, BF)] * 3,
        [me, proj, dscan, ends, cwb, by_head],
        [pltpu.VMEM((QUAD, total_rows, part), F32)],
        name="scanback",
        flops=OPT['bcost'],
    )
    got_bc = [swap(a, r + 1) for r, a in enumerate(bc)]
    if OPT['r1'] == 0:
        got76_b, got31_b = lax.optimization_barrier((got76_b, got31_b, pc_x))[0:2]
    elif OPT['r1'] == 1:
        got76_b, got31_b = lax.optimization_barrier((got76_b, got31_b, *got_bc))[0:2]
    elif OPT['r1'] == 2:
        got31_b = after(got31_b, *got_bc)
    (side,) = call(add_two_kernel, [((chunk_b, width), BF)], [keep_b[3], got76_b], name="side")
    got5_b = swap(side, QUAD)
    (near,) = call(add_two_kernel, [((chunk_b, width), BF)], [keep_b[1], got31_b], name="near")
    got2_b = swap(near, 2 * QUAD)
    pair_shapes = [((2 * rows, model), F32), ((2 * rows, model), BF)]

    def pair(keep, send, *first):
        got = swap(send, 1)
        mine, cross = call(
            pair_kernel,
            [((rows, model), F32), ((rows, model), BF)],
            [keep, after(got, *first) if first else got],
            name="pair",
        )
        return mine, swap(cross, 2)

    mine_m, cross_m = pair(*call(branch_kernel, pair_shapes, [gn, w_full], name="branch"))
    (mixed,) = call(mixed_kernel, [((rows, model), BF)], [act, mine_m, cross_m], name="mixed")
    r2 = [(cross_m, near, side), (near, side), (side,), (cross_m, side), (mine_m, near, side), (mine_m, side)][OPT['r2']]
    small = after(small, *r2)
    ingrads = call(
        ingrad_kernel,
        [((total_rows, wide), BF)]
        + [((chunk, wide), F32)] * 4
        + [((2 * chunk + SMALL, wide), BF), ((2 * chunk, wide), BF)]
        + [((SMALL, wide), F32)],
        [me, normed, pc_x, own_bc] + got_bc + [small, ngain_part, pre_b, pre] + w1,
        [pltpu.VMEM((chunks, LANES), F32)],
        name="ingrad",
    )
    pc1, *ingrads = ingrads
    keep_a, small = ingrads[0:4], ingrads[6]
    got75_a, got31_a = swap(ingrads[4], QUAD), swap(ingrads[5], QUAD)
    if OPT['r6']:
        got5_b = after(got5_b, small)
    (far,) = call(
        add_far_kernel, [((chunk_b, width), BF)], [keep_b[2], got76_b, got5_b], name="far"
    )
    got4_b = swap(far, 4 * QUAD)
    far_b = far

    riding = [((chunk + SMALL, wide), BF), ((SMALL, wide), F32)]
    if OPT['r7'] == 1:
        got75_a = after(got75_a, got2_b)
    side, small1 = call(add_near_kernel, riding, [keep_a[3], got75_a, small], name="side")
    if OPT['r7'] == 2:
        side = after(side, got31_a)
    got6_a = swap(side, 2 * QUAD)
    if OPT['r8'] == 1:
        got6_a = after(got6_a, got4_b)
    elif OPT['r8'] == 2:
        got6_a = after(got6_a, got31_a)
    far, small2 = call(add_last_kernel, riding, [keep_a[2], got6_a, got75_a, small1], name="far")
    (near,) = call(add_two_kernel, [((chunk, wide), BF)], [keep_a[1], got31_a], name="near")
    got2_a = swap(near, 2 * QUAD)
    got4_a = swap(far, 4 * QUAD)

    r3 = [(far_b,), (side,), (got31_a,), (got75_a,), (far_b, got75_a), (small,), (side, near), (got2_b, far_b)][OPT['r3']]
    tail_in = after(pc1, *r3)
    mine_t, cross_t = pair(
        *call(tail_kernel, pair_shapes, [me] + w1 + w2 + [tail_in, dz], name="tail"), *[(got4_b, got2_b), (), (got4_b,)][OPT['r5']]
    )
    (tokens_grad,) = call(
        tokgrad_kernel, [((rows, model), F32)], [act, pre, mine_t, cross_t], name="tokgrad"
    )
    if OPT['r4']:
        got4_a = after(got4_a, cross_t)

    out_shard, own, own_small, *cuts = call(
        total_kernel,
        [((size, model), F32), ((nrow, both), F32), ((SMALL, wide), F32)]
        + [((nrow + SMALL, both), BF)] * 3,
        [me, keep_a[0], got31_a, got2_a, got4_a, keep_b[0], got31_b, got2_b, got4_b, small2],
        [pltpu.VMEM((chunk, both), F32)],
        name="total",
    )
    own, mixed, tokens_grad = lax.optimization_barrier((own, mixed, tokens_grad))
    done = call(
        finish_kernel,
        [
            ((nrow, proj_width), F32),
            (conv_weight.shape, F32),
            ((conv_bias.shape[0] // LANES, LANES), F32),
            ((1, heads), F32),
            ((1, heads), F32),
            ((1, heads), F32),
            ((1, inner), F32),
            ((1, model), F32),
        ],
        [me, own, own_small] + [swap(a, r + 1) for r, a in enumerate(cuts)],
        [pltpu.VMEM((QUAD, nrow, both), F32), pltpu.VMEM((QUAD, SMALL, wide), F32), pltpu.VMEM((1, conv_bias.shape[0]), F32)],
        name="finish",
    )
    return (mixed, tokens_grad, done[0], out_shard, done[1]) + tuple(
        a.reshape(-1) for a in done[2:]
    )


def prenorm(hidden_in, gain_row):
    return (
        hidden_in
        * lax.rsqrt(jnp.mean(hidden_in * hidden_in, axis=-1, keepdims=True) + EPS)
        * gain_row
    )


def shifted(array, offset, filler):
    padding = jnp.full((offset,) + array.shape[1:], filler, array.dtype)
    return jnp.concatenate([padding, array[:-offset]], axis=0)


def segments(seq_lengths, row_count):
    seq_ends = jnp.cumsum(seq_lengths, dtype=jnp.int32)
    position = jnp.arange(row_count, dtype=jnp.int32)
    segment = jnp.sum(
        (position[:, None] >= seq_ends[None, :]).astype(jnp.int32), axis=1, dtype=jnp.int32
    )
    live_rows = (position < seq_ends[-1]).astype(jnp.float32)
    return (segment, live_rows)


def block_step(carry, block_item):
    state_mat, prev_segment = carry
    values, key_rows, read_rows, step_size, log_decay, block_segment = block_item
    cumulative = jnp.cumsum(log_decay, axis=0)
    position = jnp.arange(block_segment.shape[0], dtype=jnp.int32)
    causal = (block_segment[:, None] == block_segment[None, :]) & (
        position[:, None] >= position[None, :]
    )
    distance = cumulative[:, None, :] - cumulative[None, :, :]
    decay_mask = jnp.where(
        causal[:, :, None], jnp.exp(jnp.where(causal[:, :, None], distance, 0.0)), 0.0
    )
    scores = jnp.dot(read_rows, key_rows.T, precision=HIGH)
    weighting = scores[:, :, None] * decay_mask * step_size[None, :, :]
    inside = jnp.einsum("ijh,jhp->ihp", weighting, values, precision=HIGH)
    entering = (block_segment == prev_segment).astype(jnp.float32)
    carried = jnp.einsum("in,hnp->ihp", read_rows, state_mat, precision=HIGH)
    carried = carried * (jnp.exp(cumulative) * entering[:, None])[:, :, None]
    last_same = (block_segment == block_segment[-1]).astype(jnp.float32)
    tail_weight = jnp.exp(cumulative[-1][None, :] - cumulative) * last_same[:, None] * step_size
    new_state = state_mat * (jnp.exp(cumulative[-1]) * entering[-1])[:, None, None]
    new_state = new_state + jnp.einsum(
        "jn,jh,jhp->hnp", key_rows, tail_weight, values, precision=HIGH
    )
    return ((new_state, block_segment[-1]), inside + carried)


def mixer_core(projected, conv_weight, conv_bias, dt_bias, a_log, skip_gain, norm_gain, segment):
    inner_width = norm_gain.shape[0]
    head_count = dt_bias.shape[0]
    conv_width = conv_bias.shape[0]
    state_width = (conv_width - inner_width) // 2
    head_size = inner_width // head_count
    row_count = projected.shape[0]
    gate_in = projected[:, :inner_width]
    conv_src = projected[:, inner_width : inner_width + conv_width]
    dt_raw = projected[:, inner_width + conv_width :]
    conv_sum = conv_bias[None, :] + conv_weight[0][None, :] * conv_src
    for offset in range(1, conv_weight.shape[0]):
        same_rows = (segment == shifted(segment, offset, -1)).astype(jnp.float32)
        conv_sum = (
            conv_sum
            + conv_weight[offset][None, :] * shifted(conv_src, offset, 0.0) * same_rows[:, None]
        )
    activated = jax.nn.silu(conv_sum)
    values = activated[:, :inner_width].reshape(row_count, head_count, head_size)
    key_rows = activated[:, inner_width : inner_width + state_width]
    read_rows = activated[:, inner_width + state_width :]
    step_size = jax.nn.softplus(dt_raw + dt_bias[None, :])
    log_decay = -step_size * jnp.exp(a_log)[None, :]
    blocks = row_count // SCAN_ROWS
    items = (
        values.reshape(blocks, SCAN_ROWS, head_count, head_size),
        key_rows.reshape(blocks, SCAN_ROWS, state_width),
        read_rows.reshape(blocks, SCAN_ROWS, state_width),
        step_size.reshape(blocks, SCAN_ROWS, head_count),
        log_decay.reshape(blocks, SCAN_ROWS, head_count),
        segment.reshape(blocks, SCAN_ROWS),
    )
    start = (jnp.zeros((head_count, state_width, head_size), jnp.float32), jnp.array(-1, jnp.int32))
    _, scanned = lax.scan(jax.checkpoint(block_step), start, items)
    scan_out = scanned.reshape(row_count, inner_width) + (
        skip_gain[None, :, None] * values
    ).reshape(row_count, inner_width)
    gated_out = scan_out * jax.nn.silu(gate_in)
    return (
        gated_out
        * lax.rsqrt(jnp.mean(gated_out * gated_out, axis=-1, keepdims=True) + EPS)
        * norm_gain[None, :]
    )


def shards(
    tokens,
    lengths,
    in_weight,
    out_weight,
    conv_weight,
    conv_bias,
    dt_bias,
    a_log,
    skip_gain,
    norm_gain,
    pre_gain,
    cotangent,
):
    w_in, w_out = (
        lax.all_gather(in_weight, "dp", axis=0, tiled=True),
        lax.all_gather(out_weight, "dp", axis=0, tiled=True),
    )
    segment, live_rows = segments(lengths, tokens.shape[0])
    hidden_in = tokens.astype(jnp.float32)
    normed, norm_back = jax.vjp(prenorm, hidden_in, pre_gain)
    normed_low = normed.astype(jnp.bfloat16)
    projected = jnp.dot(normed_low, w_in, preferred_element_type=jnp.float32)
    proj_width = projected.shape[1]

    def mixer_local(proj_rows, conv_w, conv_b, bias_dt, decay_log, skip_w, gain_w):
        return mixer_core(proj_rows, conv_w, conv_b, bias_dt, decay_log, skip_w, gain_w, segment)

    gated_norm, mixer_back = jax.vjp(
        mixer_local, projected, conv_weight, conv_bias, dt_bias, a_log, skip_gain, norm_gain
    )
    gated_low = gated_norm.astype(jnp.bfloat16)
    branch = jnp.dot(gated_low, w_out, preferred_element_type=jnp.float32)
    mixed = (live_rows[:, None] * (hidden_in + branch)).astype(jnp.bfloat16)
    w_in, w_out = (
        lax.all_gather(in_weight, "dp", axis=0, tiled=True),
        lax.all_gather(out_weight, "dp", axis=0, tiled=True),
    )
    out_cot = cotangent.astype(jnp.float32) * live_rows[:, None]
    out_cot_low = out_cot.astype(jnp.bfloat16)
    norm_cot = lax.dot_general(
        out_cot_low, w_out, (((1,), (1,)), ((), ())), preferred_element_type=jnp.float32
    )
    proj_cot, conv_w_grad, conv_b_grad, bias_dt_grad, decay_grad, skip_grad, gain_grad = mixer_back(
        norm_cot
    )
    proj_cot_low = proj_cot.astype(jnp.bfloat16)
    normed_cot = lax.dot_general(
        proj_cot_low, w_in, (((1,), (1,)), ((), ())), preferred_element_type=jnp.float32
    )
    hidden_cot, pre_grad = norm_back(normed_cot)
    tokens_grad = out_cot + hidden_cot
    out_grad = lax.dot_general(
        gated_low, out_cot_low, (((0,), (0,)), ((), ())), preferred_element_type=jnp.float32
    )
    in_grad = lax.dot_general(
        normed_low, proj_cot_low, (((0,), (0,)), ((), ())), preferred_element_type=jnp.float32
    )
    in_wide = in_grad.reshape(2 * in_grad.shape[0], proj_width // 2)
    in_folded, out_shard = (
        lax.psum_scatter(in_wide, "dp", scatter_dimension=0, tiled=True),
        lax.psum_scatter(out_grad, "dp", scatter_dimension=0, tiled=True),
    )
    in_shard = in_folded.reshape(in_weight.shape[0], proj_width)
    summed = lax.psum(
        (conv_w_grad, conv_b_grad, bias_dt_grad, decay_grad, skip_grad, gain_grad, pre_grad), "dp"
    )
    return (
        mixed,
        tokens_grad,
        in_shard,
        out_shard,
        summed[0],
        summed[1],
        summed[2],
        summed[3],
        summed[4],
        summed[5],
        summed[6],
    )


def solution(mesh):
    count = mesh.shape["dp"]
    body = functools.partial(quad_shards, count) if count == 32 else shards
    return jax.shard_map(
        body,
        mesh=mesh,
        in_specs=(
            P("dp", None),
            P("dp"),
            P("dp", None),
            P("dp", None),
            P(),
            P(),
            P(),
            P(),
            P(),
            P(),
            P(),
            P("dp", None),
        ),
        out_specs=(
            P("dp", None),
            P("dp", None),
            P("dp", None),
            P("dp", None),
            P(),
            P(),
            P(),
            P(),
            P(),
            P(),
            P(),
        ),
        check_vma=False,
    )
```

```python
import functools

import jax
import jax.numpy as jnp
from jax import lax
from jax.experimental import pallas as pl
from jax.experimental.pallas import tpu as pltpu
from jax.sharding import PartitionSpec as P

SCAN_ROWS = 64


EPS = 1e-05
HIGH = lax.Precision.HIGHEST
BF = jnp.bfloat16
F32 = jnp.float32
NEG = -1e30
LANES = 128
OPT = {'along': 0, 'bsync': 1, 'abyy': 0, 'bbyy': 0, 'atie7': 1, 'btie7': 1, 'actx': 1, 'later': 1, 'turn': 1, 'pcost': 4000000000.0, 'scost': 16000000000.0, 'ucost': 1000.0, 'async': 1, 'y1b': 0, 'r1': 0, 'r2': 4, 'r3': 5, 'r4': 1, 'r5': 0, 'r6': 1, 'r7': 0, 'r8': 2, 'bcost': 1000.0}
PROJECT_COST = 4e9
SCAN_COST = 1.6e10
QUAD = 4
SMALL = 16
VMEM_BYTES = 44 * 1024 * 1024


def mm(a, b):
    return lax.dot_general(a, b, (((1,), (0,)), ((), ())), preferred_element_type=F32)


def mm_t(a, b):
    return lax.dot_general(a, b, (((1,), (1,)), ((), ())), preferred_element_type=F32)


def mm_l(a, b):
    return lax.dot_general(a, b, (((0,), (0,)), ((), ())), preferred_element_type=F32)


def mm_high(a, b):
    return lax.dot_general(
        a, b, (((1,), (0,)), ((), ())), precision=HIGH, preferred_element_type=F32
    )


def split3(v):
    high = v.astype(BF)
    rest = v - high.astype(F32)
    mid = rest.astype(BF)
    return high, mid, (rest - mid.astype(F32)).astype(BF)


def ones_left(ones, v):
    n = v.shape[1]
    out = mm(ones.astype(BF), jnp.concatenate(split3(v), 1))
    return out[:, 0:n] + out[:, n : 2 * n] + out[:, 2 * n :]


def ones_right(v, ones):
    low = ones.astype(BF)
    return mm(jnp.concatenate(split3(v), 1), jnp.concatenate([low, low, low], 0))


def call(kernel, out_shapes, inputs, scratch=(), flops=1e3, name=None, raw=(), limit=VMEM_BYTES):
    in_specs = [
        pl.BlockSpec(
            memory_space=pltpu.HBM
            if n in raw
            else (pltpu.SMEM if a.dtype == jnp.int32 else pltpu.VMEM)
        )
        for n, a in enumerate(inputs)
    ]
    shapes = [jax.ShapeDtypeStruct(s, d) for s, d in out_shapes]
    inputs = [
        pltpu.with_memory_space_constraint(a, pltpu.HBM) if n in raw else a
        for n, a in enumerate(inputs)
    ]
    return pl.pallas_call(
        kernel,
        out_shape=shapes,
        in_specs=in_specs,
        out_specs=[pl.BlockSpec(memory_space=pltpu.VMEM)] * len(shapes),
        scratch_shapes=list(scratch),
        cost_estimate=pl.CostEstimate(flops=int(flops), bytes_accessed=1024, transcendentals=0),
        compiler_params=pltpu.CompilerParams(vmem_limit_bytes=limit),
        name=name,
    )(*inputs)


def iota(shape, axis):
    return lax.broadcasted_iota(jnp.int32, shape, axis)


def sigmoid(v):
    return 1.0 / (1.0 + jnp.exp(-v))


def softplus(v):
    return jnp.maximum(v, 0.0) + jnp.log1p(jnp.exp(-jnp.abs(v)))


def segment_of(position, ends):
    seg = jnp.zeros(position.shape, jnp.int32)
    for s in range(4):
        seg = seg + (position >= ends[:, s : s + 1]).astype(jnp.int32)
    return seg


def same_masks(ends, rows, taps):
    position = iota((rows, 1), 0)
    seg = segment_of(position, ends)
    masks = []
    for k in range(1, taps):
        seg_k = segment_of(position - k, ends)
        masks.append(((seg == seg_k) & (position >= k)).astype(F32))
    return masks


def scan_bias(ends, rows):
    seg_col = segment_of(iota((rows, 1), 0), ends)
    seg_row = segment_of(iota((1, rows), 1), ends)
    causal = (seg_col == seg_row) & (iota((rows, rows), 0) >= iota((rows, rows), 1))
    return jnp.where(causal, 0.0, NEG)


def tri_block(rows):
    i, j = iota((rows, rows), 0), iota((rows, rows), 1)
    return ((i >= j) & (i // SCAN_ROWS == j // SCAN_ROWS)).astype(F32)


def steps_of(dt_raw, dtb, neg_rate, rows):
    step = softplus(dt_raw + dtb)
    log_decay = step * neg_rate
    cum = ones_left(tri_block(rows), log_decay)
    return step, log_decay, cum


def decay_of(cum, cum_t, head, bias, cross):
    dist = cum[:, head : head + 1] - cum_t[head : head + 1, :]
    last = cum[SCAN_ROWS - 1 : SCAN_ROWS, head : head + 1]
    return jnp.exp(dist + cross * last + bias)


def conv_sum_of(xbc, cw, cb, masks):
    total = cb + cw[0:1, :] * xbc
    for k in range(1, len(masks) + 1):
        total = total + cw[k : k + 1, :] * (pltpu.roll(xbc, k, 0) * masks[k - 1])
    return total


def pair_lanes(row, pair, low):
    return jnp.where(low, row[:, 2 * pair : 2 * pair + 1], row[:, 2 * pair + 1 : 2 * pair + 2])


def scan_kernel(me_ref, own_ref, g1, g2, g3, ends_ref, cw_ref, head_ref, out_ref, proj_ref, conv_ref, scr):
    rows = LANES
    width = out_ref.shape[1]
    t = me_ref[0] & (QUAD - 1)
    part = scr.shape[2]
    scr[t] = own_ref[:, width : width + part]
    for r, g in ((1, g1), (2, g2), (3, g3)):
        scr[t ^ r] = unfold(g[...].astype(F32), r)
    proj_ref[:, 0:width] = own_ref[:, 0:width]
    proj_ref[:, width : width + 2 * LANES] = jnp.concatenate([scr[q] for q in range(QUAD)], 1)
    proj_ref[:, width + 2 * LANES :] = jnp.concatenate(
        [own_ref[:, width + part :], jnp.zeros((own_ref.shape[0], LANES - part), F32)], 1
    )
    pairs = width // LANES
    convw = width + 2 * LANES
    dtb, rate, skip = head_ref[0:1, :], head_ref[1:2, :], head_ref[2:3, :]
    neg_rate = -jnp.exp(rate)
    cross = ((iota((rows, rows), 0) >= SCAN_ROWS) & (iota((rows, rows), 1) < SCAN_ROWS)).astype(F32)
    low = iota((rows, LANES), 1) < LANES // 2

    def body(b, carry):
        at = pl.ds(pl.multiple_of(b * rows, rows), rows)
        ends = ends_ref[pl.ds(b, 1), :].astype(jnp.int32)
        bias = scan_bias(ends, rows)
        masks = same_masks(ends, rows, 4)
        xbc = proj_ref[at, 0:convw]
        conv = conv_sum_of(xbc, cw_ref[...], cw_ref[4:5, :], masks)
        conv_ref[at, :] = conv
        act = conv * sigmoid(conv)
        key, read = act[:, width : width + LANES], act[:, width + LANES : convw]
        scores = mm_t(read.astype(BF), key.astype(BF))
        step, _, cum = steps_of(proj_ref[at, convw : convw + LANES], dtb, neg_rate, rows)
        cum_t = cum.T
        for p in range(pairs):
            lanes = slice(p * LANES, (p + 1) * LANES)
            x = act[:, lanes]
            xs = x * pair_lanes(step, p, low)
            weight = jnp.concatenate(
                [scores * decay_of(cum, cum_t, h, bias, cross) for h in (2 * p, 2 * p + 1)], 1
            )
            split = jnp.concatenate([jnp.where(low, xs, 0.0), jnp.where(low, 0.0, xs)], 0)
            y = mm(weight.astype(BF), split.astype(BF))
            out_ref[at, lanes] = y + pair_lanes(skip, p, low[0:1, :]) * x
        return carry

    lax.fori_loop(0, ends_ref.shape[0], body, 0, unroll=True)


def scan_back_kernel(
    me_ref, proj_ref, conv_ref, dscan_ref, ends_ref, cw_ref, head_ref, pc_ref, small_ref, p0, p1, p2, p3, scr
):
    rows = LANES
    width = dscan_ref.shape[1]
    pairs = width // LANES
    own = 2 * pairs
    convw = width + 2 * LANES
    dtb, rate, skip = head_ref[0:1, :], head_ref[1:2, :], head_ref[2:3, :]
    neg_rate = -jnp.exp(rate)
    src, dst = iota((rows, rows), 0), iota((rows, rows), 1)
    cross = ((src < SCAN_ROWS) & (dst >= SCAN_ROWS)).astype(F32)
    before = (src < dst).astype(F32)
    reach = (src >= dst).astype(BF)
    lane = iota((rows, LANES), 1)
    low = lane < LANES // 2
    by_head = (iota((width, LANES), 0) // (width // own) == iota((width, LANES), 1)).astype(F32)
    small_ref[...] = jnp.zeros(small_ref.shape, F32)
    t = me_ref[0] & (QUAD - 1)
    part = scr.shape[2]

    def add_small(k, v):
        total = jnp.sum(v, axis=0, keepdims=True)
        small_ref[k : k + 1, 0:width] += total[:, 0:width]
        small_ref[5 + k : 6 + k, 0 : 2 * LANES] += total[:, width:]

    def body(b, dskip):
        at = pl.ds(pl.multiple_of(b * rows, rows), rows)
        ends = ends_ref[pl.ds(b, 1), :].astype(jnp.int32)
        seg_col = segment_of(iota((rows, 1), 0), ends)
        seg_row = segment_of(iota((1, rows), 1), ends)
        bias = jnp.where((seg_col == seg_row) & (src <= dst), 0.0, NEG)
        masks = same_masks(ends, rows, 4)
        xbc = proj_ref[at, 0:convw]
        cw = cw_ref[...]
        conv = conv_ref[at, :]
        sig = sigmoid(conv)
        act = conv * sig
        key = act[:, width : width + LANES].astype(BF)
        read = act[:, width + LANES : convw].astype(BF)
        scores = mm_t(key, read)
        scores = jnp.concatenate([scores, scores], 1)
        raw = proj_ref[at, convw : convw + LANES]
        step, log_decay, cum = steps_of(raw, dtb, neg_rate, rows)
        cum_t = cum.T
        dscores = jnp.zeros((rows, 2 * rows), F32)
        dlogs, dxs, prods, dsk = [], [], [], []
        for p in range(pairs):
            lanes = slice(p * LANES, (p + 1) * LANES)
            x = act[:, lanes]
            s = pair_lanes(step, p, low)
            decays = []
            for h in (2 * p, 2 * p + 1):
                last = cum[SCAN_ROWS - 1 : SCAN_ROWS, h : h + 1]
                dist = cum_t[h : h + 1, :] - cum[:, h : h + 1]
                decays.append(jnp.exp(dist + (cross * last + bias)))
            decay = jnp.concatenate(decays, 1)
            weight = scores * decay
            dy = dscan_ref[at, lanes]
            split = jnp.concatenate([jnp.where(low, dy, 0.0), jnp.where(low, 0.0, dy)], 0).astype(BF)
            dweight = mm_t((x * s).astype(BF), split)
            dx_s = mm(weight.astype(BF), split)
            dscores = dscores + dweight * decay
            t = (dweight * weight).astype(BF)
            span = mm(jnp.concatenate([t[:, 0:rows], t[:, rows:]], 0), reach)
            dlogs.append(jnp.sum(span[0:rows, :] * before, axis=0, keepdims=True))
            dlogs.append(jnp.sum(span[rows:, :] * before, axis=0, keepdims=True))
            prods.append(dx_s * x)
            dsk.append(jnp.sum(dy * x, axis=0, keepdims=True))
            dxs.append(dx_s * s + pair_lanes(skip, p, low[0:1, :]) * dy)
        dlog = jnp.concatenate(dlogs + [jnp.zeros((rows - own, rows), F32)], 0).T
        dstep = ones_right(jnp.concatenate(prods, 1), by_head) + dlog * neg_rate
        ddt = jnp.where(lane < own, dstep * sigmoid(raw + dtb), 0.0)
        dsc = (dscores[:, 0:rows] + dscores[:, rows:]).astype(BF)
        dkey = mm(dsc, read)
        dread = mm_l(dsc, key)
        dconv = jnp.concatenate(dxs + [dkey, dread], 1) * (sig * (1.0 + conv * (1.0 - sig)))
        dxbc = cw[0:1, :] * dconv
        add_small(0, dconv * xbc)
        for k in range(1, 4):
            masked = dconv * masks[k - 1]
            dxbc = dxbc + cw[k : k + 1, :] * pltpu.roll(masked, rows - k, 0)
            add_small(k, masked * pltpu.roll(xbc, k, 0))
        add_small(4, dconv)
        small_ref[11:12, 0:LANES] += jnp.sum(ddt, axis=0, keepdims=True)
        small_ref[11:12, LANES : 2 * LANES] += jnp.sum(dlog * log_decay, axis=0, keepdims=True)
        pc_ref[at, 0:width] = dxbc[:, 0:width].astype(BF)
        for q in range(QUAD):
            scr[q, at, :] = dxbc[:, width + q * part : width + (q + 1) * part]
        pc_ref[at, width + part :] = ddt[:, 0:part].astype(BF)
        return dskip + jnp.concatenate(dsk, 1)

    dskip = lax.fori_loop(0, ends_ref.shape[0], body, jnp.zeros((1, width), F32), unroll=True)
    small_ref[11:12, 2 * LANES : 3 * LANES] = mm_high(dskip, by_head)
    half = scr.shape[1] // 2
    for r, out in enumerate((p0, p1, p2, p3)):
        mine = scr[t ^ r]
        out[...] = jnp.concatenate([mine[0:half, :], mine[half:, :]], 1).astype(out.dtype)


def weave(out_ref, at, parts, size):
    for k in range(8):
        for half in range(QUAD // 2):
            pair = [p[:, k * size : (k + 1) * size] for p in parts[2 * half : 2 * half + 2]]
            lo = at + (k * QUAD + 2 * half) * size
            out_ref[:, lo : lo + 2 * size] = jnp.concatenate(pair, 1)


def pick_heads(parts, heads):
    sels = []
    for q in range(QUAD):
        deep = (parts[q].shape[1], heads)
        sels.append((iota(deep, 1) == iota(deep, 0) * QUAD + q).astype(F32))
    return ones_right(jnp.concatenate(parts, 1), jnp.concatenate(sels, 0))


def prep_kernel(me_ref, len_hbm, *refs):
    raws = refs[0:11]
    act_ref, cwb_ref, head_ref, gain_ref, pre_ref = refs[11:16]
    outs, wout_ref, scr = refs[16:20], refs[20], refs[21]
    w_ref, tok_ref, cot_ref = refs[22:25]
    sems, len_ref = refs[32], refs[33]
    lens = pltpu.make_async_copy(len_hbm, len_ref, sems.at[len(raws)])
    lens.start()
    copies = [
        pltpu.make_async_copy(src, dst, sems.at[n])
        for n, (src, dst) in enumerate(zip(raws, refs[22:32] + (wout_ref,)))
    ]
    for c in copies:
        c.start()
    rows, model = tok_ref.shape
    t = me_ref[0] & (QUAD - 1)
    heads = 32
    own = heads // QUAD
    copies[0].wait()
    w = w_ref[...].astype(F32)
    inner = gain_ref.shape[1] * QUAD
    size = inner // heads
    conv_end = w.shape[1] - heads
    shared = w[:, 2 * inner : conv_end]
    dts = w[:, conv_end:].astype(BF)
    for q in range(QUAD):
        zs, xs = [], []
        for k in range(own):
            at = (k * QUAD + q) * size
            zs.append(w[:, at : at + size])
            xs.append(w[:, inner + at : inner + at + size])
        part = shared.shape[1] // QUAD
        pick = (iota((heads, part), 0) == iota((heads, part), 1) * QUAD + q) & (
            iota((heads, part), 1) < own
        )
        mine = [shared[:, q * part : (q + 1) * part], mm(dts, pick.astype(BF))]
        scr[q] = jnp.concatenate(zs + xs + mine, 1).astype(BF)
    for r in range(QUAD):
        outs[r][...] = scr[t ^ r]
    lane = iota((16, model), 1)
    lens.wait()
    end = jnp.int32(0)
    tail = jnp.zeros((16, model), jnp.int32)
    for s in range(4):
        end = end + len_ref[s]
        tail = tail + jnp.where(lane == s, end, 0)
    act_ref[rows : rows + 16, :] = tail.astype(F32).astype(BF)
    copies[1].wait()
    act_ref[0:rows, :] = tok_ref[...]
    copies[2].wait()
    live = (iota((rows, 1), 0) < end).astype(F32)
    act_ref[rows + 16 :, :] = (cot_ref[...].astype(F32) * live).astype(BF)
    for c in copies[3:]:
        c.wait()
    share_params(t, refs[25:32], cwb_ref, head_ref, gain_ref, pre_ref)


def share_params(t, given, cwb_ref, head_ref, gain_ref, pre_ref):
    cw_ref, cb_ref, dt_ref, al_ref, sk_ref, ng_ref, pg_ref = given
    pre_ref[...] = pg_ref[...]
    bias = jnp.concatenate([cb_ref[n : n + 1, :] for n in range(cb_ref.shape[0])], 1)
    heads = dt_ref.shape[1]
    own = heads // QUAD
    inner = ng_ref.shape[1]
    width = inner // QUAD
    size = inner // heads

    def mine(a):
        total = jnp.zeros((a.shape[0], width), F32)
        for q in range(QUAD):
            cut = [a[:, (k * QUAD + q) * size : (k * QUAD + q + 1) * size] for k in range(own)]
            total = jnp.where(t == q, jnp.concatenate(cut, 1), total)
        return total

    taps = cw_ref.shape[0]
    cwb_ref[...] = jnp.zeros(cwb_ref.shape, F32)
    cwb_ref[0:taps, 0:width] = mine(cw_ref[...])
    cwb_ref[0:taps, width:] = cw_ref[:, inner:]
    cwb_ref[taps : taps + 1, 0:width] = mine(bias)
    cwb_ref[taps : taps + 1, width:] = bias[:, inner:]
    gain_ref[...] = mine(ng_ref[...])
    pick = (iota((heads, LANES), 0) == iota((heads, LANES), 1) * QUAD + t) & (
        iota((heads, LANES), 1) < own
    )
    rows = jnp.concatenate(
        [dt_ref[...], al_ref[...], sk_ref[...], jnp.zeros((5, heads), F32)], 0
    )
    head_ref[...] = mm_high(rows, pick.astype(F32))


def join_kernel(me_ref, c0, c1, c2, c3, wout_ref, a_ref, b_ref):
    t = me_ref[0] & (QUAD - 1)
    nrow = c0.shape[0]
    width = b_ref.shape[1]
    for r, c in enumerate((c0, c1, c2, c3)):
        at = pl.ds(pl.multiple_of((t ^ r) * nrow, nrow), nrow)
        a_ref[at, :] = c[:, width:]
        b_ref[at, :] = c[:, 0:width]
    size = wout_ref.shape[0]
    b_ref[QUAD * nrow : QUAD * nrow + size, :] = wout_ref[:, 0:width]
    b_ref[QUAD * nrow + size :, :] = wout_ref[:, width:]


def project_kernel(me_ref, *refs):
    chunks = 8
    acts, ws = refs[0:QUAD], refs[QUAD : QUAD + chunks]
    gain_ref, norm_ref, proj_ref, ends_ref, shared_ref = refs[QUAD + chunks :]
    zy = me_ref[0] // QUAD
    rows = ends_ref.shape[1]
    for r in range(QUAD):
        hidden = acts[r][0:rows, :].astype(F32)
        scale = lax.rsqrt(jnp.mean(hidden * hidden, axis=1, keepdims=True) + EPS)
        for k in range(chunks):
            at = pl.ds(pl.multiple_of((zy ^ k) * LANES, LANES), LANES)
            part = acts[r][0:rows, at].astype(F32) * scale * gain_ref[:, at]
            norm_ref[r * rows : (r + 1) * rows, k * LANES : (k + 1) * LANES] = part.astype(BF)
        ends_ref[r : r + 1, :] = acts[r][rows : rows + 16, 0:LANES].astype(F32)[0:1, :]
    w = jnp.concatenate([c[...] for c in ws], axis=0)
    proj = mm(norm_ref[...], w)
    proj_ref[...] = proj
    part = shared_ref.shape[1] // 2
    width = proj.shape[1] - 2 * part
    half = shared_ref.shape[0]
    shared = proj[:, width : width + part]
    shared_ref[...] = jnp.concatenate([shared[0:half, :], shared[half:, :]], 1).astype(BF)


def unfold(packed, flip):
    rows, part = packed.shape[0] // 2, packed.shape[1] // 2
    blocks = []
    for b in range(QUAD):
        j = b ^ flip
        blocks.append(
            packed[(j % 2) * rows : (j % 2 + 1) * rows, (j // 2) * part : (j // 2 + 1) * part]
        )
    return jnp.concatenate(blocks, 0)


def cot_kernel(me_ref, *refs):
    chunks = 8
    ws, acts = refs[0:chunks], refs[chunks : chunks + QUAD]
    wfull_ref, cot_ref, dgn_ref = refs[chunks + QUAD :]
    zy = me_ref[0] // QUAD
    width = ws[0].shape[1]
    size = width // chunks
    rows = cot_ref.shape[0] // QUAD
    for k in range(chunks):
        at = pl.ds(pl.multiple_of((zy ^ k) * size, size), size)
        base = ws[k].shape[0] - 2 * size
        wfull_ref[at, 0:width] = ws[k][base : base + size, :]
        wfull_ref[at, width:] = ws[k][base + size :, :]
    for r in range(QUAD):
        cot_ref[r * rows : (r + 1) * rows, :] = acts[r][rows + 16 :, :]
    dgn_ref[...] = mm_t(cot_ref[...], wfull_ref[...])


def gate_kernel(*refs):
    chunks = 8
    ws = refs[0:chunks]
    norm_ref, scan_ref, dgn_ref, gain_ref, z_ref, stat_ref = refs[chunks:]
    w = jnp.concatenate([c[0:LANES, :] for c in ws], axis=0)
    z = mm(norm_ref[...], w)
    z_ref[...] = z
    gated = scan_ref[...] * (z * sigmoid(z))
    s1 = jnp.sum(gated * gated, axis=1, keepdims=True)
    s2 = jnp.sum(gain_ref[...] * dgn_ref[...] * gated, axis=1, keepdims=True)
    lane = iota((z.shape[0], LANES), 1)
    both = jnp.where(lane == 0, s1, 0.0) + jnp.where(lane == 1, s2, 0.0)
    stat_ref[...] = both.T[0:8, :]


def ungate_kernel(inner, me_ref, *refs):
    chunks = 8
    stats, ws = refs[0:QUAD], refs[QUAD : QUAD + chunks]
    z_ref, scan_ref, dgn_ref, gain_ref, norm_ref, cot_ref = refs[QUAD + chunks : QUAD + chunks + 6]
    gn_ref, dscan_ref, dz_ref, ngain_ref, pre_ref = refs[QUAD + chunks + 6 : QUAD + chunks + 11]
    outs = dict(zip((0, 2, 4, 5, 7, 3), refs[QUAD + chunks + 11 :]))
    scr = refs[QUAD + chunks + 17]
    full = outs[0].shape[0]
    for one, two in ((7, 6), (3, 1)):
        outs[one], outs[two] = outs[one].at[0:full, :], outs[one].at[full:, :]
    zy = me_ref[0] // QUAD
    rows = stats[0].shape[1] // QUAD
    total = stats[0][...]
    for r in range(1, QUAD):
        total = total + jnp.concatenate(
            [stats[r][:, (b ^ r) * rows : ((b ^ r) + 1) * rows] for b in range(QUAD)], 1
        )
    pad = jnp.concatenate([total, jnp.zeros((LANES - 8, total.shape[1]), F32)], 0).T
    s1, s2 = pad[:, 0:1], pad[:, 1:2]
    r = lax.rsqrt(s1 / inner + EPS)
    z = z_ref[...]
    sig = sigmoid(z)
    silu = z * sig
    scan = scan_ref[...]
    gain = gain_ref[...]
    unit = scan * silu * r
    gn = (unit * gain).astype(BF)
    gn_ref[...] = gn
    scr[...] = mm_l(gn, cot_ref[...])
    dgn = dgn_ref[...]
    ngain_ref[...] = jnp.sum(dgn * unit, axis=0, keepdims=True)
    dgated = r * (gain * dgn) - unit * (r * r * s2 / inner)
    dscan_ref[...] = dgated * silu
    dz = (dgated * scan * (sig * (1.0 + z * (1.0 - sig)))).astype(BF)
    dz_ref[...] = dz
    width = dz.shape[1]
    size = width // chunks
    lane = iota((LANES, LANES), 1)
    pre = jnp.zeros((LANES, LANES), F32)
    for k in range(chunks):
        grad = mm_l(norm_ref[:, k * LANES : (k + 1) * LANES], dz)
        dot = jnp.sum(grad * ws[k][0:LANES, :].astype(F32), axis=1, keepdims=True)
        pre = pre + jnp.where(lane == k, dot, 0.0)
        out = outs[k]
        out[0:LANES, :] = grad.astype(out.dtype)
        at = pl.ds(pl.multiple_of((zy ^ k) * size, size), size)
        out[LANES : LANES + size, :] = scr[at, 0:width].astype(out.dtype)
        out[LANES + size : LANES + 2 * size, :] = scr[at, width:].astype(out.dtype)
    pre_ref[...] = pre


def put_small(out_ref, base, small):
    out_ref[base : base + SMALL, :] = small.astype(BF)


def get_small(ref, base):
    return ref[base : base + SMALL, :].astype(F32)


def ingrad_kernel(
    me_ref, norm_ref, pcx_ref, own_ref, g1, g2, g3, small_ref, ngain_ref, preb_ref, gain_ref, *refs
):
    chunks = 8
    ws, pc_ref, refs = refs[0:chunks], refs[chunks], refs[0:chunks] + refs[chunks + 1 :]
    part = own_ref.shape[1] // 2
    width = pc_ref.shape[1] - 2 * part
    shared = unfold(own_ref[...], 0)
    for r, g in ((1, g1), (2, g2), (3, g3)):
        shared = shared + unfold(g[...].astype(F32), r)
    pc_ref[:, 0:width] = pcx_ref[:, 0:width]
    pc_ref[:, width:] = jnp.concatenate(
        [shared, pcx_ref[:, width + part :].astype(F32)], 1
    ).astype(BF)
    outs = dict(zip((0, 2, 4, 6, 7, 3), refs[chunks : 2 * chunks - 2]))
    pair_ref = outs[7]
    outs[7], outs[5] = pair_ref.at[0:LANES, :], pair_ref.at[LANES : 2 * LANES, :]
    mine_ref, scr = refs[2 * chunks - 2 :]
    outs[3], outs[1] = outs[3].at[0:LANES, :], outs[3].at[LANES:, :]
    zy = me_ref[0] // QUAD
    lane = iota((LANES, LANES), 1)
    pre = preb_ref[...]
    for k in range(chunks):
        grad = mm_l(norm_ref[:, k * LANES : (k + 1) * LANES], pc_ref[...])
        dot = jnp.sum(grad * ws[k][...].astype(F32), axis=1, keepdims=True)
        pre = pre + jnp.where(lane == k, dot, 0.0)
        outs[k][0:LANES, :] = grad.astype(outs[k].dtype)
    pre = pre.T
    for k in range(chunks):
        scr[pl.ds(zy ^ k, 1), :] = pre[k : k + 1, :]
    wide = mine_ref.shape[1]
    per = wide // LANES
    gain = gain_ref[...]
    placed = jnp.concatenate([scr[k : k + 1, :] for k in range(chunks)], 1) / gain
    width = ngain_ref.shape[1]
    mine_ref[...] = small_ref[...]
    mine_ref[10:11, 0:width] = ngain_ref[...]
    mine_ref[12:13, :] = placed[:, 0:wide]
    mine_ref[13:14, 0 : (chunks - per) * LANES] = placed[:, wide:]
    put_small(pair_ref, 2 * LANES, mine_ref[...])


def add_near_kernel(keep_ref, got_ref, small_ref, out_ref, sum_ref):
    out_ref[0:LANES, :] = (keep_ref[...] + got_ref[0:LANES, :].astype(F32)).astype(BF)
    total = small_ref[...] + get_small(got_ref, 2 * LANES)
    sum_ref[...] = total
    put_small(out_ref, LANES, total)


def add_two_kernel(keep_ref, got_ref, out_ref):
    full = keep_ref.shape[0]
    out_ref[...] = (keep_ref[...] + got_ref[0:full, :].astype(F32)).astype(BF)


def add_far_kernel(keep_ref, got_ref, side_ref, out_ref):
    full = keep_ref.shape[0]
    out_ref[...] = (
        keep_ref[...] + got_ref[full:, :].astype(F32) + side_ref[...].astype(F32)
    ).astype(BF)


def add_last_kernel(keep_ref, got_ref, side_ref, small_ref, out_ref, sum_ref):
    out_ref[0:LANES, :] = (
        keep_ref[...]
        + got_ref[0:LANES, :].astype(F32)
        + side_ref[LANES : 2 * LANES, :].astype(F32)
    ).astype(BF)
    total = small_ref[...] + get_small(got_ref, LANES)
    sum_ref[...] = total
    put_small(out_ref, LANES, total)


def put_rows(part, keep_ref, send_ref, at):
    rows = keep_ref.shape[0] // 2
    keep_ref[0:rows, at] = part[0:rows, :]
    send_ref[0:rows, at] = part[rows : 2 * rows, :].astype(BF)
    keep_ref[rows:, at] = part[2 * rows : 3 * rows, :]
    send_ref[rows:, at] = part[3 * rows :, :].astype(BF)


def branch_kernel(gn_ref, wfull_ref, keep_ref, send_ref):
    put_rows(mm(gn_ref[...], wfull_ref[...]), keep_ref, send_ref, pl.ds(0, wfull_ref.shape[1]))


def tail_kernel(me_ref, *refs):
    chunks = 8
    w1, w2 = refs[0:chunks], refs[chunks : 2 * chunks]
    pc_ref, dz_ref, keep_ref, send_ref = refs[2 * chunks :]
    zy = me_ref[0] // QUAD
    for k in range(chunks):
        part = mm_t(pc_ref[...], w1[k][...]) + mm_t(dz_ref[...], w2[k][0:LANES, :])
        at = pl.ds(pl.multiple_of((zy ^ k) * LANES, LANES), LANES)
        put_rows(part, keep_ref, send_ref, at)


def pair_kernel(keep_ref, got_ref, mine_ref, send_ref):
    rows = mine_ref.shape[0]
    total = keep_ref[...] + got_ref[...].astype(F32)
    mine_ref[...] = total[0:rows, :]
    send_ref[...] = total[rows:, :].astype(BF)


def mixed_kernel(act_ref, a_ref, b_ref, mixed_ref):
    rows = mixed_ref.shape[0]
    hidden = act_ref[0:rows, :].astype(F32)
    end = act_ref[rows : rows + 16, 0:LANES].astype(F32)[0:1, 3:4]
    live = (iota((rows, 1), 0).astype(F32) < end).astype(F32)
    total = a_ref[...] + b_ref[...].astype(F32)
    mixed_ref[...] = (live * (hidden + total)).astype(BF)


def tokgrad_kernel(act_ref, gain_ref, a_ref, b_ref, grad_ref):
    rows = grad_ref.shape[0]
    hidden = act_ref[0:rows, :].astype(F32)
    scale = lax.rsqrt(jnp.mean(hidden * hidden, axis=1, keepdims=True) + EPS)
    dn = (a_ref[...] + b_ref[...].astype(F32)) * gain_ref[...]
    inner = jnp.mean(dn * hidden, axis=1, keepdims=True)
    back = scale * dn - hidden * (scale * scale * scale * inner)
    grad_ref[...] = act_ref[rows + 16 :, :].astype(F32) + back


def total_kernel(me_ref, *refs):
    a, b, small_ref = refs[0:4], refs[4:8], refs[8]
    wout_ref, mine_ref, msmall_ref, s1, s2, s3, scr = refs[9:]
    t = me_ref[0] & (QUAD - 1)
    nrow = mine_ref.shape[0]
    chunk = QUAD * nrow
    ta = a[0][...] + a[1][chunk:, :].astype(F32)
    for got in a[2:]:
        ta = ta + got[0:chunk, :].astype(F32)
    small = small_ref[...] + get_small(a[3], chunk)
    tb = b[0][...] + b[1][b[0].shape[0] :, :].astype(F32)
    for got in b[2:]:
        tb = tb + got[...].astype(F32)
    size = wout_ref.shape[0]
    width = tb.shape[1]
    wout_ref[:, 0:width] = tb[chunk : chunk + size, :]
    wout_ref[:, width:] = tb[chunk + size :, :]
    scr[:, 0:width] = tb[0:chunk, :]
    scr[:, width:] = ta
    msmall_ref[...] = small
    for r, out in enumerate((mine_ref, s1, s2, s3)):
        at = pl.ds(pl.multiple_of((t ^ r) * nrow, nrow), nrow)
        out[0:nrow, :] = scr[at, :].astype(out.dtype)
    wide = small.shape[1]
    for out in (s1, s2, s3):
        put_small(out.at[:, 0:wide], nrow, small)


def finish_kernel(me_ref, mine_ref, msmall_ref, *refs):
    got = refs[0:3]
    out_ref, cw_ref, cb_ref, dt_ref, al_ref, sk_ref, ng_ref, pg_ref, scr, sscr, row_ref = refs[3:]
    t = me_ref[0] & (QUAD - 1)
    nrow = mine_ref.shape[0]
    wide = msmall_ref.shape[1]
    scr[t] = mine_ref[...]
    sscr[t] = msmall_ref[...]
    for r in range(1, QUAD):
        scr[t ^ r] = got[r - 1][0:nrow, :].astype(F32)
        sscr[t ^ r] = get_small(got[r - 1].at[:, 0:wide], nrow)
    inner = ng_ref.shape[1]
    width = inner // QUAD
    heads = dt_ref.shape[1]
    size = inner // heads
    conv_end = out_ref.shape[1] - heads
    part = (conv_end - 2 * inner) // QUAD

    def added(ref, rows, lanes):
        return (ref[0][rows, lanes] + ref[1][rows, lanes]) + (ref[2][rows, lanes] + ref[3][rows, lanes])

    weave(out_ref, 0, [scr[q][:, 0:width] for q in range(QUAD)], size)
    weave(out_ref, inner, [scr[q][:, width : 2 * width] for q in range(QUAD)], size)
    out_ref[:, 2 * inner : conv_end] = jnp.concatenate(
        [scr[q][:, 2 * width : 2 * width + part] for q in range(QUAD)], 1
    )
    out_ref[:, conv_end:] = pick_heads(
        [scr[q][:, 2 * width + part :] for q in range(QUAD)], heads
    )
    weave(cw_ref, 0, [sscr[q][0:4, 0:width] for q in range(QUAD)], size)
    cw_ref[:, inner:] = added(sscr, slice(5, 9), slice(0, 2 * LANES))
    weave(row_ref, 0, [sscr[q][4:5, 0:width] for q in range(QUAD)], size)
    row_ref[:, inner:] = added(sscr, slice(9, 10), slice(0, 2 * LANES))
    for n in range(cb_ref.shape[0]):
        cb_ref[n : n + 1, :] = row_ref[:, n * LANES : (n + 1) * LANES]
    weave(ng_ref, 0, [sscr[q][10:11, 0:width] for q in range(QUAD)], size)
    lists = [
        pick_heads([sscr[q][8:16, at : at + LANES] for q in range(QUAD)], heads)[3:4, :]
        for at in (0, LANES, 2 * LANES)
    ]
    dt_ref[...], al_ref[...], sk_ref[...] = lists
    pg_ref[:, 0:wide] = added(sscr, slice(12, 13), slice(0, wide))
    pg_ref[:, wide:] = added(sscr, slice(13, 14), slice(0, pg_ref.shape[1] - wide))


def quad_shards(
    count,
    tokens,
    lengths,
    in_weight,
    out_weight,
    conv_weight,
    conv_bias,
    dt_bias,
    a_log,
    skip_gain,
    norm_gain,
    pre_gain,
    cotangent,
):
    chunks = count // QUAD
    rows, model = tokens.shape
    inner = norm_gain.shape[0]
    heads = dt_bias.shape[0]
    width = inner // QUAD
    size = inner // heads
    nrow, proj_width = in_weight.shape
    convw = width + conv_bias.shape[0] - inner
    part = (convw - width) // QUAD
    wide = width + 2 * part
    full = convw + LANES
    both = width + wide
    total_rows = QUAD * rows
    chunk = QUAD * nrow
    chunk_b = chunk + 2 * size

    def swap(a, mask):
        return lax.ppermute(a, "dp", [(i, i ^ mask) for i in range(count)])

    def after(a, *others):
        return lax.optimization_barrier((a,) + others)[0]

    def gather(mine, o, along=(), later=(), turn=(), last=()):
        z = after(mine, *later) if later else mine
        got = [mine, None, None, None, swap(z, 4 * QUAD), None, None, None]
        got[2] = swap(z, 2 * QUAD)
        got[1] = swap(after(mine, *last) if last else mine, QUAD)
        l2 = turn + (along if OPT['along'] == 0 else ())
        if OPT[o + 'sync'] == 1:
            got[4], got[2] = lax.optimization_barrier((got[4], got[2], got[1]) + l2)[0:2]
        elif OPT[o + 'sync'] == 2:
            got[4] = after(got[4], got[1], *l2)
        elif l2:
            got[4], got[2] = lax.optimization_barrier((got[4], got[2]) + l2)[0:2]
        got[5] = swap(got[4], QUAD)
        got[6] = swap(got[4], 2 * QUAD)
        got[3] = swap(got[2], QUAD)
        l3 = along if OPT['along'] == 1 else ()
        t = OPT[o + 'tie7']
        if OPT[o + 'byy']:
            l3 = l3 + ((), (got[5],), (got[5], got[3]), (got[3],))[t]
            got[7] = swap(after(got[6], *l3) if l3 else got[6], QUAD)
        else:
            l3 = l3 + ((), (got[6],), (got[6], got[3]), (got[3],))[t]
            got[7] = swap(after(got[5], *l3) if l3 else got[5], 2 * QUAD)
        return got

    me = lax.axis_index("dp").astype(jnp.int32).reshape(1)

    lanes = conv_bias.reshape(-1, LANES)
    given = [in_weight, tokens, cotangent, conv_weight, lanes]
    given += [a[None, :] for a in (dt_bias, a_log, skip_gain, norm_gain, pre_gain)]
    given += [out_weight]
    prepped = call(
        prep_kernel,
        [
            ((2 * rows + 16, model), BF),
            ((8, convw), F32),
            ((8, LANES), F32),
            ((1, width), F32),
            ((1, model), F32),
        ]
        + [((nrow, both), BF)] * QUAD
        + [(out_weight.shape, BF)],
        [me, lengths] + given,
        [pltpu.VMEM((QUAD, nrow, both), BF)]
        + [pltpu.VMEM(a.shape, a.dtype) for a in given[:-1]]
        + [pltpu.SemaphoreType.DMA((len(given) + 1,)), pltpu.SMEM(lengths.shape, jnp.int32)],
        name="prep",
        raw=tuple(range(1, 13)),
    )
    act, cwb, by_head, gain, pre = prepped[0:5]
    cut, own_out = prepped[5:9], prepped[9]
    got = [swap(cut[r], r) for r in range(1, QUAD)]
    beside = swap(act, 1)
    got[0] = after(got[0], beside)
    own_a, own_b = call(
        join_kernel,
        [((chunk, wide), BF), ((chunk_b, width), BF)],
        [me, cut[0]] + got + [own_out],
        name="join",
    )
    act_x = OPT['actx']
    if act_x == 0:
        across = swap(after(act, own_a), 2)
    elif act_x == 1:
        across = swap(after(act, *got), 2)
    if act_x < 2:
        w1 = gather(own_a, 'a', (across,))
    else:
        w1 = gather(own_a, 'a')
        across = swap(after(act, w1[(2, 4, 1)[act_x - 2]]), 2)
    beyond = swap(across, 1)
    acts = [act, beside, across, beyond]
    later = [(), (w1[2],), (w1[4],), (w1[1],), (w1[2], w1[4], w1[1])][OPT['later']]
    turn = [(), (w1[3], w1[5]), (w1[5],), (w1[7],), (w1[6],), (w1[3],), (w1[5], w1[6])][OPT['turn']]
    last = [(), (w1[1],), (w1[5],), (w1[3],), (w1[2],)][OPT['y1b']]
    w2 = gather(own_b, 'b', (), later, turn, last)
    normed, proj_own, ends, shared = call(
        project_kernel,
        [
            ((total_rows, model), BF),
            ((total_rows, wide), F32),
            ((QUAD, rows), F32),
            ((total_rows // 2, 2 * part), BF),
        ],
        [me] + acts + w1 + [pre],
        flops=OPT['pcost'],
        name="project",
    )
    scan_out, proj, conv = call(
        scan_kernel,
        [((total_rows, width), F32), ((total_rows, full), F32), ((total_rows, convw), F32)],
        [me, proj_own] + [swap(shared, r) for r in range(1, QUAD)] + [ends, cwb, by_head],
        [pltpu.VMEM((QUAD, total_rows, part), F32)],
        flops=OPT['scost'],
        name="scan",
    )
    w_full, cot_all, dgn = call(
        cot_kernel,
        [((width, model), BF), ((total_rows, model), BF), ((total_rows, width), F32)],
        [me] + w2 + acts,
        name="normcot",
    )
    z, stat = call(
        gate_kernel,
        [((total_rows, width), F32), ((8, total_rows), F32)],
        w2 + [normed, scan_out, dgn, gain],
        name="gate",
    )
    stats = [stat] + [swap(stat, r) for r in range(1, QUAD)]
    ungated = call(
        functools.partial(ungate_kernel, float(inner)),
        [
            ((total_rows, width), BF),
            ((total_rows, width), F32),
            ((total_rows, width), BF),
            ((1, width), F32),
            ((LANES, LANES), F32),
        ]
        + [((chunk_b, width), F32)] * 4
        + [((2 * chunk_b, width), BF)] * 2,
        [me] + stats + w2 + [z, scan_out, dgn, gain, normed, cot_all],
        [pltpu.VMEM((width, model), F32)],
        name="ungate",
        flops=OPT['ucost'],
    )
    gn, dscan, dz, ngain_part, pre_b = ungated[0:5]
    keep_b = ungated[5:9]

    got76_b, got31_b = swap(ungated[9], 2 * QUAD), swap(ungated[10], QUAD)
    fold = (total_rows // 2, 2 * part)
    pc_x, small, own_bc, *bc = call(
        scan_back_kernel,
        [((total_rows, wide), BF), ((SMALL, wide), F32), (fold, F32)] + [(fold, BF)] * 3,
        [me, proj, conv, dscan, ends, cwb, by_head],
        [pltpu.VMEM((QUAD, total_rows, part), F32)],
        name="scanback",
        flops=OPT['bcost'],
    )
    got_bc = [swap(a, r + 1) for r, a in enumerate(bc)]
    if OPT['r1'] == 0:
        got76_b, got31_b = lax.optimization_barrier((got76_b, got31_b, pc_x))[0:2]
    elif OPT['r1'] == 1:
        got76_b, got31_b = lax.optimization_barrier((got76_b, got31_b, *got_bc))[0:2]
    elif OPT['r1'] == 2:
        got31_b = after(got31_b, *got_bc)
    (side,) = call(add_two_kernel, [((chunk_b, width), BF)], [keep_b[3], got76_b], name="side")
    got5_b = swap(side, QUAD)
    (near,) = call(add_two_kernel, [((chunk_b, width), BF)], [keep_b[1], got31_b], name="near")
    got2_b = swap(near, 2 * QUAD)
    pair_shapes = [((2 * rows, model), F32), ((2 * rows, model), BF)]

    def pair(keep, send, *first):
        got = swap(send, 1)
        mine, cross = call(
            pair_kernel,
            [((rows, model), F32), ((rows, model), BF)],
            [keep, after(got, *first) if first else got],
            name="pair",
        )
        return mine, swap(cross, 2)

    mine_m, cross_m = pair(*call(branch_kernel, pair_shapes, [gn, w_full], name="branch"))
    (mixed,) = call(mixed_kernel, [((rows, model), BF)], [act, mine_m, cross_m], name="mixed")
    r2 = [(cross_m, near, side), (near, side), (side,), (cross_m, side), (mine_m, near, side), (mine_m, side)][OPT['r2']]
    small = after(small, *r2)
    ingrads = call(
        ingrad_kernel,
        [((total_rows, wide), BF)]
        + [((chunk, wide), F32)] * 4
        + [((2 * chunk + SMALL, wide), BF), ((2 * chunk, wide), BF)]
        + [((SMALL, wide), F32)],
        [me, normed, pc_x, own_bc] + got_bc + [small, ngain_part, pre_b, pre] + w1,
        [pltpu.VMEM((chunks, LANES), F32)],
        name="ingrad",
    )
    pc1, *ingrads = ingrads
    keep_a, small = ingrads[0:4], ingrads[6]
    got75_a, got31_a = swap(ingrads[4], QUAD), swap(ingrads[5], QUAD)
    if OPT['r6']:
        got5_b = after(got5_b, small)
    (far,) = call(
        add_far_kernel, [((chunk_b, width), BF)], [keep_b[2], got76_b, got5_b], name="far"
    )
    got4_b = swap(far, 4 * QUAD)
    far_b = far

    riding = [((chunk + SMALL, wide), BF), ((SMALL, wide), F32)]
    if OPT['r7'] == 1:
        got75_a = after(got75_a, got2_b)
    side, small1 = call(add_near_kernel, riding, [keep_a[3], got75_a, small], name="side")
    if OPT['r7'] == 2:
        side = after(side, got31_a)
    got6_a = swap(side, 2 * QUAD)
    if OPT['r8'] == 1:
        got6_a = after(got6_a, got4_b)
    elif OPT['r8'] == 2:
        got6_a = after(got6_a, got31_a)
    far, small2 = call(add_last_kernel, riding, [keep_a[2], got6_a, got75_a, small1], name="far")
    (near,) = call(add_two_kernel, [((chunk, wide), BF)], [keep_a[1], got31_a], name="near")
    got2_a = swap(near, 2 * QUAD)
    got4_a = swap(far, 4 * QUAD)

    r3 = [(far_b,), (side,), (got31_a,), (got75_a,), (far_b, got75_a), (small,), (side, near), (got2_b, far_b)][OPT['r3']]
    tail_in = after(pc1, *r3)
    mine_t, cross_t = pair(
        *call(tail_kernel, pair_shapes, [me] + w1 + w2 + [tail_in, dz], name="tail"), *[(got4_b, got2_b), (), (got4_b,)][OPT['r5']]
    )
    (tokens_grad,) = call(
        tokgrad_kernel, [((rows, model), F32)], [act, pre, mine_t, cross_t], name="tokgrad"
    )
    if OPT['r4']:
        got4_a = after(got4_a, cross_t)

    out_shard, own, own_small, *cuts = call(
        total_kernel,
        [((size, model), F32), ((nrow, both), F32), ((SMALL, wide), F32)]
        + [((nrow + SMALL, both), BF)] * 3,
        [me, keep_a[0], got31_a, got2_a, got4_a, keep_b[0], got31_b, got2_b, got4_b, small2],
        [pltpu.VMEM((chunk, both), F32)],
        name="total",
    )
    own, mixed, tokens_grad = lax.optimization_barrier((own, mixed, tokens_grad))
    done = call(
        finish_kernel,
        [
            ((nrow, proj_width), F32),
            (conv_weight.shape, F32),
            ((conv_bias.shape[0] // LANES, LANES), F32),
            ((1, heads), F32),
            ((1, heads), F32),
            ((1, heads), F32),
            ((1, inner), F32),
            ((1, model), F32),
        ],
        [me, own, own_small] + [swap(a, r + 1) for r, a in enumerate(cuts)],
        [pltpu.VMEM((QUAD, nrow, both), F32), pltpu.VMEM((QUAD, SMALL, wide), F32), pltpu.VMEM((1, conv_bias.shape[0]), F32)],
        name="finish",
    )
    return (mixed, tokens_grad, done[0], out_shard, done[1]) + tuple(
        a.reshape(-1) for a in done[2:]
    )


def prenorm(hidden_in, gain_row):
    return (
        hidden_in
        * lax.rsqrt(jnp.mean(hidden_in * hidden_in, axis=-1, keepdims=True) + EPS)
        * gain_row
    )


def shifted(array, offset, filler):
    padding = jnp.full((offset,) + array.shape[1:], filler, array.dtype)
    return jnp.concatenate([padding, array[:-offset]], axis=0)


def segments(seq_lengths, row_count):
    seq_ends = jnp.cumsum(seq_lengths, dtype=jnp.int32)
    position = jnp.arange(row_count, dtype=jnp.int32)
    segment = jnp.sum(
        (position[:, None] >= seq_ends[None, :]).astype(jnp.int32), axis=1, dtype=jnp.int32
    )
    live_rows = (position < seq_ends[-1]).astype(jnp.float32)
    return (segment, live_rows)


def block_step(carry, block_item):
    state_mat, prev_segment = carry
    values, key_rows, read_rows, step_size, log_decay, block_segment = block_item
    cumulative = jnp.cumsum(log_decay, axis=0)
    position = jnp.arange(block_segment.shape[0], dtype=jnp.int32)
    causal = (block_segment[:, None] == block_segment[None, :]) & (
        position[:, None] >= position[None, :]
    )
    distance = cumulative[:, None, :] - cumulative[None, :, :]
    decay_mask = jnp.where(
        causal[:, :, None], jnp.exp(jnp.where(causal[:, :, None], distance, 0.0)), 0.0
    )
    scores = jnp.dot(read_rows, key_rows.T, precision=HIGH)
    weighting = scores[:, :, None] * decay_mask * step_size[None, :, :]
    inside = jnp.einsum("ijh,jhp->ihp", weighting, values, precision=HIGH)
    entering = (block_segment == prev_segment).astype(jnp.float32)
    carried = jnp.einsum("in,hnp->ihp", read_rows, state_mat, precision=HIGH)
    carried = carried * (jnp.exp(cumulative) * entering[:, None])[:, :, None]
    last_same = (block_segment == block_segment[-1]).astype(jnp.float32)
    tail_weight = jnp.exp(cumulative[-1][None, :] - cumulative) * last_same[:, None] * step_size
    new_state = state_mat * (jnp.exp(cumulative[-1]) * entering[-1])[:, None, None]
    new_state = new_state + jnp.einsum(
        "jn,jh,jhp->hnp", key_rows, tail_weight, values, precision=HIGH
    )
    return ((new_state, block_segment[-1]), inside + carried)


def mixer_core(projected, conv_weight, conv_bias, dt_bias, a_log, skip_gain, norm_gain, segment):
    inner_width = norm_gain.shape[0]
    head_count = dt_bias.shape[0]
    conv_width = conv_bias.shape[0]
    state_width = (conv_width - inner_width) // 2
    head_size = inner_width // head_count
    row_count = projected.shape[0]
    gate_in = projected[:, :inner_width]
    conv_src = projected[:, inner_width : inner_width + conv_width]
    dt_raw = projected[:, inner_width + conv_width :]
    conv_sum = conv_bias[None, :] + conv_weight[0][None, :] * conv_src
    for offset in range(1, conv_weight.shape[0]):
        same_rows = (segment == shifted(segment, offset, -1)).astype(jnp.float32)
        conv_sum = (
            conv_sum
            + conv_weight[offset][None, :] * shifted(conv_src, offset, 0.0) * same_rows[:, None]
        )
    activated = jax.nn.silu(conv_sum)
    values = activated[:, :inner_width].reshape(row_count, head_count, head_size)
    key_rows = activated[:, inner_width : inner_width + state_width]
    read_rows = activated[:, inner_width + state_width :]
    step_size = jax.nn.softplus(dt_raw + dt_bias[None, :])
    log_decay = -step_size * jnp.exp(a_log)[None, :]
    blocks = row_count // SCAN_ROWS
    items = (
        values.reshape(blocks, SCAN_ROWS, head_count, head_size),
        key_rows.reshape(blocks, SCAN_ROWS, state_width),
        read_rows.reshape(blocks, SCAN_ROWS, state_width),
        step_size.reshape(blocks, SCAN_ROWS, head_count),
        log_decay.reshape(blocks, SCAN_ROWS, head_count),
        segment.reshape(blocks, SCAN_ROWS),
    )
    start = (jnp.zeros((head_count, state_width, head_size), jnp.float32), jnp.array(-1, jnp.int32))
    _, scanned = lax.scan(jax.checkpoint(block_step), start, items)
    scan_out = scanned.reshape(row_count, inner_width) + (
        skip_gain[None, :, None] * values
    ).reshape(row_count, inner_width)
    gated_out = scan_out * jax.nn.silu(gate_in)
    return (
        gated_out
        * lax.rsqrt(jnp.mean(gated_out * gated_out, axis=-1, keepdims=True) + EPS)
        * norm_gain[None, :]
    )


def shards(
    tokens,
    lengths,
    in_weight,
    out_weight,
    conv_weight,
    conv_bias,
    dt_bias,
    a_log,
    skip_gain,
    norm_gain,
    pre_gain,
    cotangent,
):
    w_in, w_out = (
        lax.all_gather(in_weight, "dp", axis=0, tiled=True),
        lax.all_gather(out_weight, "dp", axis=0, tiled=True),
    )
    segment, live_rows = segments(lengths, tokens.shape[0])
    hidden_in = tokens.astype(jnp.float32)
    normed, norm_back = jax.vjp(prenorm, hidden_in, pre_gain)
    normed_low = normed.astype(jnp.bfloat16)
    projected = jnp.dot(normed_low, w_in, preferred_element_type=jnp.float32)
    proj_width = projected.shape[1]

    def mixer_local(proj_rows, conv_w, conv_b, bias_dt, decay_log, skip_w, gain_w):
        return mixer_core(proj_rows, conv_w, conv_b, bias_dt, decay_log, skip_w, gain_w, segment)

    gated_norm, mixer_back = jax.vjp(
        mixer_local, projected, conv_weight, conv_bias, dt_bias, a_log, skip_gain, norm_gain
    )
    gated_low = gated_norm.astype(jnp.bfloat16)
    branch = jnp.dot(gated_low, w_out, preferred_element_type=jnp.float32)
    mixed = (live_rows[:, None] * (hidden_in + branch)).astype(jnp.bfloat16)
    w_in, w_out = (
        lax.all_gather(in_weight, "dp", axis=0, tiled=True),
        lax.all_gather(out_weight, "dp", axis=0, tiled=True),
    )
    out_cot = cotangent.astype(jnp.float32) * live_rows[:, None]
    out_cot_low = out_cot.astype(jnp.bfloat16)
    norm_cot = lax.dot_general(
        out_cot_low, w_out, (((1,), (1,)), ((), ())), preferred_element_type=jnp.float32
    )
    proj_cot, conv_w_grad, conv_b_grad, bias_dt_grad, decay_grad, skip_grad, gain_grad = mixer_back(
        norm_cot
    )
    proj_cot_low = proj_cot.astype(jnp.bfloat16)
    normed_cot = lax.dot_general(
        proj_cot_low, w_in, (((1,), (1,)), ((), ())), preferred_element_type=jnp.float32
    )
    hidden_cot, pre_grad = norm_back(normed_cot)
    tokens_grad = out_cot + hidden_cot
    out_grad = lax.dot_general(
        gated_low, out_cot_low, (((0,), (0,)), ((), ())), preferred_element_type=jnp.float32
    )
    in_grad = lax.dot_general(
        normed_low, proj_cot_low, (((0,), (0,)), ((), ())), preferred_element_type=jnp.float32
    )
    in_wide = in_grad.reshape(2 * in_grad.shape[0], proj_width // 2)
    in_folded, out_shard = (
        lax.psum_scatter(in_wide, "dp", scatter_dimension=0, tiled=True),
        lax.psum_scatter(out_grad, "dp", scatter_dimension=0, tiled=True),
    )
    in_shard = in_folded.reshape(in_weight.shape[0], proj_width)
    summed = lax.psum(
        (conv_w_grad, conv_b_grad, bias_dt_grad, decay_grad, skip_grad, gain_grad, pre_grad), "dp"
    )
    return (
        mixed,
        tokens_grad,
        in_shard,
        out_shard,
        summed[0],
        summed[1],
        summed[2],
        summed[3],
        summed[4],
        summed[5],
        summed[6],
    )


def solution(mesh):
    count = mesh.shape["dp"]
    body = functools.partial(quad_shards, count) if count == 32 else shards
    return jax.shard_map(
        body,
        mesh=mesh,
        in_specs=(
            P("dp", None),
            P("dp"),
            P("dp", None),
            P("dp", None),
            P(),
            P(),
            P(),
            P(),
            P(),
            P(),
            P(),
            P("dp", None),
        ),
        out_specs=(
            P("dp", None),
            P("dp", None),
            P("dp", None),
            P("dp", None),
            P(),
            P(),
            P(),
            P(),
            P(),
            P(),
            P(),
        ),
        check_vma=False,
    )
```
